32 devices in a mesh: vir: 8 (over y, x, core), out: 4 (over z).
Axes of the slice: x: 2, y: 2, z: 4, core: 2. Of those that a mesh axis runs over, the one named last changes fastest.
Arguments:
- factors: bfloat16 [512, 512, 1536], P('out', 'vir'), may hold values from -2.5 to 2.5
- amplitudes: bfloat16 [128, 512, 512], P('out', 'vir'), may hold values from -0.015991211 to 0.015991211
Outputs:
- ladder: float32 [2, 128, 512], P(None, 'vir', 'out')
The draws below stay inside these ranges and needn't reach their ends.
All inputs are finite; a program needn't handle non-finite values.
Results may differ from the reference program's by a relative error of at most 0.0029.
Values may be sent and summed in bfloat16 or wider, within the bound.
No kernel may reach another device: no remote copies, remote signals or barrier semaphores. Data moves between devices by JAX's collectives and lax.ppermute only.
A program may use at most 128 MiB of HBM per device.

```python
import jax
import jax.numpy as jnp
from jax import lax

V = 512
NAUX = 1536
PAIRS = 128
BB = 2


def raised(drawn, key, source, target, blocks, factor):
    def block_of(axis_at):
        return (jnp.arange(drawn.shape[axis_at]) // (drawn.shape[axis_at] // blocks)).reshape((-1,) + (1,) * (drawn.ndim - 1 - axis_at))

    one_side = jax.random.permutation(key, blocks)[block_of(target)]
    second = (block_of(target) + blocks // 2) % blocks
    return jnp.where((block_of(source) == one_side) | (block_of(source) == second), factor * drawn, drawn)


def shard_levels(rng, extent, pieces, smallest, largest):
    factor_of = 1.0
    for dim, parts in pieces:
        steps = jax.random.uniform(jax.random.fold_in(jax.random.fold_in(rng, 6), dim), (parts,), jnp.float32, smallest / len(pieces), largest / len(pieces))
        factor_of = factor_of * jnp.repeat(jnp.exp(steps), extent[dim] // parts).reshape((-1,) + (1,) * (len(extent) - 1 - dim))
    return factor_of


def bell_draw(own_key, dims, scale, limit, split=(), held_as=jnp.bfloat16):
    values = jax.random.normal(own_key, dims, jnp.float32) * scale
    if len(split) > 0:
        values = shard_levels(own_key, dims, split, -0.22, 0.18) * values
    return jnp.clip(values, min=-limit, max=limit).astype(held_as)


def noise_with(key, extent, spread, bound, pieces, heavy, kind=jnp.bfloat16):
    drawn = spread * jax.random.normal(key, extent, jnp.float32)
    if pieces:
        drawn = drawn * shard_levels(key, extent, pieces, -0.22, 0.18)
    return jnp.clip(raised(drawn, jax.random.fold_in(key, 3), *heavy), -bound, bound).astype(kind)


def setup_inputs(seed: int = 0) -> dict:
    streams_of = jax.random.split(jax.random.key(seed), 3)
    return {
        "factors": bell_draw(streams_of[0], (V, V, NAUX), 0.16, 2.5, ((0, 4), (1, 8))),
        "amplitudes": noise_with(streams_of[1], (PAIRS, V, V), 0.002, 0.015991211, ((0, 4), (1, 8)), (1, 0, 8, 2.0)),
    }


def reference(factors, amplitudes):
    slab_rows = factors[:BB].astype(jnp.float32).reshape(BB * V, NAUX)
    amplitude_rows = amplitudes.astype(jnp.float32).reshape(PAIRS, V * V)
    block_len = min(64, V)

    def per_block(factor_block):
        tiles = jnp.dot(factor_block.astype(jnp.float32).reshape(block_len * V, NAUX), slab_rows.T)
        tiles = lax.optimization_barrier(tiles.astype(jnp.bfloat16)).astype(jnp.float32)
        tiles = tiles.reshape(block_len, V, BB, V).transpose(0, 2, 1, 3).reshape(block_len * BB, V * V)
        result = jnp.dot(tiles, amplitude_rows.T)
        return result.reshape(block_len, BB, PAIRS)

    blocks = lax.map(per_block, factors.reshape(V // block_len, block_len, V, NAUX))
    return blocks.reshape(V, BB, PAIRS).transpose(1, 2, 0)
```

```python
import functools

import jax
import jax.numpy as jnp
from jax import lax
from jax.experimental import pallas as pl
from jax.experimental.pallas import tpu as pltpu
from jax.sharding import PartitionSpec as P

BB = 2
LANES = 128
NT = (((1,), (1,)), ((), ()))


def largest_part(extent, limit):
    part = min(extent, limit)
    while extent % part:
        part -= 1
    return part


def integral_kernel(factor_ref, batch_ref, out_ref, tile_ref):
    a_len, c_len, aux_len = factor_ref.shape
    d_len = out_ref.shape[3]
    rows = factor_ref[...].reshape(a_len * c_len, aux_len)
    for b in range(out_ref.shape[1]):
        tile = lax.dot_general(rows, batch_ref[b], NT, preferred_element_type=jnp.float32)
        for j in range(d_len // LANES):
            tile_ref[j] = tile[:, j * LANES : (j + 1) * LANES]
        for c in range(c_len):
            for j in range(d_len // LANES):
                picked = tile_ref[j, pl.ds(c, a_len, stride=c_len), :]
                out_ref[c, b, :, j * LANES : (j + 1) * LANES] = picked.astype(jnp.bfloat16)


def integrals(factors, batch):
    a_rows, c_rows, aux_len = factors.shape
    bb, d_len, _ = batch.shape
    a_len = largest_part(a_rows, 16)
    return pl.pallas_call(
        integral_kernel,
        grid=(a_rows // a_len,),
        in_specs=[
            pl.BlockSpec((a_len, c_rows, aux_len), lambda i: (i, 0, 0)),
            pl.BlockSpec((bb, d_len, aux_len), lambda i: (0, 0, 0)),
        ],
        out_specs=pl.BlockSpec((c_rows, bb, a_len, d_len), lambda i: (0, 0, i, 0)),
        out_shape=jax.ShapeDtypeStruct((c_rows, bb, a_rows, d_len), jnp.bfloat16),
        scratch_shapes=[pltpu.VMEM((d_len // LANES, a_len * c_rows, LANES), jnp.float32)],
        compiler_params=pltpu.CompilerParams(vmem_limit_bytes=48 * 2**20),
        cost_estimate=pl.CostEstimate(
            flops=2 * a_rows * c_rows * bb * d_len * aux_len,
            bytes_accessed=2 * (factors.size + batch.size + a_rows * c_rows * bb * d_len),
            transcendentals=0,
        ),
    )(factors, batch)


def ladder_kernel(count, *refs):
    tau_refs, integral_ref, out_ref = refs[:count], refs[count], refs[count + 1]
    c_len, bb, a_rows, d_len = integral_ref.shape

    @pl.when(pl.program_id(0) == 0)
    def _():
        out_ref[...] = jnp.zeros_like(out_ref)

    total = out_ref[...]
    for c in range(c_len):
        taus = [r[c] for r in tau_refs]
        left = taus[0] if count == 1 else jnp.concatenate(taus, axis=0)
        right = integral_ref[c].reshape(bb * a_rows, d_len)
        total += lax.dot_general(left, right, NT, preferred_element_type=jnp.float32)
    out_ref[...] = total


def ladder_terms(taus, integral, c_start):
    c_rows, pairs, d_len = taus[0].shape
    _, bb, a_rows, _ = integral.shape
    c_len = largest_part(c_rows, 4)
    first = c_start // c_len
    count = len(taus)
    return pl.pallas_call(
        functools.partial(ladder_kernel, count),
        grid=(c_rows // c_len,),
        in_specs=[pl.BlockSpec((c_len, pairs, d_len), lambda i: (i, 0, 0))] * count
        + [pl.BlockSpec((c_len, bb, a_rows, d_len), lambda i: (first + i, 0, 0, 0))],
        out_specs=pl.BlockSpec((count * pairs, bb * a_rows), lambda i: (0, 0)),
        out_shape=jax.ShapeDtypeStruct((count * pairs, bb * a_rows), jnp.float32),
        compiler_params=pltpu.CompilerParams(vmem_limit_bytes=32 * 2**20),
        cost_estimate=pl.CostEstimate(
            flops=2 * count * pairs * bb * a_rows * c_rows * d_len,
            bytes_accessed=2 * c_rows * d_len * (count * pairs + bb * a_rows),
            transcendentals=0,
        ),
    )(*taus, integral)


def body(parts, factors, amplitudes):
    a_rows, c_rows, aux_len = factors.shape
    pairs = amplitudes.shape[0]
    n = lax.axis_size("out")
    vir = lax.axis_size("vir")
    z = lax.axis_index("out")

    batch_rows = factors[:BB]
    shared = batch_rows
    for k in range(1, n):
        here = lax.ppermute(batch_rows, "out", [(0, k)])
        shared = jnp.where(z == k, here, shared)
    batch = lax.all_gather(shared, "vir", axis=1, tiled=True)

    piece = c_rows // parts
    own = [
        amplitudes[:, k * piece : (k + 1) * piece].transpose(1, 0, 2) for k in range(parts)
    ]
    ups, downs = [own], [own]
    for s in range(n - 1):
        rise = [(k, k + 1) for k in range(s, n - 1)]
        fall = [(k + 1, k) for k in range(n - 1 - s)]
        ups.append([lax.ppermute(t, "out", rise) for t in ups[-1]])
        downs.append([lax.ppermute(t, "out", fall) for t in downs[-1]])

    integral = integrals(factors, batch)

    def summed(groups):
        return functools.reduce(
            jnp.add, [ladder_terms(list(g), integral, k * piece) for k, g in enumerate(groups)]
        )

    middle = summed([(t,) for t in own])
    both = [summed(zip(ups[s], downs[s])) for s in range(1, n)]
    stacked = jnp.concatenate(
        [t[:pairs] for t in reversed(both)] + [middle] + [t[pairs:] for t in both]
    )
    terms = lax.dynamic_slice_in_dim(stacked, (n - 1 - z) * pairs, n * pairs, axis=0)
    pieces = terms.reshape(vir, n * pairs // vir, BB * a_rows)
    swapped = lax.all_to_all(pieces, "vir", split_axis=0, concat_axis=0)
    out = jnp.sum(swapped, axis=0)
    return out.reshape(-1, BB, a_rows).transpose(1, 0, 2)


def solution(mesh):
    def run(factors, amplitudes):
        c_rows = factors.shape[1] // mesh.shape["vir"]
        parts = 4 if c_rows % 4 == 0 else 1
        placed = (P("out", "vir", None), P("out", "vir", None))
        return jax.shard_map(
            functools.partial(body, parts),
            mesh=mesh,
            in_specs=placed,
            out_specs=P(None, "vir", "out"),
            check_vma=False,
        )(factors, amplitudes)

    return run
```

```python
import functools

import jax
import jax.numpy as jnp
from jax import lax
from jax.experimental import pallas as pl
from jax.experimental.pallas import tpu as pltpu
from jax.sharding import PartitionSpec as P

BB = 2
LANES = 128
NT = (((1,), (1,)), ((), ()))
NN = (((1,), (0,)), ((), ()))
LITTLE = pl.CostEstimate(flops=1024, bytes_accessed=1024, transcendentals=0)


def largest_part(extent, limit):
    part = min(extent, limit)
    while extent % part:
        part -= 1
    return part


def call(kernel, inputs, in_specs, out_shape, out_spec, through, grid=(1,), scratch=(), into=None):
    n_in, n_thru = len(inputs), len(through)
    kept = [] if into is None else [into]

    def run(*refs):
        outs = refs[n_in + len(kept) + n_thru :]
        kernel(*refs[:n_in], outs[0], *outs[1 + n_thru :])

    anywhere = pl.BlockSpec(memory_space=pl.ANY)
    first = n_in + len(kept)
    aliases = {first + k: 1 + k for k in range(n_thru)}
    if kept:
        aliases[n_in] = 0
    out = pl.pallas_call(
        run,
        grid=grid,
        in_specs=list(in_specs) + [anywhere] * (len(kept) + n_thru),
        out_specs=[out_spec] + [anywhere] * n_thru,
        out_shape=[out_shape] + [jax.ShapeDtypeStruct(t.shape, t.dtype) for t in through],
        input_output_aliases=aliases,
        scratch_shapes=list(scratch),
        compiler_params=pltpu.CompilerParams(vmem_limit_bytes=48 * 2**20),
        cost_estimate=LITTLE,
    )(*inputs, *kept, *through)
    return out[0], list(out[1:])


def fence(arrays):
    def nothing(*refs):
        pass

    anywhere = [pl.BlockSpec(memory_space=pl.ANY)] * len(arrays)
    return list(
        pl.pallas_call(
            nothing,
            in_specs=anywhere,
            out_specs=anywhere,
            out_shape=[jax.ShapeDtypeStruct(t.shape, t.dtype) for t in arrays],
            input_output_aliases={k: k for k in range(len(arrays))},
            cost_estimate=LITTLE,
        )(*arrays)
    )


def turn_kernel(batch_ref, out_ref):
    for b in range(out_ref.shape[0]):
        out_ref[b] = batch_ref[b].T


def turn(batch, through):
    bb, d_len, aux_len = batch.shape
    vmem = pl.BlockSpec(memory_space=pltpu.VMEM)
    out_shape = jax.ShapeDtypeStruct((bb, aux_len, d_len), jnp.bfloat16)
    return call(turn_kernel, [batch], [vmem], out_shape, vmem, through)


def integral_kernel(factor_ref, batch_ref, out_ref):
    a_len, c_len, aux_len = factor_ref.shape
    d_len = out_ref.shape[3]
    rows = factor_ref[...].reshape(a_len * c_len, aux_len)
    wide = largest_part(d_len // LANES, 2) * LANES
    for b in range(out_ref.shape[1]):
        for j in range(0, d_len, wide):
            tile = lax.dot_general(
                rows, batch_ref[b, :, j : j + wide], NN, preferred_element_type=jnp.float32
            )
            turned = jnp.swapaxes(tile.reshape(a_len, c_len, wide), 0, 1)
            out_ref[:, b, :, j : j + wide] = turned.astype(jnp.bfloat16)


def integrals(factors, batch, part, parts, through, into):
    a_rows, c_rows, aux_len = factors.shape
    bb, _, d_len = batch.shape
    c_len = c_rows // parts
    a_len = largest_part(a_rows, 16)
    return call(
        integral_kernel,
        [factors, batch],
        [
            pl.BlockSpec((a_len, c_len, aux_len), lambda i: (i, part, 0)),
            pl.BlockSpec((bb, aux_len, d_len), lambda i: (0, 0, 0)),
        ],
        jax.ShapeDtypeStruct((c_rows, bb, a_rows, d_len), jnp.bfloat16),
        pl.BlockSpec((c_len, bb, a_len, d_len), lambda i: (part, 0, i, 0)),
        through,
        grid=(a_rows // a_len,),
        into=into,
    )


def ladder_kernel(count, *refs):
    tau_refs, integral_ref, out_ref = refs[:count], refs[count], refs[count + 1]
    c_len, bb, a_rows, d_len = integral_ref.shape

    @pl.when(pl.program_id(0) == 0)
    def _():
        out_ref[...] = jnp.zeros_like(out_ref)

    total = out_ref[...]
    for c in range(c_len):
        taus = [r[c] for r in tau_refs]
        left = taus[0] if count == 1 else jnp.concatenate(taus, axis=0)
        right = integral_ref[c].reshape(bb * a_rows, d_len)
        total += lax.dot_general(left, right, NT, preferred_element_type=jnp.float32)
    out_ref[...] = total


def ladder_terms(taus, integral, c_start, through):
    c_rows, pairs, d_len = taus[0].shape
    _, bb, a_rows, _ = integral.shape
    c_len = largest_part(c_rows, 4)
    first = c_start // c_len
    count = len(taus)
    return call(
        functools.partial(ladder_kernel, count),
        list(taus) + [integral],
        [pl.BlockSpec((c_len, pairs, d_len), lambda i: (i, 0, 0))] * count
        + [pl.BlockSpec((c_len, bb, a_rows, d_len), lambda i: (first + i, 0, 0, 0))],
        jax.ShapeDtypeStruct((count * pairs, bb * a_rows), jnp.float32),
        pl.BlockSpec((count * pairs, bb * a_rows), lambda i: (0, 0)),
        through,
        grid=(c_rows // c_len,),
    )


def body(pieces, slices, factors, amplitudes):
    a_rows, c_rows, _ = factors.shape
    pairs = amplitudes.shape[0]
    n = lax.axis_size("out")
    vir = lax.axis_size("vir")
    z = lax.axis_index("out")
    piece = c_rows // pieces
    last = (n - 1) * pieces

    token = [jnp.zeros((8, LANES), jnp.float32)]
    batch_rows = factors[:BB]
    heres = [lax.ppermute(batch_rows, "out", [(0, k)]) for k in range(1, n)]

    arrived = []
    for k in range(pieces):
        own = amplitudes[:, k * piece : (k + 1) * piece].transpose(1, 0, 2)
        arrived.append([own, own])

    def send(upto):
        while len(arrived) < min(upto, last) + pieces:
            step = len(arrived) // pieces
            rise = [(k, k + 1) for k in range(step - 1, n - 1)]
            fall = [(k + 1, k) for k in range(n - step)]
            up, down = arrived[-pieces]
            arrived.append([lax.ppermute(up, "out", rise), lax.ppermute(down, "out", fall)])

    def ordered(step, items, others=()):
        items = [i + pieces for i in items if i < last - pieces]
        through = token + [t for i in items for t in arrived[i]]
        made, passed = step(through + list(others))
        token[0] = passed[0]
        for k, i in enumerate(items):
            arrived[i] = passed[1 + 2 * k : 3 + 2 * k]
        return made, passed[1 + 2 * len(items) :]

    downs = [(k + 1, k) for k in range(n - 1)]
    top = lax.ppermute(arrived[0][0], "out", [(n - 2, n - 1)])
    fallen = lax.ppermute(arrived[0][1], "out", downs)
    _, passed = ordered(lambda t: (None, fence(t)), [], heres + [top, fallen])
    heres, (top, fallen) = passed[: n - 1], passed[n - 1 :]
    shared = batch_rows
    for k in range(1, n):
        shared = jnp.where(z == k, heres[k - 1], shared)
    gathered = lax.all_gather(shared, "vir", axis=1, tiled=True)
    risen = lax.ppermute(arrived[0][0], "out", [(k, k + 1) for k in range(n - 2)])
    arrived.append([jnp.where(z == n - 1, top, risen), fallen])
    send(pieces)
    ordered(lambda t: (None, fence(t)), [0])
    send(pieces + 1)
    batch, _ = ordered(lambda t: turn(gathered, t), [1])
    send(pieces + 2)

    integral = None
    for q in range(slices):
        item = [pieces] if q == slices - 2 else []
        integral, _ = ordered(
            lambda t: integrals(factors, batch, q, slices, t, integral), item
        )
        if item:
            send(2 * pieces + 1)
    done = len(arrived) - 2 * pieces
    while done < (n - 3) * pieces + 1:
        ordered(lambda t: (None, fence(t)), [done])
        done += 1
        send(done + pieces)

    def taus(steps, k):
        return [t for s in steps for t in (arrived[s * pieces + k][:1] if s == 0 else arrived[s * pieces + k])]

    before = []
    for k in range(pieces):
        items = [done] if done < (n - 2) * pieces and done % pieces != k else []
        made, _ = ordered(
            lambda t: ladder_terms(taus(range(n - 1), k), integral, k * piece, t), items
        )
        before.append(made)
        done += 1
        send(done + pieces)
    after = [
        ordered(lambda t: ladder_terms(taus([n - 1], k), integral, k * piece, t), [])[0]
        for k in range(pieces)
    ]
    early = functools.reduce(jnp.add, before)
    late = functools.reduce(jnp.add, after)

    blocks = {0: early[:pairs]}
    for s in range(1, n):
        pair = late if s == n - 1 else early[(2 * s - 1) * pairs : (2 * s + 1) * pairs]
        blocks[-s], blocks[s] = pair[:pairs], pair[pairs:]
    stacked = jnp.concatenate([blocks[s] for s in range(1 - n, n)])
    terms = lax.dynamic_slice_in_dim(stacked, (n - 1 - z) * pairs, n * pairs, axis=0)
    parts = terms.reshape(vir, n * pairs // vir, BB * a_rows)
    swapped = lax.all_to_all(parts, "vir", split_axis=0, concat_axis=0)
    out = jnp.sum(swapped, axis=0)
    return out.reshape(-1, BB, a_rows).transpose(1, 0, 2)


def solution(mesh):
    def run(factors, amplitudes):
        c_rows = factors.shape[1] // mesh.shape["vir"]
        pieces = 2 if c_rows % 2 == 0 else 1
        slices = 4 if c_rows % 32 == 0 else 1
        placed = (P("out", "vir", None), P("out", "vir", None))
        return jax.shard_map(
            functools.partial(body, pieces, slices),
            mesh=mesh,
            in_specs=placed,
            out_specs=P(None, "vir", "out"),
            check_vma=False,
        )(factors, amplitudes)

    return run
```

```python
import functools

import jax
import jax.numpy as jnp
from jax import lax
from jax.experimental import pallas as pl
from jax.experimental.pallas import tpu as pltpu
from jax.sharding import PartitionSpec as P

BB = 2
LANES = 128
NT = (((1,), (1,)), ((), ()))
NN = (((1,), (0,)), ((), ()))
LITTLE = pl.CostEstimate(flops=1024, bytes_accessed=1024, transcendentals=0)


def largest_part(extent, limit):
    part = min(extent, limit)
    while extent % part:
        part -= 1
    return part


def call(kernel, inputs, in_specs, out_shape, out_spec, through, grid=(1,), scratch=(), into=None):
    n_in, n_thru = len(inputs), len(through)
    kept = [] if into is None else [into]

    def run(*refs):
        outs = refs[n_in + len(kept) + n_thru :]
        kernel(*refs[:n_in], outs[0], *outs[1 + n_thru :])

    anywhere = pl.BlockSpec(memory_space=pl.ANY)
    first = n_in + len(kept)
    aliases = {first + k: 1 + k for k in range(n_thru)}
    if kept:
        aliases[n_in] = 0
    out = pl.pallas_call(
        run,
        grid=grid,
        in_specs=list(in_specs) + [anywhere] * (len(kept) + n_thru),
        out_specs=[out_spec] + [anywhere] * n_thru,
        out_shape=[out_shape] + [jax.ShapeDtypeStruct(t.shape, t.dtype) for t in through],
        input_output_aliases=aliases,
        scratch_shapes=list(scratch),
        compiler_params=pltpu.CompilerParams(vmem_limit_bytes=48 * 2**20),
        cost_estimate=LITTLE,
    )(*inputs, *kept, *through)
    return out[0], list(out[1:])


def fence(arrays):
    def nothing(*refs):
        pass

    anywhere = [pl.BlockSpec(memory_space=pl.ANY)] * len(arrays)
    return list(
        pl.pallas_call(
            nothing,
            in_specs=anywhere,
            out_specs=anywhere,
            out_shape=[jax.ShapeDtypeStruct(t.shape, t.dtype) for t in arrays],
            input_output_aliases={k: k for k in range(len(arrays))},
            cost_estimate=LITTLE,
        )(*arrays)
    )


def assemble_kernel(*refs):
    place_ref, slabs, out_ref, whole_ref = refs[0], refs[1:-2], refs[-2], refs[-1]
    piece = slabs[0].shape[1]
    for k, slab in enumerate(slabs):
        start = pl.multiple_of(place_ref[k] * piece, piece)
        whole_ref[:, pl.ds(start, piece), :] = slab[...]
    for b in range(out_ref.shape[0]):
        out_ref[b] = whole_ref[b].T


def assemble(slabs, places, through):
    bb, piece, aux_len = slabs[0].shape
    d_len = piece * len(slabs)
    vmem = pl.BlockSpec(memory_space=pltpu.VMEM)
    return call(
        assemble_kernel,
        [places] + slabs,
        [pl.BlockSpec(memory_space=pltpu.SMEM)] + [vmem] * len(slabs),
        jax.ShapeDtypeStruct((bb, aux_len, d_len), jnp.bfloat16),
        vmem,
        through,
        scratch=[pltpu.VMEM((bb, d_len, aux_len), jnp.bfloat16)],
    )


def integral_kernel(factor_ref, batch_ref, out_ref):
    a_len, c_len, aux_len = factor_ref.shape
    d_len = out_ref.shape[3]
    rows = factor_ref[...].reshape(a_len * c_len, aux_len)
    wide = largest_part(d_len // LANES, 2) * LANES
    for b in range(out_ref.shape[1]):
        for j in range(0, d_len, wide):
            tile = lax.dot_general(
                rows, batch_ref[b, :, j : j + wide], NN, preferred_element_type=jnp.float32
            )
            turned = jnp.swapaxes(tile.reshape(a_len, c_len, wide), 0, 1)
            out_ref[:, b, :, j : j + wide] = turned.astype(jnp.bfloat16)


def integrals(factors, batch, start, stop, through):
    a_rows, c_rows, aux_len = factors.shape
    bb, _, d_len = batch.shape
    c_len = largest_part(c_rows, 8)
    first = start // c_len
    return call(
        integral_kernel,
        [factors, batch],
        [
            pl.BlockSpec((a_rows, c_len, aux_len), lambda i: (0, first + i, 0)),
            pl.BlockSpec((bb, aux_len, d_len), lambda i: (0, 0, 0)),
        ],
        jax.ShapeDtypeStruct((stop - start, bb, a_rows, d_len), jnp.bfloat16),
        pl.BlockSpec((c_len, bb, a_rows, d_len), lambda i: (i, 0, 0, 0)),
        through,
        grid=((stop - start) // c_len,),
    )


def ladder_kernel(tau_ref, integral_ref, out_ref, total_ref):
    places, c_len, pairs, d_len = tau_ref.shape
    _, bb, a_rows, _ = integral_ref.shape
    step = pl.program_id(0)

    @pl.when(step == 0)
    def _():
        total_ref[...] = jnp.zeros_like(total_ref)

    total = total_ref[...]
    for c in range(c_len):
        left = integral_ref[c].reshape(bb * a_rows, d_len)
        right = tau_ref[:, c].reshape(places * pairs, d_len)
        total += lax.dot_general(left, right, NT, preferred_element_type=jnp.float32)
    total_ref[...] = total

    @pl.when(step == pl.num_programs(0) - 1)
    def _():
        out_ref[...] = total_ref[...].T


def ladder_terms(tau, integral, start, through):
    places, c_rows, pairs, d_len = tau.shape
    _, bb, a_rows, _ = integral.shape
    c_len = largest_part(c_rows, 4)
    first = start // c_len
    shape = (bb * a_rows, places * pairs)
    return call(
        ladder_kernel,
        [tau, integral],
        [
            pl.BlockSpec((places, c_len, pairs, d_len), lambda i: (0, i, 0, 0)),
            pl.BlockSpec((c_len, bb, a_rows, d_len), lambda i: (first + i, 0, 0, 0)),
        ],
        jax.ShapeDtypeStruct(shape[::-1], jnp.float32),
        pl.BlockSpec(shape[::-1], lambda i: (0, 0)),
        through,
        grid=(c_rows // c_len,),
        scratch=[pltpu.VMEM(shape, jnp.float32)],
    )


def everywhere(shared, vir, token):
    me = lax.axis_index("vir")
    if vir & (vir - 1) or not 2 < vir <= 8:
        gathered = lax.all_gather(shared, "vir", axis=1, tiled=True)
        return [gathered], jnp.zeros((1,), jnp.int32), token

    def swap(array, mask):
        return lax.ppermute(array, "vir", [(k, k ^ mask) for k in range(vir)])

    masks = list(range(2, vir, 2))
    across = [swap(shared, m) for m in masks]
    beside = swap(shared, 1)
    token, *passed = fence([token, beside] + across)
    beside, across = passed[0], passed[1:]
    slabs = [shared, beside] + across + [swap(t, 1) for t in across]
    order = [0, 1] + masks + [m ^ 1 for m in masks]
    return slabs, jnp.stack([me ^ m for m in order]).astype(jnp.int32), token


def body(cuts, factors, amplitudes):
    a_rows, c_rows, _ = factors.shape
    n = lax.axis_size("out")
    vir = lax.axis_size("vir")
    z = lax.axis_index("out")

    token = jnp.zeros((8, LANES), jnp.float32)
    turned = [amplitudes[:, i:j].transpose(1, 0, 2) for i, j in zip(cuts, cuts[1:])]
    token, batch_rows, *turned = fence([token, factors[:BB]] + turned)
    taus = [lax.all_gather(t, "out") for t in turned]

    heres = [lax.ppermute(batch_rows, "out", [(0, k)]) for k in range(1, n)]
    token, *heres = fence([token] + heres)
    shared = batch_rows
    for k in range(1, n):
        shared = jnp.where(z == k, heres[k - 1], shared)
    slabs, places, token = everywhere(shared, vir, token)
    batch, [token] = assemble(slabs, places, [token])
    integral, [token] = integrals(factors, batch, 0, c_rows, [token])

    total = None
    for tau, start in zip(taus, cuts):
        terms, [token] = ladder_terms(tau, integral, start, [token])
        total = terms if total is None else total + terms

    parts = total.reshape(vir, -1, BB * a_rows)
    swapped = lax.all_to_all(parts, "vir", split_axis=0, concat_axis=0)
    out = jnp.sum(swapped, axis=0)
    return out.reshape(-1, BB, a_rows).transpose(1, 0, 2)


def solution(mesh):
    def run(factors, amplitudes):
        c_rows = factors.shape[1] // mesh.shape["vir"]
        cuts = (0, 3 * c_rows // 4, c_rows) if c_rows % 32 == 0 else (0, c_rows)
        placed = (P("out", "vir", None), P("out", "vir", None))
        return jax.shard_map(
            functools.partial(body, cuts),
            mesh=mesh,
            in_specs=placed,
            out_specs=P(None, "vir", "out"),
            check_vma=False,
        )(factors, amplitudes)

    return run
```

```python
import functools

import jax
import jax.numpy as jnp
from jax import lax
from jax.experimental import pallas as pl
from jax.experimental.pallas import tpu as pltpu
from jax.sharding import PartitionSpec as P

BB = 2
LANES = 128
NT = (((1,), (1,)), ((), ()))
NN = (((1,), (0,)), ((), ()))
LITTLE = pl.CostEstimate(flops=1024, bytes_accessed=1024, transcendentals=0)


def largest_part(extent, limit):
    part = min(extent, limit)
    while extent % part:
        part -= 1
    return part


def call(kernel, inputs, in_specs, out_shape, out_spec, through, grid=(1,), scratch=(), into=None):
    n_in, n_thru = len(inputs), len(through)
    kept = [] if into is None else [into]

    def run(*refs):
        outs = refs[n_in + len(kept) + n_thru :]
        kernel(*refs[:n_in], outs[0], *outs[1 + n_thru :])

    anywhere = pl.BlockSpec(memory_space=pltpu.HBM)
    first = n_in + len(kept)
    aliases = {first + k: 1 + k for k in range(n_thru)}
    if kept:
        aliases[n_in] = 0
    out = pl.pallas_call(
        run,
        grid=grid,
        in_specs=list(in_specs) + [anywhere] * (len(kept) + n_thru),
        out_specs=[out_spec] + [anywhere] * n_thru,
        out_shape=[out_shape] + [jax.ShapeDtypeStruct(t.shape, t.dtype) for t in through],
        input_output_aliases=aliases,
        scratch_shapes=list(scratch),
        compiler_params=pltpu.CompilerParams(vmem_limit_bytes=48 * 2**20),
        cost_estimate=LITTLE,
    )(*inputs, *kept, *through)
    return out[0], list(out[1:])


def fence(arrays):
    def nothing(*refs):
        pass

    anywhere = [pl.BlockSpec(memory_space=pltpu.HBM)] * len(arrays)
    return list(
        pl.pallas_call(
            nothing,
            in_specs=anywhere,
            out_specs=anywhere,
            out_shape=[jax.ShapeDtypeStruct(t.shape, t.dtype) for t in arrays],
            input_output_aliases={k: k for k in range(len(arrays))},
            cost_estimate=LITTLE,
        )(*arrays)
    )


def pack_kernel(*refs):
    for k, slab in enumerate(refs[:-1]):
        refs[-1][k] = slab[...]


def pack(slabs, through):
    vmem = pl.BlockSpec(memory_space=pltpu.VMEM)
    shape = jax.ShapeDtypeStruct((len(slabs),) + slabs[0].shape, slabs[0].dtype)
    return call(pack_kernel, slabs, [vmem] * len(slabs), shape, vmem, through)


def assemble_kernel(*refs):
    place_ref, packs, out_ref, whole_ref = refs[0], refs[1:-2], refs[-2], refs[-1]
    piece = packs[0].shape[2]
    for i, packed in enumerate(packs):
        for k in range(packed.shape[0]):
            start = pl.multiple_of(place_ref[i * packed.shape[0] + k] * piece, piece)
            whole_ref[:, pl.ds(start, piece), :] = packed[k]
    for b in range(out_ref.shape[0]):
        out_ref[b] = whole_ref[b].T


def assemble(packs, places, through):
    count, bb, piece, aux_len = packs[0].shape
    d_len = piece * count * len(packs)
    vmem = pl.BlockSpec(memory_space=pltpu.VMEM)
    return call(
        assemble_kernel,
        [places] + packs,
        [pl.BlockSpec(memory_space=pltpu.SMEM)] + [vmem] * len(packs),
        jax.ShapeDtypeStruct((bb, aux_len, d_len), jnp.bfloat16),
        vmem,
        through,
        scratch=[pltpu.VMEM((bb, d_len, aux_len), jnp.bfloat16)],
    )


def integral_kernel(factor_ref, batch_ref, out_ref):
    a_len, c_len, aux_len = factor_ref.shape
    d_len = out_ref.shape[3]
    rows = factor_ref[...].reshape(a_len * c_len, aux_len)
    wide = largest_part(d_len // LANES, 2) * LANES
    for b in range(out_ref.shape[1]):
        for j in range(0, d_len, wide):
            tile = lax.dot_general(
                rows, batch_ref[b, :, j : j + wide], NN, preferred_element_type=jnp.float32
            )
            turned = jnp.swapaxes(tile.reshape(a_len, c_len, wide), 0, 1)
            out_ref[:, b, :, j : j + wide] = turned.astype(jnp.bfloat16)


def integrals(factors, batch, part, parts, through, into):
    a_rows, c_rows, aux_len = factors.shape
    bb, _, d_len = batch.shape
    c_len = largest_part(c_rows // parts, 8)
    count = c_rows // parts // c_len
    return call(
        integral_kernel,
        [factors, batch],
        [
            pl.BlockSpec((a_rows, c_len, aux_len), lambda i: (0, part * count + i, 0)),
            pl.BlockSpec((bb, aux_len, d_len), lambda i: (0, 0, 0)),
        ],
        jax.ShapeDtypeStruct((c_rows, bb, a_rows, d_len), jnp.bfloat16),
        pl.BlockSpec((c_len, bb, a_rows, d_len), lambda i: (part * count + i, 0, 0, 0)),
        through,
        grid=(count,),
        into=into,
    )


def ladder_kernel(count, *refs):
    tau_refs, (integral_ref, out_ref, total_ref) = refs[:count], refs[count:]
    c_len, bb, a_rows, d_len = integral_ref.shape
    step = pl.program_id(0)

    @pl.when(step == 0)
    def _():
        total_ref[...] = jnp.zeros_like(total_ref)

    total = total_ref[...]
    for c in range(c_len):
        left = integral_ref[c].reshape(bb * a_rows, d_len)
        right = jnp.concatenate([r[c] for r in tau_refs], axis=0)
        total += lax.dot_general(left, right, NT, preferred_element_type=jnp.float32)
    total_ref[...] = total

    @pl.when(step == pl.num_programs(0) - 1)
    def _():
        out_ref[...] = total_ref[...].T


def ladder_terms(taus, integral, start, through):
    c_rows, pairs, d_len = taus[0].shape
    _, bb, a_rows, _ = integral.shape
    c_len = largest_part(c_rows, 8)
    first = start // c_len
    count = len(taus)
    shape = (bb * a_rows, count * pairs)
    return call(
        functools.partial(ladder_kernel, count),
        taus + [integral],
        [pl.BlockSpec((c_len, pairs, d_len), lambda i: (i, 0, 0))] * count
        + [pl.BlockSpec((c_len, bb, a_rows, d_len), lambda i: (first + i, 0, 0, 0))],
        jax.ShapeDtypeStruct(shape[::-1], jnp.float32),
        pl.BlockSpec(shape[::-1], lambda i: (0, 0)),
        through,
        grid=(c_rows // c_len,),
        scratch=[pltpu.VMEM(shape, jnp.float32)],
    )


def body(pieces, slices, factors, amplitudes):
    a_rows, c_rows, _ = factors.shape
    pairs = amplitudes.shape[0]
    n = lax.axis_size("out")
    vir = lax.axis_size("vir")
    z = lax.axis_index("out")
    me = lax.axis_index("vir")
    piece = c_rows // pieces
    token = jnp.zeros((8, LANES), jnp.float32)
    chain = {}
    left = []

    def send(array, up, step, k, pairs_of=None):
        if up:
            ways = [(i, i + 1) for i in range(step - 1, n - 1)]
        else:
            ways = [(i + 1, i) for i in range(n - step)]
        return lax.ppermute(array, "out", ways if pairs_of is None else pairs_of)

    def ordered(step, keys=(), others=(), held=()):
        nonlocal token
        keys = [key for key in keys if key in chain]
        both = keys + [key for key in held if key in chain]
        made, passed = step([token] + [chain[key] for key in both] + list(others))
        token = passed[0]
        for key, array in zip(both, passed[1:]):
            chain[key] = array
        for up, s, k in keys:
            left.append((up, s, k))
            if s + 1 < n:
                chain[up, s + 1, k] = send(chain[up, s, k], up, s + 1, k)
        return made, passed[1 + len(both) :]

    def wait(keys=(), others=(), held=()):
        return ordered(lambda t: (None, fence(t)), keys, others, held)[1]

    batch_rows = factors[:BB]
    whole = amplitudes.transpose(1, 0, 2)
    own = [whole[k * piece : (k + 1) * piece] for k in range(pieces)]
    for k in range(pieces):
        chain[False, 1, k] = send(own[k], False, 1, k)
    top = send(whole, True, 1, 0, [(n - 2, n - 1)])
    rest = None
    stride = 1
    while 2 * stride < n:
        stride *= 2
    shared = batch_rows
    while stride:
        ways = [(i, i + stride) for i in range(0, n - stride, 2 * stride)]
        here = lax.ppermute(shared, "out", ways)
        [here] = wait([], [here], [(False, 1, 0)] if stride == 1 else [])
        taking = functools.reduce(jnp.logical_or, [z == t for _, t in ways])
        shared = jnp.where(taking, here, shared)
        if rest is None:
            rest = [send(t, True, 1, k, [(i, i + 1) for i in range(n - 2)]) for k, t in enumerate(own)]
        stride //= 2
    def swap(array, mask):
        return lax.ppermute(array, "vir", [(k, k ^ mask) for k in range(vir)])

    if vir & (vir - 1) == 0 and 2 < vir <= 8:
        near = [m for m in range(2, vir, 2) if m & (m - 1) == 0]
        far = [m for m in range(2, vir, 2) if m & (m - 1)]
        slabs = [swap(shared, m) for m in near]
        shared, *slabs = wait([(False, 1, 0)], [shared] + slabs)
        slabs += [swap(shared, m) for m in far]
        packed, [top, first] = ordered(
            lambda t: pack([shared] + slabs, t), [(False, 1, 1)], [top, rest[0]]
        )
        packs = [packed, swap(packed, 1)]
        places = jnp.stack([me ^ m ^ core for core in (0, 1) for m in [0] + near + far])
    else:
        packs = [lax.all_gather(shared, "vir", axis=1, tiled=True)[None]]
        places = jnp.zeros((1,), jnp.int32)
        top, first = wait([(False, 1, 0), (False, 1, 1)], [top, rest[0]])
    def joined(top, array, k):
        return jnp.where(z == n - 1, top[k * piece : (k + 1) * piece], array)

    chain[True, 1, 0] = joined(top, first, 0)
    chain[True, 2, 0] = send(chain[True, 1, 0], True, 2, 0)
    left.append((True, 1, 0))
    batch, [top] = ordered(
        lambda t: assemble(packs, places.astype(jnp.int32), t), others=[top]
    )

    plan = [[], [(False, 2, 0)], [(True, 2, 0)], [(False, 2, 1)]]
    integral = None
    for q in range(slices):
        late = rest[1:] if q == slices // 2 - 1 or slices == 1 else []
        integral, late = ordered(
            lambda t: integrals(factors, batch, q, slices, t, integral),
            plan[q] if slices == len(plan) else [],
            late,
        )
        for k, array in enumerate(late):
            chain[True, 1, k + 1] = joined(top, array, k + 1)
            chain[True, 2, k + 1] = send(chain[True, 1, k + 1], True, 2, k + 1)
            left.append((True, 1, k + 1))

    def unsent(step, k):
        return [(up, step, k) for up in (False, True) if (up, step, k) not in left]

    for s in range(1, n - 2):
        for k in range(pieces):
            for key in unsent(s, k):
                wait([key])

    def terms(taus, k, keys=()):
        return ordered(lambda t: ladder_terms(taus, integral, k * piece, t), keys)[0]

    before, after = [], []
    for k in range(pieces):
        for key in unsent(n - 2, k):
            wait([key])
        others = [key for q in range(k + 1, pieces) for key in unsent(n - 2, q)]
        taus = [own[k]] + [chain[up, s, k] for s in range(1, n - 1) for up in (True, False)]
        before.append(terms(taus, k, others))
    for k in range(pieces):
        after.append(terms([chain[True, n - 1, k], chain[False, n - 1, k]], k))
    early = functools.reduce(jnp.add, before)
    late = functools.reduce(jnp.add, after)

    blocks = {0: early[:pairs]}
    for s in range(1, n):
        pair = late if s == n - 1 else early[(2 * s - 1) * pairs : (2 * s + 1) * pairs]
        blocks[-s], blocks[s] = pair[:pairs], pair[pairs:]
    stacked = jnp.concatenate([blocks[s] for s in range(1 - n, n)])
    total = lax.dynamic_slice_in_dim(stacked, (n - 1 - z) * pairs, n * pairs, axis=0)
    parts = total.reshape(vir, -1, BB * a_rows)
    swapped = lax.all_to_all(parts, "vir", split_axis=0, concat_axis=0)
    out = jnp.sum(swapped, axis=0)
    return out.reshape(-1, BB, a_rows).transpose(1, 0, 2)


def solution(mesh):
    def run(factors, amplitudes):
        c_rows = factors.shape[1] // mesh.shape["vir"]
        pieces = 2 if c_rows % 2 == 0 else 1
        slices = 4 if c_rows % 32 == 0 else 1
        placed = (P("out", "vir", None), P("out", "vir", None))
        return jax.shard_map(
            functools.partial(body, pieces, slices),
            mesh=mesh,
            in_specs=placed,
            out_specs=P(None, "vir", "out"),
            check_vma=False,
        )(factors, amplitudes)

    return run
```

```python
import functools

import jax
import jax.numpy as jnp
from jax import lax
from jax.experimental import pallas as pl
from jax.experimental.pallas import tpu as pltpu
from jax.sharding import PartitionSpec as P

BB = 2
LANES = 128
NT = (((1,), (1,)), ((), ()))
NN = (((1,), (0,)), ((), ()))
LITTLE = pl.CostEstimate(flops=1024, bytes_accessed=1024, transcendentals=0)


def largest_part(extent, limit):
    part = min(extent, limit)
    while extent % part:
        part -= 1
    return part


def call(kernel, inputs, in_specs, out_shape, out_spec, through, grid=(1,), scratch=(), vmem=28):
    n_in, n_thru = len(inputs), len(through)

    def run(*refs):
        outs = refs[n_in + n_thru :]
        kernel(*refs[:n_in], outs[0], *outs[1 + n_thru :])

    anywhere = pl.BlockSpec(memory_space=pl.ANY)
    out = pl.pallas_call(
        run,
        grid=grid,
        in_specs=list(in_specs) + [anywhere] * n_thru,
        out_specs=[out_spec] + [anywhere] * n_thru,
        out_shape=[out_shape] + [jax.ShapeDtypeStruct(t.shape, t.dtype) for t in through],
        input_output_aliases={n_in + k: 1 + k for k in range(n_thru)},
        scratch_shapes=list(scratch),
        compiler_params=pltpu.CompilerParams(vmem_limit_bytes=vmem * 2**20),
        cost_estimate=LITTLE,
    )(*inputs, *through)
    return out[0], list(out[1:])


def fixed(array):
    anywhere = pl.BlockSpec(memory_space=pl.ANY)
    return pl.pallas_call(
        lambda *refs: None,
        in_specs=[anywhere],
        out_specs=anywhere,
        out_shape=jax.ShapeDtypeStruct(array.shape, array.dtype),
        input_output_aliases={0: 0},
        cost_estimate=LITTLE,
    )(array)


def pack_kernel(*refs):
    for k, slab in enumerate(refs[:-1]):
        refs[-1][k] = slab[...]


def pack(slabs, through):
    vmem = pl.BlockSpec(memory_space=pltpu.VMEM)
    shape = jax.ShapeDtypeStruct((len(slabs),) + slabs[0].shape, slabs[0].dtype)
    return call(pack_kernel, slabs, [vmem] * len(slabs), shape, vmem, through)


def assemble_kernel(*refs):
    place_ref, packs, out_ref, whole_ref = refs[0], refs[1:-2], refs[-2], refs[-1]
    piece = packs[0].shape[2]
    for i, packed in enumerate(packs):
        for k in range(packed.shape[0]):
            start = pl.multiple_of(place_ref[i * packed.shape[0] + k] * piece, piece)
            whole_ref[:, pl.ds(start, piece), :] = packed[k]
    for b in range(out_ref.shape[0]):
        out_ref[b] = whole_ref[b].T


def assemble(packs, places, through):
    count, bb, piece, aux_len = packs[0].shape
    d_len = piece * count * len(packs)
    vmem = pl.BlockSpec(memory_space=pltpu.VMEM)
    return call(
        assemble_kernel,
        [places] + packs,
        [pl.BlockSpec(memory_space=pltpu.SMEM)] + [vmem] * len(packs),
        jax.ShapeDtypeStruct((bb, aux_len, d_len), jnp.bfloat16),
        vmem,
        through,
        scratch=[pltpu.VMEM((bb, d_len, aux_len), jnp.bfloat16)],
    )


def integral_kernel(factor_ref, batch_ref, out_ref):
    a_len, c_len, aux_len = factor_ref.shape
    d_len = out_ref.shape[3]
    rows = factor_ref[...].reshape(a_len * c_len, aux_len)
    wide = largest_part(d_len // LANES, 2) * LANES
    for b in range(out_ref.shape[1]):
        for j in range(0, d_len, wide):
            tile = lax.dot_general(
                rows, batch_ref[b, :, j : j + wide], NN, preferred_element_type=jnp.float32
            )
            turned = jnp.swapaxes(tile.reshape(a_len, c_len, wide), 0, 1)
            out_ref[:, b, :, j : j + wide] = turned.astype(jnp.bfloat16)


def integrals(factors, batch, start, stop, through):
    a_rows, c_rows, aux_len = factors.shape
    bb, _, d_len = batch.shape
    c_len = largest_part(c_rows, 8)
    first = start // c_len
    return call(
        integral_kernel,
        [factors, batch],
        [
            pl.BlockSpec((a_rows, c_len, aux_len), lambda i: (0, first + i, 0)),
            pl.BlockSpec((bb, aux_len, d_len), lambda i: (0, 0, 0)),
        ],
        jax.ShapeDtypeStruct((stop - start, bb, a_rows, d_len), jnp.bfloat16),
        pl.BlockSpec((c_len, bb, a_rows, d_len), lambda i: (i, 0, 0, 0)),
        through,
        grid=((stop - start) // c_len,),
    )


def ladder_kernel(count, *refs):
    tau_refs, (integral_ref, out_ref, total_ref) = refs[:count], refs[count:]
    c_len, bb, a_rows, d_len = integral_ref.shape
    step = pl.program_id(0)

    @pl.when(step == 0)
    def _():
        total_ref[...] = jnp.zeros_like(total_ref)

    total = total_ref[...]
    for c in range(c_len):
        left = integral_ref[c].reshape(bb * a_rows, d_len)
        right = jnp.concatenate([r[i, c] for r in tau_refs for i in range(r.shape[0])], axis=0)
        total += lax.dot_general(left, right, NT, preferred_element_type=jnp.float32)
    total_ref[...] = total

    @pl.when(step == pl.num_programs(0) - 1)
    def _():
        out_ref[...] = total_ref[...].T


def ladder_terms(taus, integral, through):
    _, c_rows, pairs, d_len = taus[0].shape
    _, bb, a_rows, _ = integral.shape
    c_len = largest_part(c_rows, 8)
    places = [t.shape[0] for t in taus]
    shape = (bb * a_rows, sum(places) * pairs)
    return call(
        functools.partial(ladder_kernel, len(taus)),
        taus + [integral],
        [pl.BlockSpec((k, c_len, pairs, d_len), lambda i: (0, i, 0, 0)) for k in places]
        + [pl.BlockSpec((c_len, bb, a_rows, d_len), lambda i: (i, 0, 0, 0))],
        jax.ShapeDtypeStruct(shape[::-1], jnp.float32),
        pl.BlockSpec(shape[::-1], lambda i: (0, 0)),
        through,
        grid=(c_rows // c_len,),
        scratch=[pltpu.VMEM(shape, jnp.float32)],
        vmem=16,
    )


def spread(rows, n, z):
    stride = 1
    while 2 * stride < n:
        stride *= 2
    while stride:
        ways = [(i, i + stride) for i in range(0, n - stride, 2 * stride)]
        here = lax.ppermute(rows, "out", ways)
        taking = functools.reduce(jnp.logical_or, [z == t for _, t in ways])
        rows = jnp.where(taking, here, rows)
        stride //= 2
    return rows


def everywhere(shared, vir, through):
    me = lax.axis_index("vir")

    def swap(array, mask):
        return lax.ppermute(array, "vir", [(k, k ^ mask) for k in range(vir)])

    if vir & (vir - 1) == 0 and 2 < vir <= 8:
        masks = list(range(0, vir, 2))
        slabs = [shared] + [swap(shared, m) for m in masks[1:]]
        packed, through = pack(slabs, through)
        packs = [packed, swap(packed, 1)]
        places = jnp.stack([me ^ m ^ core for core in (0, 1) for m in masks])
    else:
        packs = [lax.all_gather(shared, "vir", axis=1, tiled=True)[None]]
        places = jnp.zeros((1,), jnp.int32)
    return assemble(packs, places.astype(jnp.int32), through)


def body(inward, factors, amplitudes):
    a_rows, c_rows, _ = factors.shape
    pairs = amplitudes.shape[0]
    n = lax.axis_size("out")
    vir = lax.axis_size("vir")
    z = lax.axis_index("out")
    cut = c_rows - inward

    outer = fixed(amplitudes[:, :cut].transpose(1, 0, 2))
    tau = lax.all_gather(outer, "out")
    shared = spread(factors[:BB], n, z)
    token = jnp.zeros((8, LANES), jnp.float32)

    if inward:
        inner = amplitudes[:, cut:].transpose(1, 0, 2)
        batch, [token, inner] = everywhere(shared, vir, [token, inner])
        sent, [token] = integrals(factors, batch, cut, c_rows, [token])
        came = lax.ppermute(sent, "out", [(0, 1), (n - 1, n - 2)])
        kept, [token] = integrals(factors, batch, 0, cut, [token])
        below, above = [], []
        for k in range(1, n - 1):
            below.append(lax.ppermute(inner, "out", [(i, i + k) for i in range(n - 1 - k)]))
            above.append(lax.ppermute(inner, "out", [(i + k, i) for i in range(1, n - k)]))
        nearby = [t[None] for t in below[::-1] + [inner] + above]
        mine, [token] = ladder_terms(nearby, sent, [token])
        theirs, [token] = ladder_terms(nearby, came, [token])

        def all_pairs(terms):
            return lax.dynamic_slice_in_dim(terms, (n - 2 - z) * pairs, n * pairs, axis=0)

        back = lax.ppermute(all_pairs(theirs), "out", [(1, 0), (n - 2, n - 1)])
        rest = jnp.where((z == 0) | (z == n - 1), back, all_pairs(mine))
    else:
        batch, [token] = everywhere(shared, vir, [token])
        kept, [token] = integrals(factors, batch, 0, cut, [token])
        rest = jnp.zeros((n * pairs, BB * a_rows), jnp.float32)

    terms, _ = ladder_terms([tau], kept, [token])
    parts = (terms + rest).reshape(vir, -1, BB * a_rows)
    swapped = lax.all_to_all(parts, "vir", split_axis=0, concat_axis=0)
    out = jnp.sum(swapped, axis=0)
    return out.reshape(-1, BB, a_rows).transpose(1, 0, 2)


def solution(mesh):
    def run(factors, amplitudes):
        c_rows = factors.shape[1] // mesh.shape["vir"]
        inward = c_rows // 8 if c_rows % 64 == 0 and mesh.shape["out"] == 4 else 0
        placed = (P("out", "vir", None), P("out", "vir", None))
        return jax.shard_map(
            functools.partial(body, inward),
            mesh=mesh,
            in_specs=placed,
            out_specs=P(None, "vir", "out"),
            check_vma=False,
        )(factors, amplitudes)

    return run
```

```python
import functools

import jax
import jax.numpy as jnp
from jax import lax
from jax.experimental import pallas as pl
from jax.experimental.pallas import tpu as pltpu
from jax.sharding import PartitionSpec as P

BB = 2
LANES = 128
NT = (((1,), (1,)), ((), ()))
NN = (((1,), (0,)), ((), ()))
LITTLE = pl.CostEstimate(flops=1024, bytes_accessed=1024, transcendentals=0)


def largest_part(extent, limit):
    part = min(extent, limit)
    while extent % part:
        part -= 1
    return part


def call(kernel, inputs, in_specs, out_shape, out_spec, through, grid=(1,), scratch=(), vmem=28):
    n_in, n_thru = len(inputs), len(through)

    def run(*refs):
        outs = refs[n_in + n_thru :]
        kernel(*refs[:n_in], outs[0], *outs[1 + n_thru :])

    anywhere = pl.BlockSpec(memory_space=pl.ANY)
    out = pl.pallas_call(
        run,
        grid=grid,
        in_specs=list(in_specs) + [anywhere] * n_thru,
        out_specs=[out_spec] + [anywhere] * n_thru,
        out_shape=[out_shape] + [jax.ShapeDtypeStruct(t.shape, t.dtype) for t in through],
        input_output_aliases={n_in + k: 1 + k for k in range(n_thru)},
        scratch_shapes=list(scratch),
        compiler_params=pltpu.CompilerParams(vmem_limit_bytes=vmem * 2**20),
        cost_estimate=LITTLE,
    )(*inputs, *through)
    return out[0], list(out[1:])


def pack_kernel(*refs):
    for k, slab in enumerate(refs[:-1]):
        refs[-1][k] = slab[...]


def pack(slabs, through):
    vmem = pl.BlockSpec(memory_space=pltpu.VMEM)
    shape = jax.ShapeDtypeStruct((len(slabs),) + slabs[0].shape, slabs[0].dtype)
    return call(pack_kernel, slabs, [vmem] * len(slabs), shape, vmem, through)


def assemble_kernel(*refs):
    place_ref, packs, out_ref, whole_ref = refs[0], refs[1:-2], refs[-2], refs[-1]
    piece = packs[0].shape[2]
    for i, packed in enumerate(packs):
        for k in range(packed.shape[0]):
            start = pl.multiple_of(place_ref[i * packed.shape[0] + k] * piece, piece)
            whole_ref[:, pl.ds(start, piece), :] = packed[k]
    for b in range(out_ref.shape[0]):
        out_ref[b] = whole_ref[b].T


def assemble(packs, places, through):
    count, bb, piece, aux_len = packs[0].shape
    d_len = piece * count * len(packs)
    vmem = pl.BlockSpec(memory_space=pltpu.VMEM)
    return call(
        assemble_kernel,
        [places] + packs,
        [pl.BlockSpec(memory_space=pltpu.SMEM)] + [vmem] * len(packs),
        jax.ShapeDtypeStruct((bb, aux_len, d_len), jnp.bfloat16),
        vmem,
        through,
        scratch=[pltpu.VMEM((bb, d_len, aux_len), jnp.bfloat16)],
    )


def integral_kernel(factor_ref, batch_ref, out_ref):
    a_len, c_len, aux_len = factor_ref.shape
    d_len = out_ref.shape[3]
    rows = factor_ref[...].reshape(a_len * c_len, aux_len)
    wide = largest_part(d_len // LANES, 2) * LANES
    for b in range(out_ref.shape[1]):
        for j in range(0, d_len, wide):
            tile = lax.dot_general(
                rows, batch_ref[b, :, j : j + wide], NN, preferred_element_type=jnp.float32
            )
            turned = jnp.swapaxes(tile.reshape(a_len, c_len, wide), 0, 1)
            out_ref[:, b, :, j : j + wide] = turned.astype(jnp.bfloat16)


def integrals(factors, batch, start, stop, through):
    a_rows, c_rows, aux_len = factors.shape
    bb, _, d_len = batch.shape
    c_len = largest_part(c_rows, 8)
    first = start // c_len
    return call(
        integral_kernel,
        [factors, batch],
        [
            pl.BlockSpec((a_rows, c_len, aux_len), lambda i: (0, first + i, 0)),
            pl.BlockSpec((bb, aux_len, d_len), lambda i: (0, 0, 0)),
        ],
        jax.ShapeDtypeStruct((stop - start, bb, a_rows, d_len), jnp.bfloat16),
        pl.BlockSpec((c_len, bb, a_rows, d_len), lambda i: (i, 0, 0, 0)),
        through,
        grid=((stop - start) // c_len,),
    )


def sums(tau_of, integral_ref, total_ref):
    c_len, bb, a_rows, d_len = integral_ref.shape

    @pl.when(pl.program_id(0) == 0)
    def _():
        total_ref[...] = jnp.zeros_like(total_ref)

    total = total_ref[...]
    for c in range(c_len):
        left = integral_ref[c].reshape(bb * a_rows, d_len)
        total += lax.dot_general(left, tau_of(c), NT, preferred_element_type=jnp.float32)
    total_ref[...] = total


def early_kernel(count, *refs):
    tau_refs, (integral_ref, out_ref, total_ref) = refs[:count], refs[count:]
    sums(
        lambda c: jnp.concatenate([r[c] for r in tau_refs], axis=0),
        integral_ref,
        total_ref,
    )

    @pl.when(pl.program_id(0) == pl.num_programs(0) - 1)
    def _():
        out_ref[...] = total_ref[...].T


def late_kernel(count, *refs):
    slot_ref, early_ref, refs = refs[0], refs[1], refs[2:]
    tau_refs, (integral_ref, out_ref, total_ref, all_ref) = refs[:count], refs[count:]
    pairs = tau_refs[0].shape[1]
    sums(
        lambda c: jnp.concatenate([r[c] for r in tau_refs], axis=0),
        integral_ref,
        total_ref,
    )

    @pl.when(pl.program_id(0) == pl.num_programs(0) - 1)
    def _():
        known = early_ref.shape[0]
        all_ref[:known] = early_ref[...]
        all_ref[known:] = total_ref[...].T
        for j in range(out_ref.shape[0] // pairs):
            start = pl.multiple_of(slot_ref[j] * pairs, pairs)
            out_ref[j * pairs : (j + 1) * pairs] = all_ref[pl.ds(start, pairs), :]


def ladder_specs(taus, integral):
    c_rows, pairs, d_len = taus[0].shape
    _, bb, a_rows, _ = integral.shape
    c_len = largest_part(c_rows, 8)
    specs = [pl.BlockSpec((c_len, pairs, d_len), lambda i: (i, 0, 0)) for _ in taus]
    specs.append(pl.BlockSpec((c_len, bb, a_rows, d_len), lambda i: (i, 0, 0, 0)))
    return specs, (bb * a_rows, len(taus) * pairs), (c_rows // c_len,)


def ladder_early(taus, integral, through):
    specs, shape, grid = ladder_specs(taus, integral)
    return call(
        functools.partial(early_kernel, len(taus)),
        taus + [integral],
        specs,
        jax.ShapeDtypeStruct(shape[::-1], jnp.float32),
        pl.BlockSpec(shape[::-1], lambda i: (0, 0)),
        through,
        grid=grid,
        scratch=[pltpu.VMEM(shape, jnp.float32)],
        vmem=16,
    )


def ladder_late(slots, early, taus, integral, through):
    specs, shape, grid = ladder_specs(taus, integral)
    pairs = taus[0].shape[1]
    out = (slots.shape[0] * pairs, shape[0])
    return call(
        functools.partial(late_kernel, len(taus)),
        [slots, early] + taus + [integral],
        [pl.BlockSpec(memory_space=pltpu.SMEM), pl.BlockSpec(early.shape, lambda i: (0, 0))]
        + specs,
        jax.ShapeDtypeStruct(out, jnp.float32),
        pl.BlockSpec(out, lambda i: (0, 0)),
        through,
        grid=grid,
        scratch=[
            pltpu.VMEM(shape, jnp.float32),
            pltpu.VMEM((early.shape[0] + shape[1], shape[0]), jnp.float32),
        ],
        vmem=16,
    )


def spread(rows, n, z):
    stride = 1
    while 2 * stride < n:
        stride *= 2
    while stride:
        ways = [(i, i + stride) for i in range(0, n - stride, 2 * stride)]
        here = lax.ppermute(rows, "out", ways)
        taking = functools.reduce(jnp.logical_or, [z == t for _, t in ways])
        rows = jnp.where(taking, here, rows)
        stride //= 2
    return rows


def everywhere(shared, vir, through):
    me = lax.axis_index("vir")

    def swap(array, mask):
        return lax.ppermute(array, "vir", [(k, k ^ mask) for k in range(vir)])

    if vir & (vir - 1) == 0 and 2 < vir <= 8:
        masks = list(range(0, vir, 2))
        slabs = [shared] + [swap(shared, m) for m in masks[1:]]
        packed, through = pack(slabs, through)
        packs = [packed, swap(packed, 1)]
        places = jnp.stack([me ^ m ^ core for core in (0, 1) for m in masks])
    else:
        packs = [lax.all_gather(shared, "vir", axis=1, tiled=True)[None]]
        places = jnp.zeros((1,), jnp.int32)
    return assemble(packs, places.astype(jnp.int32), through)


def body(factors, amplitudes):
    a_rows, c_rows, _ = factors.shape
    n = lax.axis_size("out")
    vir = lax.axis_size("vir")
    z = lax.axis_index("out")

    def send(array, *ways):
        return lax.ppermute(array, "out", ways)

    own = amplitudes.transpose(1, 0, 2)
    if n == 4:
        first = send(amplitudes, (3, 1), (1, 0), (0, 2), (2, 3)).transpose(1, 0, 2)
        shared = spread(factors[:BB], n, z)
        second = send(own, (2, 0), (1, 3))
        third = send(first, (1, 0), (2, 3))
        middle = send(own, (2, 1), (1, 2))
        inward = send(own, (3, 2), (0, 1))
        early, late = [own, first, second], [third, middle, inward]
        slots = jnp.array([[0, 1, 2, 3], [5, 0, 4, 1], [1, 4, 0, 5], [3, 2, 1, 0]], jnp.int32)[z]
    else:
        shared = spread(factors[:BB], n, z)
        gathered = lax.all_gather(own, "out")
        early, late = [own], [gathered[k] for k in range(n)]
        slots = jnp.arange(1, n + 1, dtype=jnp.int32)

    batch, [token] = everywhere(shared, vir, [jnp.zeros((8, LANES), jnp.float32)])
    integral, [token] = integrals(factors, batch, 0, c_rows, [token])
    known, [token] = ladder_early(early, integral, [token])
    total, _ = ladder_late(slots, known, late, integral, [token])

    parts = total.reshape(vir, -1, BB * a_rows)
    swapped = lax.all_to_all(parts, "vir", split_axis=0, concat_axis=0)
    out = jnp.sum(swapped, axis=0)
    return out.reshape(-1, BB, a_rows).transpose(1, 0, 2)


def solution(mesh):
    placed = (P("out", "vir", None), P("out", "vir", None))
    return jax.shard_map(
        body, mesh=mesh, in_specs=placed, out_specs=P(None, "vir", "out"), check_vma=False
    )
```

```python
import functools

import jax
import jax.numpy as jnp
from jax import lax
from jax.experimental import pallas as pl
from jax.experimental.pallas import tpu as pltpu
from jax.sharding import PartitionSpec as P

BB = 2
LANES = 128
NT = (((1,), (1,)), ((), ()))
NN = (((1,), (0,)), ((), ()))
LITTLE = pl.CostEstimate(flops=1024, bytes_accessed=1024, transcendentals=0)


def largest_part(extent, limit):
    part = min(extent, limit)
    while extent % part:
        part -= 1
    return part


def call(kernel, inputs, in_specs, out_shape, out_spec, through, grid=(1,), scratch=(), vmem=28, into=None):
    n_in, n_thru = len(inputs), len(through)
    kept = [] if into is None else [into]
    first = n_in + len(kept)

    def run(*refs):
        outs = refs[first + n_thru :]
        kernel(*refs[:n_in], outs[0], *outs[1 + n_thru :])

    anywhere = pl.BlockSpec(memory_space=pl.ANY)
    aliases = {first + k: 1 + k for k in range(n_thru)}
    if kept:
        aliases[n_in] = 0
    out = pl.pallas_call(
        run,
        grid=grid,
        in_specs=list(in_specs) + [anywhere] * (len(kept) + n_thru),
        out_specs=[out_spec] + [anywhere] * n_thru,
        out_shape=[out_shape] + [jax.ShapeDtypeStruct(t.shape, t.dtype) for t in through],
        input_output_aliases=aliases,
        scratch_shapes=list(scratch),
        compiler_params=pltpu.CompilerParams(vmem_limit_bytes=vmem * 2**20),
        cost_estimate=LITTLE,
    )(*inputs, *kept, *through)
    return out[0], list(out[1:])


def fence(arrays):
    anywhere = [pl.BlockSpec(memory_space=pl.ANY)] * len(arrays)
    return pl.pallas_call(
        lambda *refs: None,
        in_specs=anywhere,
        out_specs=anywhere,
        out_shape=[jax.ShapeDtypeStruct(t.shape, t.dtype) for t in arrays],
        input_output_aliases={k: k for k in range(len(arrays))},
        cost_estimate=LITTLE,
    )(*arrays)


def pack_kernel(*refs):
    for k, slab in enumerate(refs[:-1]):
        refs[-1][k] = slab[...]


def pack(slabs, through):
    vmem = pl.BlockSpec(memory_space=pltpu.VMEM)
    shape = jax.ShapeDtypeStruct((len(slabs),) + slabs[0].shape, slabs[0].dtype)
    return call(pack_kernel, slabs, [vmem] * len(slabs), shape, vmem, through)


def assemble_kernel(*refs):
    place_ref, packs, out_ref, whole_ref = refs[0], refs[1:-2], refs[-2], refs[-1]
    piece = packs[0].shape[2]
    for i, packed in enumerate(packs):
        for k in range(packed.shape[0]):
            start = pl.multiple_of(place_ref[i * packed.shape[0] + k] * piece, piece)
            whole_ref[:, pl.ds(start, piece), :] = packed[k]
    for b in range(out_ref.shape[0]):
        out_ref[b] = whole_ref[b].T


def assemble(packs, places, through):
    count, bb, piece, aux_len = packs[0].shape
    d_len = piece * count * len(packs)
    vmem = pl.BlockSpec(memory_space=pltpu.VMEM)
    return call(
        assemble_kernel,
        [places] + packs,
        [pl.BlockSpec(memory_space=pltpu.SMEM)] + [vmem] * len(packs),
        jax.ShapeDtypeStruct((bb, aux_len, d_len), jnp.bfloat16),
        vmem,
        through,
        scratch=[pltpu.VMEM((bb, d_len, aux_len), jnp.bfloat16)],
    )


def integral_kernel(factor_ref, batch_ref, out_ref):
    a_len, c_len, aux_len = factor_ref.shape
    d_len = out_ref.shape[3]
    rows = factor_ref[...].reshape(a_len * c_len, aux_len)
    wide = largest_part(d_len // LANES, 2) * LANES
    for b in range(out_ref.shape[1]):
        for j in range(0, d_len, wide):
            tile = lax.dot_general(
                rows, batch_ref[b, :, j : j + wide], NN, preferred_element_type=jnp.float32
            )
            turned = jnp.swapaxes(tile.reshape(a_len, c_len, wide), 0, 1)
            out_ref[:, b, :, j : j + wide] = turned.astype(jnp.bfloat16)


def integrals(factors, batch, part, parts, through, into):
    a_rows, c_rows, aux_len = factors.shape
    bb, _, d_len = batch.shape
    c_len = largest_part(c_rows // parts, 8)
    count = c_rows // parts // c_len
    return call(
        integral_kernel,
        [factors, batch],
        [
            pl.BlockSpec((a_rows, c_len, aux_len), lambda i: (0, part * count + i, 0)),
            pl.BlockSpec((bb, aux_len, d_len), lambda i: (0, 0, 0)),
        ],
        jax.ShapeDtypeStruct((c_rows, bb, a_rows, d_len), jnp.bfloat16),
        pl.BlockSpec((c_len, bb, a_rows, d_len), lambda i: (part * count + i, 0, 0, 0)),
        through,
        grid=(count,),
        into=into,
    )


def sums(tau_of, integral_ref, total_ref):
    c_len, bb, a_rows, d_len = integral_ref.shape

    @pl.when(pl.program_id(0) == 0)
    def _():
        total_ref[...] = jnp.zeros_like(total_ref)

    total = total_ref[...]
    for c in range(c_len):
        left = integral_ref[c].reshape(bb * a_rows, d_len)
        total += lax.dot_general(left, tau_of(c), NT, preferred_element_type=jnp.float32)
    total_ref[...] = total


def early_kernel(count, *refs):
    tau_refs, (integral_ref, out_ref, total_ref) = refs[:count], refs[count:]
    sums(
        lambda c: jnp.concatenate([r[c] for r in tau_refs], axis=0),
        integral_ref,
        total_ref,
    )

    @pl.when(pl.program_id(0) == pl.num_programs(0) - 1)
    def _():
        out_ref[...] = total_ref[...].T


def late_kernel(count, *refs):
    slot_ref, early_ref, refs = refs[0], refs[1], refs[2:]
    tau_refs, (integral_ref, out_ref, total_ref, all_ref) = refs[:count], refs[count:]
    pairs = tau_refs[0].shape[1]
    sums(
        lambda c: jnp.concatenate([r[c] for r in tau_refs], axis=0),
        integral_ref,
        total_ref,
    )

    @pl.when(pl.program_id(0) == pl.num_programs(0) - 1)
    def _():
        known = early_ref.shape[0]
        all_ref[:known] = early_ref[...]
        all_ref[known:] = total_ref[...].T
        for j in range(out_ref.shape[0] // pairs):
            start = pl.multiple_of(slot_ref[j] * pairs, pairs)
            out_ref[j * pairs : (j + 1) * pairs] = all_ref[pl.ds(start, pairs), :]


def ladder_specs(taus, integral):
    c_rows, pairs, d_len = taus[0].shape
    _, bb, a_rows, _ = integral.shape
    c_len = largest_part(c_rows, 8)
    specs = [pl.BlockSpec((c_len, pairs, d_len), lambda i: (i, 0, 0)) for _ in taus]
    specs.append(pl.BlockSpec((c_len, bb, a_rows, d_len), lambda i: (i, 0, 0, 0)))
    return specs, (bb * a_rows, len(taus) * pairs), (c_rows // c_len,)


def ladder_early(taus, integral, through):
    specs, shape, grid = ladder_specs(taus, integral)
    return call(
        functools.partial(early_kernel, len(taus)),
        taus + [integral],
        specs,
        jax.ShapeDtypeStruct(shape[::-1], jnp.float32),
        pl.BlockSpec(shape[::-1], lambda i: (0, 0)),
        through,
        grid=grid,
        scratch=[pltpu.VMEM(shape, jnp.float32)],
        vmem=16,
    )


def ladder_late(slots, early, taus, integral, through):
    specs, shape, grid = ladder_specs(taus, integral)
    pairs = taus[0].shape[1]
    out = (slots.shape[0] * pairs, shape[0])
    return call(
        functools.partial(late_kernel, len(taus)),
        [slots, early] + taus + [integral],
        [pl.BlockSpec(memory_space=pltpu.SMEM), pl.BlockSpec(early.shape, lambda i: (0, 0))]
        + specs,
        jax.ShapeDtypeStruct(out, jnp.float32),
        pl.BlockSpec(out, lambda i: (0, 0)),
        through,
        grid=grid,
        scratch=[
            pltpu.VMEM(shape, jnp.float32),
            pltpu.VMEM((early.shape[0] + shape[1], shape[0]), jnp.float32),
        ],
        vmem=16,
    )


def spread(rows, n, z):
    heres = [lax.ppermute(rows, "out", [(0, k)]) for k in range(n - 1, 0, -1)]
    for k, here in zip(range(n - 1, 0, -1), heres):
        rows = jnp.where(z == k, here, rows)
    return rows


def everywhere(shared, vir, through):
    me = lax.axis_index("vir")

    def swap(array, mask):
        return lax.ppermute(array, "vir", [(k, k ^ mask) for k in range(vir)])

    if vir & (vir - 1) == 0 and 2 < vir <= 8:
        masks = list(range(0, vir, 2))
        slabs = [shared] + [swap(shared, m) for m in masks[1:]]
        packed, through = pack(slabs, through)
        packs = [packed, swap(packed, 1)]
        places = jnp.stack([me ^ m ^ core for core in (0, 1) for m in masks])
    else:
        packs = [lax.all_gather(shared, "vir", axis=1, tiled=True)[None]]
        places = jnp.zeros((1,), jnp.int32)
    return assemble(packs, places.astype(jnp.int32), through)


def body(factors, amplitudes):
    a_rows, c_rows, _ = factors.shape
    n = lax.axis_size("out")
    vir = lax.axis_size("vir")
    z = lax.axis_index("out")

    def send(array, *ways):
        return lax.ppermute(array, "out", ways)

    own = amplitudes.transpose(1, 0, 2)
    token = jnp.zeros((8, LANES), jnp.float32)
    shared = spread(factors[:BB], n, z)
    batch, [token] = everywhere(shared, vir, [token])
    if n == 4:
        far = send(own, (3, 1), (2, 0), (1, 3), (0, 2))
        near = send(own, (1, 0), (0, 1), (2, 3), (3, 2))
        integral, [token] = integrals(factors, batch, 0, 2, [token], None)
        token, far, near, own = fence([token, far, near, own])
        ends = send(far, (1, 0), (2, 3))
        middle = send(own, (2, 1), (1, 2))
        integral, [token] = integrals(factors, batch, 1, 2, [token], integral)
        early, late = [own, far, near], [ends, middle]
        slots = jnp.array([[0, 2, 1, 3], [2, 0, 4, 1], [1, 4, 0, 2], [3, 1, 2, 0]], jnp.int32)[z]
    else:
        gathered = lax.all_gather(own, "out")
        integral, [token] = integrals(factors, batch, 0, 1, [token], None)
        early, late = [own], [gathered[k] for k in range(n)]
        slots = jnp.arange(1, n + 1, dtype=jnp.int32)

    known, [token] = ladder_early(early, integral, [token])
    total, _ = ladder_late(slots, known, late, integral, [token])

    parts = total.reshape(vir, -1, BB * a_rows)
    swapped = lax.all_to_all(parts, "vir", split_axis=0, concat_axis=0)
    out = jnp.sum(swapped, axis=0)
    return out.reshape(-1, BB, a_rows).transpose(1, 0, 2)


def solution(mesh):
    placed = (P("out", "vir", None), P("out", "vir", None))
    return jax.shard_map(
        body, mesh=mesh, in_specs=placed, out_specs=P(None, "vir", "out"), check_vma=False
    )
```

```python
import functools

import jax
import jax.numpy as jnp
from jax import lax
from jax.experimental import pallas as pl
from jax.experimental.pallas import tpu as pltpu
from jax.sharding import PartitionSpec as P

BB = 2
LANES = 128
NT = (((1,), (1,)), ((), ()))
NN = (((1,), (0,)), ((), ()))
LITTLE = pl.CostEstimate(flops=1024, bytes_accessed=1024, transcendentals=0)


def largest_part(extent, limit):
    part = min(extent, limit)
    while extent % part:
        part -= 1
    return part


def call(kernel, inputs, in_specs, out_shape, out_spec, through, grid=(1,), scratch=(), vmem=28):
    n_in, n_thru = len(inputs), len(through)

    def run(*refs):
        outs = refs[n_in + n_thru :]
        kernel(*refs[:n_in], outs[0], *outs[1 + n_thru :])

    anywhere = pl.BlockSpec(memory_space=pl.ANY)
    out = pl.pallas_call(
        run,
        grid=grid,
        in_specs=list(in_specs) + [anywhere] * n_thru,
        out_specs=[out_spec] + [anywhere] * n_thru,
        out_shape=[out_shape] + [jax.ShapeDtypeStruct(t.shape, t.dtype) for t in through],
        input_output_aliases={n_in + k: 1 + k for k in range(n_thru)},
        scratch_shapes=list(scratch),
        compiler_params=pltpu.CompilerParams(vmem_limit_bytes=vmem * 2**20),
        cost_estimate=LITTLE,
    )(*inputs, *through)
    return out[0], list(out[1:])


def fence(arrays):
    anywhere = [pl.BlockSpec(memory_space=pl.ANY)] * len(arrays)
    return pl.pallas_call(
        lambda *refs: None,
        in_specs=anywhere,
        out_specs=anywhere,
        out_shape=[jax.ShapeDtypeStruct(t.shape, t.dtype) for t in arrays],
        input_output_aliases={k: k for k in range(len(arrays))},
        cost_estimate=LITTLE,
    )(*arrays)


def pack_kernel(*refs):
    for k, slab in enumerate(refs[:-1]):
        refs[-1][k] = slab[...]


def pack(slabs, through):
    vmem = pl.BlockSpec(memory_space=pltpu.VMEM)
    shape = jax.ShapeDtypeStruct((len(slabs),) + slabs[0].shape, slabs[0].dtype)
    return call(pack_kernel, slabs, [vmem] * len(slabs), shape, vmem, through)


def assemble_kernel(*refs):
    place_ref, packs, out_ref, whole_ref = refs[0], refs[1:-2], refs[-2], refs[-1]
    piece = packs[0].shape[2]
    for i, packed in enumerate(packs):
        for k in range(packed.shape[0]):
            start = pl.multiple_of(place_ref[i * packed.shape[0] + k] * piece, piece)
            whole_ref[:, pl.ds(start, piece), :] = packed[k]
    for b in range(out_ref.shape[0]):
        out_ref[b] = whole_ref[b].T


def assemble(packs, places, through):
    count, bb, piece, aux_len = packs[0].shape
    d_len = piece * count * len(packs)
    vmem = pl.BlockSpec(memory_space=pltpu.VMEM)
    return call(
        assemble_kernel,
        [places] + packs,
        [pl.BlockSpec(memory_space=pltpu.SMEM)] + [vmem] * len(packs),
        jax.ShapeDtypeStruct((bb, aux_len, d_len), jnp.bfloat16),
        vmem,
        through,
        scratch=[pltpu.VMEM((bb, d_len, aux_len), jnp.bfloat16)],
    )


def integral_kernel(factor_ref, batch_ref, out_ref):
    a_len, c_len, aux_len = factor_ref.shape
    d_len = out_ref.shape[3]
    rows = factor_ref[...].reshape(a_len * c_len, aux_len)
    wide = largest_part(d_len // LANES, 2) * LANES
    for b in range(out_ref.shape[1]):
        for j in range(0, d_len, wide):
            tile = lax.dot_general(
                rows, batch_ref[b, :, j : j + wide], NN, preferred_element_type=jnp.float32
            )
            turned = jnp.swapaxes(tile.reshape(a_len, c_len, wide), 0, 1)
            out_ref[:, b, :, j : j + wide] = turned.astype(jnp.bfloat16)


def integrals(factors, batch, part, parts, through):
    a_rows, c_rows, aux_len = factors.shape
    bb, _, d_len = batch.shape
    c_len = largest_part(c_rows // parts, 8)
    count = c_rows // parts // c_len
    return call(
        integral_kernel,
        [factors, batch],
        [
            pl.BlockSpec((a_rows, c_len, aux_len), lambda i: (0, part * count + i, 0)),
            pl.BlockSpec((bb, aux_len, d_len), lambda i: (0, 0, 0)),
        ],
        jax.ShapeDtypeStruct((c_rows // parts, bb, a_rows, d_len), jnp.bfloat16),
        pl.BlockSpec((c_len, bb, a_rows, d_len), lambda i: (i, 0, 0, 0)),
        through,
        grid=(count,),
    )


def sums(tau_of, integral_ref, total_ref):
    c_len, bb, a_rows, d_len = integral_ref.shape

    @pl.when(pl.program_id(0) == 0)
    def _():
        total_ref[...] = jnp.zeros_like(total_ref)

    total = total_ref[...]
    for c in range(c_len):
        left = integral_ref[c].reshape(bb * a_rows, d_len)
        total += lax.dot_general(left, tau_of(c), NT, preferred_element_type=jnp.float32)
    total_ref[...] = total


def early_kernel(count, *refs):
    tau_refs, (integral_ref, out_ref, total_ref) = refs[:count], refs[count:]
    sums(
        lambda c: jnp.concatenate([r[c] for r in tau_refs], axis=0),
        integral_ref,
        total_ref,
    )

    @pl.when(pl.program_id(0) == pl.num_programs(0) - 1)
    def _():
        out_ref[...] = total_ref[...].T


def late_kernel(count, *refs):
    (slot_ref, early_ref, added_ref), refs = refs[:3], refs[3:]
    tau_refs, (integral_ref, out_ref, total_ref, all_ref) = refs[:count], refs[count:]
    pairs = tau_refs[0].shape[1]
    sums(
        lambda c: jnp.concatenate([r[c] for r in tau_refs], axis=0),
        integral_ref,
        total_ref,
    )

    @pl.when(pl.program_id(0) == pl.num_programs(0) - 1)
    def _():
        known = early_ref.shape[0]
        all_ref[:known] = early_ref[...]
        all_ref[known:] = added_ref[...] + total_ref[...].T
        for j in range(out_ref.shape[0] // pairs):
            start = pl.multiple_of(slot_ref[j] * pairs, pairs)
            out_ref[j * pairs : (j + 1) * pairs] = all_ref[pl.ds(start, pairs), :]


def ladder_specs(taus, integral, start):
    _, pairs, d_len = taus[0].shape
    c_rows, bb, a_rows, _ = integral.shape
    c_len = largest_part(c_rows, 8)
    first = start // c_len
    specs = [pl.BlockSpec((c_len, pairs, d_len), lambda i: (first + i, 0, 0)) for _ in taus]
    specs.append(pl.BlockSpec((c_len, bb, a_rows, d_len), lambda i: (i, 0, 0, 0)))
    return specs, (bb * a_rows, len(taus) * pairs), (c_rows // c_len,)


def ladder_early(taus, integral, start, through):
    specs, shape, grid = ladder_specs(taus, integral, start)
    return call(
        functools.partial(early_kernel, len(taus)),
        taus + [integral],
        specs,
        jax.ShapeDtypeStruct(shape[::-1], jnp.float32),
        pl.BlockSpec(shape[::-1], lambda i: (0, 0)),
        through,
        grid=grid,
        scratch=[pltpu.VMEM(shape, jnp.float32)],
        vmem=16,
    )


def ladder_late(slots, early, added, taus, integral, start, through):
    specs, shape, grid = ladder_specs(taus, integral, start)
    pairs = taus[0].shape[1]
    out = (slots.shape[0] * pairs, shape[0])
    return call(
        functools.partial(late_kernel, len(taus)),
        [slots, early, added] + taus + [integral],
        [pl.BlockSpec(memory_space=pltpu.SMEM)]
        + [pl.BlockSpec(t.shape, lambda i: (0, 0)) for t in (early, added)]
        + specs,
        jax.ShapeDtypeStruct(out, jnp.float32),
        pl.BlockSpec(out, lambda i: (0, 0)),
        through,
        grid=grid,
        scratch=[
            pltpu.VMEM(shape, jnp.float32),
            pltpu.VMEM((early.shape[0] + shape[1], shape[0]), jnp.float32),
        ],
        vmem=16,
    )


def spread(rows, n, z):
    heres = [lax.ppermute(rows, "out", [(0, k)]) for k in range(n - 1, 0, -1)]
    for k, here in zip(range(n - 1, 0, -1), heres):
        rows = jnp.where(z == k, here, rows)
    return rows


def everywhere(shared, vir, through):
    me = lax.axis_index("vir")

    def swap(array, mask):
        return lax.ppermute(array, "vir", [(k, k ^ mask) for k in range(vir)])

    if vir & (vir - 1) == 0 and 2 < vir <= 8:
        masks = list(range(0, vir, 2))
        slabs = [shared] + [swap(shared, m) for m in masks[1:]]
        packed, through = pack(slabs, through)
        packs = [packed, swap(packed, 1)]
        places = jnp.stack([me ^ m ^ core for core in (0, 1) for m in masks])
    else:
        packs = [lax.all_gather(shared, "vir", axis=1, tiled=True)[None]]
        places = jnp.zeros((1,), jnp.int32)
    return assemble(packs, places.astype(jnp.int32), through)


def body(factors, amplitudes):
    a_rows, c_rows, _ = factors.shape
    n = lax.axis_size("out")
    vir = lax.axis_size("vir")
    z = lax.axis_index("out")

    def send(array, *ways):
        return lax.ppermute(array, "out", ways)

    own = amplitudes.transpose(1, 0, 2)
    token = jnp.zeros((8, LANES), jnp.float32)
    shared = spread(factors[:BB], n, z)
    batch, [token] = everywhere(shared, vir, [token])
    halves = 2 if c_rows % 16 == 0 else 1
    half = c_rows // halves
    made = []

    def make():
        nonlocal token
        part, [token] = integrals(factors, batch, len(made), halves, [token])
        made.append(part)

    make()
    if n == 4:
        far = send(own, (3, 1), (2, 0), (1, 3), (0, 2))
        near = send(own, (1, 0), (2, 3))
        token, far, near, own = fence([token, far, near, own])
        ends = send(far, (1, 0), (2, 3))
        middle = send(own, (2, 1), (1, 2))
        inward = send(own, (3, 2), (0, 1))
        early, late = [own, far, near], [ends, middle, inward]
        slots = jnp.array([[0, 2, 1, 3], [5, 0, 4, 1], [1, 4, 0, 5], [3, 1, 2, 0]], jnp.int32)[z]
    else:
        gathered = lax.all_gather(own, "out")
        early, late = [own], [gathered[k] for k in range(n)]
        slots = jnp.arange(1, n + 1, dtype=jnp.int32)
    while len(made) < halves:
        make()

    known, waiting = None, None
    for k, part in enumerate(made):
        terms, [token] = ladder_early(early, part, k * half, [token])
        known = terms if known is None else known + terms
    for k, part in enumerate(made[:-1]):
        terms, [token] = ladder_early(late, part, k * half, [token])
        waiting = terms if waiting is None else waiting + terms
    if waiting is None:
        waiting = jnp.zeros((sum(t.shape[1] for t in late), BB * a_rows), jnp.float32)
    total, _ = ladder_late(slots, known, waiting, late, made[-1], c_rows - half, [token])

    parts = total.reshape(vir, -1, BB * a_rows)
    swapped = lax.all_to_all(parts, "vir", split_axis=0, concat_axis=0)
    out = jnp.sum(swapped, axis=0)
    return out.reshape(-1, BB, a_rows).transpose(1, 0, 2)


def solution(mesh):
    placed = (P("out", "vir", None), P("out", "vir", None))
    return jax.shard_map(
        body, mesh=mesh, in_specs=placed, out_specs=P(None, "vir", "out"), check_vma=False
    )
```

```python
import functools

import jax
import jax.numpy as jnp
from jax import lax
from jax.experimental import pallas as pl
from jax.experimental.pallas import tpu as pltpu
from jax.sharding import PartitionSpec as P

BB = 2
LANES = 128
NT = (((1,), (1,)), ((), ()))
NN = (((1,), (0,)), ((), ()))
LITTLE = pl.CostEstimate(flops=1024, bytes_accessed=1024, transcendentals=0)
MUCH = pl.CostEstimate(flops=2 * 10**10, bytes_accessed=4 * 10**7, transcendentals=0)


def largest_part(extent, limit):
    part = min(extent, limit)
    while extent % part:
        part -= 1
    return part


def call(kernel, inputs, in_specs, out_shape, out_spec, through, grid=(1,), scratch=(), vmem=28):
    n_in, n_thru = len(inputs), len(through)

    def run(*refs):
        outs = refs[n_in + n_thru :]
        kernel(*refs[:n_in], outs[0], *outs[1 + n_thru :])

    anywhere = pl.BlockSpec(memory_space=pl.ANY)
    out = pl.pallas_call(
        run,
        grid=grid,
        in_specs=list(in_specs) + [anywhere] * n_thru,
        out_specs=[out_spec] + [anywhere] * n_thru,
        out_shape=[out_shape] + [jax.ShapeDtypeStruct(t.shape, t.dtype) for t in through],
        input_output_aliases={n_in + k: 1 + k for k in range(n_thru)},
        scratch_shapes=list(scratch),
        compiler_params=pltpu.CompilerParams(vmem_limit_bytes=vmem * 2**20),
        cost_estimate=LITTLE,
    )(*inputs, *through)
    return out[0], list(out[1:])


def fence(arrays, cost=LITTLE):
    anywhere = [pl.BlockSpec(memory_space=pl.ANY)] * len(arrays)
    return pl.pallas_call(
        lambda *refs: None,
        in_specs=anywhere,
        out_specs=anywhere,
        out_shape=[jax.ShapeDtypeStruct(t.shape, t.dtype) for t in arrays],
        input_output_aliases={k: k for k in range(len(arrays))},
        cost_estimate=cost,
    )(*arrays)


def pick_kernel(flag_ref, first_ref, other_ref, out_ref):
    @pl.when(flag_ref[0] == 1)
    def _():
        out_ref[...] = first_ref[...]

    @pl.when(flag_ref[0] == 0)
    def _():
        out_ref[...] = other_ref[...]


def pick(flag, first, other, through):
    block = (largest_part(first.shape[0], 16),) + first.shape[1:]
    spec = pl.BlockSpec(block, lambda i: (i, 0, 0))
    return call(
        pick_kernel,
        [flag.astype(jnp.int32).reshape(1), first, other],
        [pl.BlockSpec(memory_space=pltpu.SMEM), spec, spec],
        jax.ShapeDtypeStruct(first.shape, first.dtype),
        spec,
        through,
        grid=(first.shape[0] // block[0],),
    )


def pack_kernel(*refs):
    for k, slab in enumerate(refs[:-1]):
        refs[-1][k] = slab[...]


def pack(slabs, through):
    vmem = pl.BlockSpec(memory_space=pltpu.VMEM)
    shape = jax.ShapeDtypeStruct((len(slabs),) + slabs[0].shape, slabs[0].dtype)
    return call(pack_kernel, slabs, [vmem] * len(slabs), shape, vmem, through)


def assemble_kernel(*refs):
    place_ref, packs, out_ref, whole_ref = refs[0], refs[1:-2], refs[-2], refs[-1]
    piece = packs[0].shape[2]
    for i, packed in enumerate(packs):
        for k in range(packed.shape[0]):
            start = pl.multiple_of(place_ref[i * packed.shape[0] + k] * piece, piece)
            whole_ref[:, pl.ds(start, piece), :] = packed[k]
    for b in range(out_ref.shape[0]):
        out_ref[b] = whole_ref[b].T


def assemble(packs, places, through):
    count, bb, piece, aux_len = packs[0].shape
    d_len = piece * count * len(packs)
    vmem = pl.BlockSpec(memory_space=pltpu.VMEM)
    return call(
        assemble_kernel,
        [places] + packs,
        [pl.BlockSpec(memory_space=pltpu.SMEM)] + [vmem] * len(packs),
        jax.ShapeDtypeStruct((bb, aux_len, d_len), jnp.bfloat16),
        vmem,
        through,
        scratch=[pltpu.VMEM((bb, d_len, aux_len), jnp.bfloat16)],
    )


def integral_kernel(factor_ref, batch_ref, out_ref):
    a_len, c_len, aux_len = factor_ref.shape
    d_len = out_ref.shape[3]
    rows = factor_ref[...].reshape(a_len * c_len, aux_len)
    wide = largest_part(d_len // LANES, 2) * LANES
    for b in range(out_ref.shape[1]):
        for j in range(0, d_len, wide):
            tile = lax.dot_general(
                rows, batch_ref[b, :, j : j + wide], NN, preferred_element_type=jnp.float32
            )
            turned = jnp.swapaxes(tile.reshape(a_len, c_len, wide), 0, 1)
            out_ref[:, b, :, j : j + wide] = turned.astype(jnp.bfloat16)


def integrals(factors, batch, part, parts, through):
    a_rows, c_rows, aux_len = factors.shape
    bb, _, d_len = batch.shape
    c_len = largest_part(c_rows // parts, 8)
    count = c_rows // parts // c_len
    return call(
        integral_kernel,
        [factors, batch],
        [
            pl.BlockSpec((a_rows, c_len, aux_len), lambda i: (0, part * count + i, 0)),
            pl.BlockSpec((bb, aux_len, d_len), lambda i: (0, 0, 0)),
        ],
        jax.ShapeDtypeStruct((c_rows // parts, bb, a_rows, d_len), jnp.bfloat16),
        pl.BlockSpec((c_len, bb, a_rows, d_len), lambda i: (i, 0, 0, 0)),
        through,
        grid=(count,),
    )


def sums(tau_of, integral_ref, total_ref):
    c_len, bb, a_rows, d_len = integral_ref.shape

    @pl.when(pl.program_id(0) == 0)
    def _():
        total_ref[...] = jnp.zeros_like(total_ref)

    total = total_ref[...]
    for c in range(c_len):
        left = integral_ref[c].reshape(bb * a_rows, d_len)
        total += lax.dot_general(left, tau_of(c), NT, preferred_element_type=jnp.float32)
    total_ref[...] = total


def early_kernel(count, *refs):
    tau_refs, (integral_ref, out_ref, total_ref) = refs[:count], refs[count:]
    sums(
        lambda c: jnp.concatenate([r[c] for r in tau_refs], axis=0),
        integral_ref,
        total_ref,
    )

    @pl.when(pl.program_id(0) == pl.num_programs(0) - 1)
    def _():
        out_ref[...] = total_ref[...].T


def late_kernel(count, *refs):
    (slot_ref, early_ref, added_ref), refs = refs[:3], refs[3:]
    tau_refs, (integral_ref, out_ref, total_ref, all_ref) = refs[:count], refs[count:]
    pairs = tau_refs[0].shape[1]
    sums(
        lambda c: jnp.concatenate([r[c] for r in tau_refs], axis=0),
        integral_ref,
        total_ref,
    )

    @pl.when(pl.program_id(0) == pl.num_programs(0) - 1)
    def _():
        known = early_ref.shape[0]
        all_ref[:known] = early_ref[...]
        all_ref[known:] = added_ref[...] + total_ref[...].T
        owners, bb, rows, a_rows = out_ref.shape
        each = pairs // rows
        for j in range(owners):
            start = pl.multiple_of(slot_ref[j // each] * pairs, pairs) + j % each * rows
            for b in range(bb):
                out_ref[j, b] = all_ref[pl.ds(start, rows), b * a_rows : (b + 1) * a_rows]


def ladder_specs(taus, integral, start):
    _, pairs, d_len = taus[0].shape
    c_rows, bb, a_rows, _ = integral.shape
    c_len = largest_part(c_rows, 8)
    first = start // c_len
    specs = [pl.BlockSpec((c_len, pairs, d_len), lambda i: (first + i, 0, 0)) for _ in taus]
    specs.append(pl.BlockSpec((c_len, bb, a_rows, d_len), lambda i: (i, 0, 0, 0)))
    return specs, (bb * a_rows, len(taus) * pairs), (c_rows // c_len,)


def ladder_early(taus, integral, start):
    specs, shape, grid = ladder_specs(taus, integral, start)
    return call(
        functools.partial(early_kernel, len(taus)),
        taus + [integral],
        specs,
        jax.ShapeDtypeStruct(shape[::-1], jnp.float32),
        pl.BlockSpec(shape[::-1], lambda i: (0, 0)),
        [],
        grid=grid,
        scratch=[pltpu.VMEM(shape, jnp.float32)],
        vmem=16,
    )[0]


def ladder_late(slots, early, added, taus, integral, start, owners):
    specs, shape, grid = ladder_specs(taus, integral, start)
    pairs = taus[0].shape[1]
    _, bb, a_rows, _ = integral.shape
    out = (owners, bb, slots.shape[0] * pairs // owners, a_rows)
    return call(
        functools.partial(late_kernel, len(taus)),
        [slots, early, added] + taus + [integral],
        [pl.BlockSpec(memory_space=pltpu.SMEM)]
        + [pl.BlockSpec(t.shape, lambda i: (0, 0)) for t in (early, added)]
        + specs,
        jax.ShapeDtypeStruct(out, jnp.float32),
        pl.BlockSpec(out, lambda i: (0, 0, 0, 0)),
        [],
        grid=grid,
        scratch=[
            pltpu.VMEM(shape, jnp.float32),
            pltpu.VMEM((early.shape[0] + shape[1], shape[0]), jnp.float32),
        ],
        vmem=16,
    )[0]


def spread(rows, n, z):
    heres = [lax.ppermute(rows, "out", [(0, k)]) for k in range(n - 1, 0, -1)]
    for k, here in zip(range(n - 1, 0, -1), heres):
        rows = jnp.where(z == k, here, rows)
    return rows


def everywhere(shared, vir, through):
    me = lax.axis_index("vir")

    def swap(array, mask):
        return lax.ppermute(array, "vir", [(k, k ^ mask) for k in range(vir)])

    if vir & (vir - 1) == 0 and 2 < vir <= 8:
        masks = list(range(0, vir, 2))
        slabs = [shared] + [swap(shared, m) for m in masks[1:]]
        packed, through = pack(slabs, through)
        packs = [packed, swap(packed, 1)]
        places = jnp.stack([me ^ m ^ core for core in (0, 1) for m in masks])
    else:
        packs = [lax.all_gather(shared, "vir", axis=1, tiled=True)[None]]
        places = jnp.zeros((1,), jnp.int32)
    return assemble(packs, places.astype(jnp.int32), through)


def body(factors, amplitudes):
    a_rows, c_rows, _ = factors.shape
    n = lax.axis_size("out")
    vir = lax.axis_size("vir")
    z = lax.axis_index("out")

    def send(array, *ways):
        return lax.ppermute(array, "out", ways)

    own = amplitudes.transpose(1, 0, 2)
    token = jnp.zeros((8, LANES), jnp.float32)
    shared = spread(factors[:BB], n, z)
    batch, [token] = everywhere(shared, vir, [token])
    halves = 2 if c_rows % 16 == 0 else 1
    half = c_rows // halves
    made = []

    def make():
        nonlocal token
        part, [token] = integrals(factors, batch, len(made), halves, [token])
        made.append(part)

    make()
    if n == 4:
        inside = (z == 1) | (z == 2)
        first = send(own, (3, 1), (1, 0), (0, 2), (2, 3))
        second = send(own, (2, 0), (1, 3))
        onward, [token] = pick(inside, first, own, [token])
        sides = send(onward, (1, 0), (0, 1), (2, 3), (3, 2))
        token, second, own = fence([token, second, own], MUCH)
        middle = send(own, (2, 1), (1, 2))
        early, late = [own, first, second], [sides, middle]
        slots = jnp.array([[0, 1, 2, 3], [3, 0, 4, 1], [1, 4, 0, 3], [3, 2, 1, 0]], jnp.int32)[z]
    else:
        gathered = lax.all_gather(own, "out")
        early, late = [own], [gathered[k] for k in range(n)]
        slots = jnp.arange(1, n + 1, dtype=jnp.int32)
    while len(made) < halves:
        make()

    if n == 4:
        late[0] = fence(late[:1], MUCH)[0]
    known, added = None, jnp.zeros((sum(t.shape[1] for t in late), BB * a_rows), jnp.float32)
    for k, part in enumerate(made):
        terms = ladder_early(early, part, k * half)
        known = terms if known is None else known + terms
    for k, part in enumerate(made[:-1]):
        terms = ladder_early(late, part, k * half)
        added = terms if k == 0 else added + terms
    parts = ladder_late(slots, known, added, late, made[-1], c_rows - half, vir)
    swapped = lax.all_to_all(parts, "vir", split_axis=0, concat_axis=0)
    return jnp.sum(swapped, axis=0)


def solution(mesh):
    placed = (P("out", "vir", None), P("out", "vir", None))
    return jax.shard_map(
        body, mesh=mesh, in_specs=placed, out_specs=P(None, "vir", "out"), check_vma=False
    )
```

```python
import functools

import jax
import jax.numpy as jnp
from jax import lax
from jax.experimental import pallas as pl
from jax.experimental.pallas import tpu as pltpu
from jax.sharding import PartitionSpec as P

BB = 2
LANES = 128
NT = (((1,), (1,)), ((), ()))
NN = (((1,), (0,)), ((), ()))
LITTLE = pl.CostEstimate(flops=1024, bytes_accessed=1024, transcendentals=0)
MUCH = pl.CostEstimate(flops=2 * 10**10, bytes_accessed=4 * 10**7, transcendentals=0)


def largest_part(extent, limit):
    part = min(extent, limit)
    while extent % part:
        part -= 1
    return part


def call(kernel, inputs, in_specs, out_shape, out_spec, through, grid=(1,), scratch=(), vmem=20):
    n_in, n_thru = len(inputs), len(through)

    def run(*refs):
        outs = refs[n_in + n_thru :]
        kernel(*refs[:n_in], outs[0], *outs[1 + n_thru :])

    anywhere = pl.BlockSpec(memory_space=pl.ANY)
    out = pl.pallas_call(
        run,
        grid=grid,
        in_specs=list(in_specs) + [anywhere] * n_thru,
        out_specs=[out_spec] + [anywhere] * n_thru,
        out_shape=[out_shape] + [jax.ShapeDtypeStruct(t.shape, t.dtype) for t in through],
        input_output_aliases={n_in + k: 1 + k for k in range(n_thru)},
        scratch_shapes=list(scratch),
        compiler_params=pltpu.CompilerParams(vmem_limit_bytes=vmem * 2**20),
        cost_estimate=LITTLE,
    )(*inputs, *through)
    return out[0], list(out[1:])


def fence(arrays, cost=LITTLE):
    anywhere = [pl.BlockSpec(memory_space=pl.ANY)] * len(arrays)
    return pl.pallas_call(
        lambda *refs: None,
        in_specs=anywhere,
        out_specs=anywhere,
        out_shape=[jax.ShapeDtypeStruct(t.shape, t.dtype) for t in arrays],
        input_output_aliases={k: k for k in range(len(arrays))},
        cost_estimate=cost,
    )(*arrays)


def pick_kernel(flag_ref, first_ref, other_ref, out_ref):
    @pl.when(flag_ref[0] == 1)
    def _():
        out_ref[...] = first_ref[...]

    @pl.when(flag_ref[0] == 0)
    def _():
        out_ref[...] = other_ref[...]


def pick(flag, first, other, through):
    block = (largest_part(first.shape[0], 16),) + first.shape[1:]
    spec = pl.BlockSpec(block, lambda i: (i, 0, 0))
    return call(
        pick_kernel,
        [flag.astype(jnp.int32).reshape(1), first, other],
        [pl.BlockSpec(memory_space=pltpu.SMEM), spec, spec],
        jax.ShapeDtypeStruct(first.shape, first.dtype),
        spec,
        through,
        grid=(first.shape[0] // block[0],),
    )


def pack_kernel(*refs):
    for k, slab in enumerate(refs[:-1]):
        refs[-1][k] = slab[...]


def pack(slabs, through):
    vmem = pl.BlockSpec(memory_space=pltpu.VMEM)
    shape = jax.ShapeDtypeStruct((len(slabs),) + slabs[0].shape, slabs[0].dtype)
    return call(pack_kernel, slabs, [vmem] * len(slabs), shape, vmem, through)


def assemble_kernel(*refs):
    place_ref, packs, out_ref, whole_ref = refs[0], refs[1:-2], refs[-2], refs[-1]
    piece = packs[0].shape[2]
    for i, packed in enumerate(packs):
        for k in range(packed.shape[0]):
            start = pl.multiple_of(place_ref[i * packed.shape[0] + k] * piece, piece)
            whole_ref[:, pl.ds(start, piece), :] = packed[k]
    for b in range(out_ref.shape[0]):
        out_ref[b] = whole_ref[b].T


def assemble(packs, places, through):
    count, bb, piece, aux_len = packs[0].shape
    d_len = piece * count * len(packs)
    vmem = pl.BlockSpec(memory_space=pltpu.VMEM)
    return call(
        assemble_kernel,
        [places] + packs,
        [pl.BlockSpec(memory_space=pltpu.SMEM)] + [vmem] * len(packs),
        jax.ShapeDtypeStruct((bb, aux_len, d_len), jnp.bfloat16),
        vmem,
        through,
        scratch=[pltpu.VMEM((bb, d_len, aux_len), jnp.bfloat16)],
    )


def integral_kernel(factor_ref, batch_ref, out_ref):
    a_len, c_len, aux_len = factor_ref.shape
    d_len = out_ref.shape[3]
    rows = factor_ref[...].reshape(a_len * c_len, aux_len)
    wide = largest_part(d_len // LANES, 2) * LANES
    for b in range(out_ref.shape[1]):
        for j in range(0, d_len, wide):
            tile = lax.dot_general(
                rows, batch_ref[b, :, j : j + wide], NN, preferred_element_type=jnp.float32
            )
            turned = jnp.swapaxes(tile.reshape(a_len, c_len, wide), 0, 1)
            out_ref[:, b, :, j : j + wide] = turned.astype(jnp.bfloat16)


def integrals(factors, batch, part, parts, through):
    a_rows, c_rows, aux_len = factors.shape
    bb, _, d_len = batch.shape
    c_len = largest_part(c_rows // parts, 8)
    count = c_rows // parts // c_len
    return call(
        integral_kernel,
        [factors, batch],
        [
            pl.BlockSpec((a_rows, c_len, aux_len), lambda i: (0, part * count + i, 0)),
            pl.BlockSpec((bb, aux_len, d_len), lambda i: (0, 0, 0)),
        ],
        jax.ShapeDtypeStruct((c_rows // parts, bb, a_rows, d_len), jnp.bfloat16),
        pl.BlockSpec((c_len, bb, a_rows, d_len), lambda i: (i, 0, 0, 0)),
        through,
        grid=(count,),
    )


def sums(tau_of, integral_ref, total_ref):
    c_len, bb, a_rows, d_len = integral_ref.shape

    @pl.when(pl.program_id(0) == 0)
    def _():
        total_ref[...] = jnp.zeros_like(total_ref)

    left = [integral_ref[c].reshape(bb * a_rows, d_len) for c in range(c_len)]
    right = [tau_of(c) for c in range(c_len)]
    total_ref[...] += lax.dot_general(
        jnp.concatenate(left, axis=1),
        jnp.concatenate(right, axis=1),
        NT,
        preferred_element_type=jnp.float32,
    )


def early_kernel(count, *refs):
    tau_refs, (integral_ref, out_ref, total_ref) = refs[:count], refs[count:]
    sums(
        lambda c: jnp.concatenate([r[c] for r in tau_refs], axis=0),
        integral_ref,
        total_ref,
    )

    @pl.when(pl.program_id(0) == pl.num_programs(0) - 1)
    def _():
        out_ref[...] = total_ref[...].T


def late_kernel(count, *refs):
    (slot_ref, early_ref, added_ref), refs = refs[:3], refs[3:]
    tau_refs, (integral_ref, out_ref, total_ref, all_ref) = refs[:count], refs[count:]
    pairs = tau_refs[0].shape[1]
    sums(
        lambda c: jnp.concatenate([r[c] for r in tau_refs], axis=0),
        integral_ref,
        total_ref,
    )

    @pl.when(pl.program_id(0) == pl.num_programs(0) - 1)
    def _():
        known = early_ref.shape[0]
        all_ref[:known] = early_ref[...]
        all_ref[known:] = added_ref[...] + total_ref[...].T
        owners, bb, rows, a_rows = out_ref.shape
        each = pairs // rows
        for j in range(owners):
            start = pl.multiple_of(slot_ref[j // each] * pairs, pairs) + j % each * rows
            for b in range(bb):
                out_ref[j, b] = all_ref[pl.ds(start, rows), b * a_rows : (b + 1) * a_rows]


def ladder_specs(taus, integral, start):
    _, pairs, d_len = taus[0].shape
    c_rows, bb, a_rows, _ = integral.shape
    c_len = largest_part(c_rows, 8)
    first = start // c_len
    specs = [pl.BlockSpec((c_len, pairs, d_len), lambda i: (first + i, 0, 0)) for _ in taus]
    specs.append(pl.BlockSpec((c_len, bb, a_rows, d_len), lambda i: (i, 0, 0, 0)))
    return specs, (bb * a_rows, len(taus) * pairs), (c_rows // c_len,)


def ladder_early(taus, integral, start):
    specs, shape, grid = ladder_specs(taus, integral, start)
    return call(
        functools.partial(early_kernel, len(taus)),
        taus + [integral],
        specs,
        jax.ShapeDtypeStruct(shape[::-1], jnp.float32),
        pl.BlockSpec(shape[::-1], lambda i: (0, 0)),
        [],
        grid=grid,
        scratch=[pltpu.VMEM(shape, jnp.float32)],
        vmem=10,
    )[0]


def ladder_late(slots, early, added, taus, integral, start, owners):
    specs, shape, grid = ladder_specs(taus, integral, start)
    pairs = taus[0].shape[1]
    _, bb, a_rows, _ = integral.shape
    out = (owners, bb, slots.shape[0] * pairs // owners, a_rows)
    return call(
        functools.partial(late_kernel, len(taus)),
        [slots, early, added] + taus + [integral],
        [pl.BlockSpec(memory_space=pltpu.SMEM)]
        + [pl.BlockSpec(t.shape, lambda i: (0, 0)) for t in (early, added)]
        + specs,
        jax.ShapeDtypeStruct(out, jnp.float32),
        pl.BlockSpec(out, lambda i: (0, 0, 0, 0)),
        [],
        grid=grid,
        scratch=[
            pltpu.VMEM(shape, jnp.float32),
            pltpu.VMEM((early.shape[0] + shape[1], shape[0]), jnp.float32),
        ],
        vmem=10,
    )[0]


def spread(rows, n, z):
    heres = [lax.ppermute(rows, "out", [(0, k)]) for k in range(n - 1, 0, -1)]
    for k, here in zip(range(n - 1, 0, -1), heres):
        rows = jnp.where(z == k, here, rows)
    return rows


def everywhere(shared, vir, through):
    me = lax.axis_index("vir")

    def swap(array, mask):
        return lax.ppermute(array, "vir", [(k, k ^ mask) for k in range(vir)])

    if vir & (vir - 1) == 0 and 2 < vir <= 8:
        masks = list(range(0, vir, 2))
        slabs = [shared] + [swap(shared, m) for m in masks[1:]]
        packed, through = pack(slabs, through)
        packs = [packed, swap(packed, 1)]
        places = jnp.stack([me ^ m ^ core for core in (0, 1) for m in masks])
    else:
        packs = [lax.all_gather(shared, "vir", axis=1, tiled=True)[None]]
        places = jnp.zeros((1,), jnp.int32)
    return assemble(packs, places.astype(jnp.int32), through)


def body(factors, amplitudes):
    a_rows, c_rows, _ = factors.shape
    n = lax.axis_size("out")
    vir = lax.axis_size("vir")
    z = lax.axis_index("out")

    def send(array, *ways):
        return lax.ppermute(array, "out", ways)

    own = amplitudes.transpose(1, 0, 2)
    token = jnp.zeros((8, LANES), jnp.float32)
    shared = spread(factors[:BB], n, z)
    batch, [token] = everywhere(shared, vir, [token])
    halves = 2 if c_rows % 16 == 0 else 1
    half = c_rows // halves
    made = []

    def make():
        nonlocal token
        part, [token] = integrals(factors, batch, len(made), halves, [token])
        made.append(part)

    make()
    if n == 4:
        inside = (z == 1) | (z == 2)
        first = send(own, (3, 1), (1, 0), (0, 2), (2, 3))
        second = send(own, (2, 0), (1, 3))
        onward, [token] = pick(inside, first, own, [token])
        sides = send(onward, (1, 0), (0, 1), (2, 3), (3, 2))
        token, second, own = fence([token, second, own], MUCH)
        middle = send(own, (2, 1), (1, 2))
        early, late = [own, first, second], [sides, middle]
        slots = jnp.array([[0, 1, 2, 3], [3, 0, 4, 1], [1, 4, 0, 3], [3, 2, 1, 0]], jnp.int32)[z]
    else:
        gathered = lax.all_gather(own, "out")
        early, late = [own], [gathered[k] for k in range(n)]
        slots = jnp.arange(1, n + 1, dtype=jnp.int32)
    while len(made) < halves:
        make()

    if n == 4:
        late[0] = fence(late[:1], MUCH)[0]
    known, added = None, jnp.zeros((sum(t.shape[1] for t in late), BB * a_rows), jnp.float32)
    for k, part in enumerate(made):
        terms = ladder_early(early, part, k * half)
        known = terms if known is None else known + terms
    for k, part in enumerate(made[:-1]):
        terms = ladder_early(late, part, k * half)
        added = terms if k == 0 else added + terms
    parts = ladder_late(slots, known, added, late, made[-1], c_rows - half, vir)
    swapped = lax.all_to_all(parts, "vir", split_axis=0, concat_axis=0)
    return jnp.sum(swapped, axis=0)


def solution(mesh):
    placed = (P("out", "vir", None), P("out", "vir", None))
    return jax.shard_map(
        body, mesh=mesh, in_specs=placed, out_specs=P(None, "vir", "out"), check_vma=False
    )
```

```python
import functools

import jax
import jax.numpy as jnp
from jax import lax
from jax.experimental import pallas as pl
from jax.experimental.pallas import tpu as pltpu
from jax.sharding import PartitionSpec as P

BB = 2
LANES = 128
NT = (((1,), (1,)), ((), ()))
NN = (((1,), (0,)), ((), ()))
LITTLE = pl.CostEstimate(flops=1024, bytes_accessed=1024, transcendentals=0)
MUCH = pl.CostEstimate(flops=2 * 10**10, bytes_accessed=4 * 10**7, transcendentals=0)


def largest_part(extent, limit):
    part = min(extent, limit)
    while extent % part:
        part -= 1
    return part


def call(kernel, inputs, in_specs, out_shape, out_spec, through, grid=(1,), scratch=(), vmem=52):
    n_in, n_thru = len(inputs), len(through)

    def run(*refs):
        outs = refs[n_in + n_thru :]
        kernel(*refs[:n_in], outs[0], *outs[1 + n_thru :])

    anywhere = pl.BlockSpec(memory_space=pl.ANY)
    out = pl.pallas_call(
        run,
        grid=grid,
        in_specs=list(in_specs) + [anywhere] * n_thru,
        out_specs=[out_spec] + [anywhere] * n_thru,
        out_shape=[out_shape] + [jax.ShapeDtypeStruct(t.shape, t.dtype) for t in through],
        input_output_aliases={n_in + k: 1 + k for k in range(n_thru)},
        scratch_shapes=list(scratch),
        compiler_params=pltpu.CompilerParams(vmem_limit_bytes=vmem * 2**20),
        cost_estimate=LITTLE,
    )(*inputs, *through)
    return out[0], list(out[1:])


def fence(arrays, cost=LITTLE):
    anywhere = [pl.BlockSpec(memory_space=pl.ANY)] * len(arrays)
    return pl.pallas_call(
        lambda *refs: None,
        in_specs=anywhere,
        out_specs=anywhere,
        out_shape=[jax.ShapeDtypeStruct(t.shape, t.dtype) for t in arrays],
        input_output_aliases={k: k for k in range(len(arrays))},
        cost_estimate=cost,
    )(*arrays)


def pick_kernel(flag_ref, first_ref, other_ref, out_ref):
    @pl.when(flag_ref[0] == 1)
    def _():
        out_ref[...] = first_ref[...]

    @pl.when(flag_ref[0] == 0)
    def _():
        out_ref[...] = other_ref[...]


def pick(flag, first, other, start, stop, through):
    c_len = largest_part(stop - start, 16)
    begin = start // c_len
    block = (c_len,) + first.shape[1:]
    spec = pl.BlockSpec(block, lambda i: (begin + i, 0, 0))
    return call(
        pick_kernel,
        [flag.astype(jnp.int32).reshape(1), first, other],
        [pl.BlockSpec(memory_space=pltpu.SMEM), spec, spec],
        jax.ShapeDtypeStruct((stop - start,) + first.shape[1:], first.dtype),
        pl.BlockSpec(block, lambda i: (i, 0, 0)),
        through,
        grid=((stop - start) // c_len,),
    )


def pack_kernel(*refs):
    for k, slab in enumerate(refs[:-1]):
        refs[-1][k] = slab[...]


def pack(slabs, through):
    vmem = pl.BlockSpec(memory_space=pltpu.VMEM)
    shape = jax.ShapeDtypeStruct((len(slabs),) + slabs[0].shape, slabs[0].dtype)
    return call(pack_kernel, slabs, [vmem] * len(slabs), shape, vmem, through)


def assemble_kernel(*refs):
    place_ref, packs, out_ref, whole_ref = refs[0], refs[1:-2], refs[-2], refs[-1]
    piece = packs[0].shape[2]
    for i, packed in enumerate(packs):
        for k in range(packed.shape[0]):
            start = pl.multiple_of(place_ref[i * packed.shape[0] + k] * piece, piece)
            whole_ref[:, pl.ds(start, piece), :] = packed[k]
    for b in range(out_ref.shape[0]):
        out_ref[b] = whole_ref[b].T


def assemble(packs, places, through):
    count, bb, piece, aux_len = packs[0].shape
    d_len = piece * count * len(packs)
    vmem = pl.BlockSpec(memory_space=pltpu.VMEM)
    return call(
        assemble_kernel,
        [places] + packs,
        [pl.BlockSpec(memory_space=pltpu.SMEM)] + [vmem] * len(packs),
        jax.ShapeDtypeStruct((bb, aux_len, d_len), jnp.bfloat16),
        vmem,
        through,
        scratch=[pltpu.VMEM((bb, d_len, aux_len), jnp.bfloat16)],
    )


def integral_kernel(factor_ref, batch_ref, out_ref):
    a_len, c_len, aux_len = factor_ref.shape
    d_len = out_ref.shape[3]
    rows = factor_ref[...].reshape(a_len * c_len, aux_len)
    wide = largest_part(d_len // LANES, 2) * LANES
    for b in range(out_ref.shape[1]):
        for j in range(0, d_len, wide):
            tile = lax.dot_general(
                rows, batch_ref[b, :, j : j + wide], NN, preferred_element_type=jnp.float32
            )
            turned = jnp.swapaxes(tile.reshape(a_len, c_len, wide), 0, 1)
            out_ref[:, b, :, j : j + wide] = turned.astype(jnp.bfloat16)


def integrals(factors, batch, start, stop, through):
    a_rows, c_rows, aux_len = factors.shape
    bb, _, d_len = batch.shape
    c_len = largest_part(c_rows, 8)
    first = start // c_len
    return call(
        integral_kernel,
        [factors, batch],
        [
            pl.BlockSpec((a_rows, c_len, aux_len), lambda i: (0, first + i, 0)),
            pl.BlockSpec((bb, aux_len, d_len), lambda i: (0, 0, 0)),
        ],
        jax.ShapeDtypeStruct((stop - start, bb, a_rows, d_len), jnp.bfloat16),
        pl.BlockSpec((c_len, bb, a_rows, d_len), lambda i: (i, 0, 0, 0)),
        through,
        grid=((stop - start) // c_len,),
    )


def sums(tau_of, integral_ref, total_ref):
    c_len, bb, a_rows, d_len = integral_ref.shape

    @pl.when(pl.program_id(0) == 0)
    def _():
        total_ref[...] = jnp.zeros_like(total_ref)

    left = [integral_ref[c].reshape(bb * a_rows, d_len) for c in range(c_len)]
    right = [tau_of(c) for c in range(c_len)]
    total_ref[...] += lax.dot_general(
        jnp.concatenate(left, axis=1),
        jnp.concatenate(right, axis=1),
        NT,
        preferred_element_type=jnp.float32,
    )


def early_kernel(count, *refs):
    tau_refs, (integral_ref, out_ref, total_ref) = refs[:count], refs[count:]
    sums(
        lambda c: jnp.concatenate([r[c] for r in tau_refs], axis=0),
        integral_ref,
        total_ref,
    )

    @pl.when(pl.program_id(0) == pl.num_programs(0) - 1)
    def _():
        out_ref[...] = total_ref[...].T


def late_kernel(count, *refs):
    (slot_ref, early_ref, added_ref), refs = refs[:3], refs[3:]
    tau_refs, (integral_ref, out_ref, total_ref, all_ref) = refs[:count], refs[count:]
    pairs = tau_refs[0].shape[1]
    sums(
        lambda c: jnp.concatenate([r[c] for r in tau_refs], axis=0),
        integral_ref,
        total_ref,
    )

    @pl.when(pl.program_id(0) == pl.num_programs(0) - 1)
    def _():
        known = early_ref.shape[0]
        all_ref[:known] = early_ref[...]
        all_ref[known:] = added_ref[...] + total_ref[...].T
        owners, bb, rows, a_rows = out_ref.shape
        each = pairs // rows
        for j in range(owners):
            start = pl.multiple_of(slot_ref[j // each] * pairs, pairs) + j % each * rows
            for b in range(bb):
                out_ref[j, b] = all_ref[pl.ds(start, rows), b * a_rows : (b + 1) * a_rows]


def ladder_specs(taus, integral, start):
    _, pairs, d_len = taus[0].shape
    c_rows, bb, a_rows, _ = integral.shape
    c_len = largest_part(c_rows, 8)
    first = start // c_len
    specs = [pl.BlockSpec((c_len, pairs, d_len), lambda i: (first + i, 0, 0)) for _ in taus]
    specs.append(pl.BlockSpec((c_len, bb, a_rows, d_len), lambda i: (i, 0, 0, 0)))
    return specs, (bb * a_rows, len(taus) * pairs), (c_rows // c_len,)


def ladder_early(taus, integral, start):
    specs, shape, grid = ladder_specs(taus, integral, start)
    return call(
        functools.partial(early_kernel, len(taus)),
        taus + [integral],
        specs,
        jax.ShapeDtypeStruct(shape[::-1], jnp.float32),
        pl.BlockSpec(shape[::-1], lambda i: (0, 0)),
        [],
        grid=grid,
        scratch=[pltpu.VMEM(shape, jnp.float32)],
        vmem=52,
    )[0]


def ladder_late(slots, early, added, taus, integral, start, owners):
    specs, shape, grid = ladder_specs(taus, integral, start)
    pairs = taus[0].shape[1]
    _, bb, a_rows, _ = integral.shape
    out = (owners, bb, slots.shape[0] * pairs // owners, a_rows)
    return call(
        functools.partial(late_kernel, len(taus)),
        [slots, early, added] + taus + [integral],
        [pl.BlockSpec(memory_space=pltpu.SMEM)]
        + [pl.BlockSpec(t.shape, lambda i: (0, 0)) for t in (early, added)]
        + specs,
        jax.ShapeDtypeStruct(out, jnp.float32),
        pl.BlockSpec(out, lambda i: (0, 0, 0, 0)),
        [],
        grid=grid,
        scratch=[
            pltpu.VMEM(shape, jnp.float32),
            pltpu.VMEM((early.shape[0] + shape[1], shape[0]), jnp.float32),
        ],
        vmem=52,
    )[0]


def spread(rows, n, z):
    heres = [lax.ppermute(rows, "out", [(0, k)]) for k in range(n - 1, 0, -1)]
    for k, here in zip(range(n - 1, 0, -1), heres):
        rows = jnp.where(z == k, here, rows)
    return rows


def everywhere(shared, vir, through):
    me = lax.axis_index("vir")

    def swap(array, mask):
        return lax.ppermute(array, "vir", [(k, k ^ mask) for k in range(vir)])

    if vir & (vir - 1) == 0 and 2 < vir <= 8:
        masks = list(range(0, vir, 2))
        slabs = [shared] + [swap(shared, m) for m in masks[1:]]
        packed, through = pack(slabs, through)
        packs = [packed, swap(packed, 1)]
        places = jnp.stack([me ^ m ^ core for core in (0, 1) for m in masks])
    else:
        packs = [lax.all_gather(shared, "vir", axis=1, tiled=True)[None]]
        places = jnp.zeros((1,), jnp.int32)
    return assemble(packs, places.astype(jnp.int32), through)


def body(factors, amplitudes):
    a_rows, c_rows, _ = factors.shape
    n = lax.axis_size("out")
    vir = lax.axis_size("vir")
    z = lax.axis_index("out")

    def send(array, *ways):
        return lax.ppermute(array, "out", ways)

    own = amplitudes.transpose(1, 0, 2)
    token = jnp.zeros((8, LANES), jnp.float32)
    shared = spread(factors[:BB], n, z)
    batch, [token] = everywhere(shared, vir, [token])
    cut = 3 * c_rows // 4 if c_rows % 64 == 0 else c_rows
    spans = [(0, cut), (cut, c_rows)] if cut < c_rows else [(0, c_rows)]
    made = []

    def make():
        nonlocal token
        part, [token] = integrals(factors, batch, *spans[len(made)], [token])
        made.append(part)

    make()
    if n == 4:
        inside = (z == 1) | (z == 2)
        first = send(own, (3, 1), (1, 0), (0, 2), (2, 3))
        second = send(own, (2, 0), (1, 3))
        onward = []
        for span in spans:
            part, [token] = pick(inside, first, own, *span, [token])
            onward.append(part)
        token, second, *kept = fence([token, second] + [own[i:j] for i, j in spans], MUCH)
        late = []
        for part, mine in zip(onward, kept):
            middle = send(mine, (2, 1), (1, 2))
            late.append([send(part, (1, 0), (0, 1), (2, 3), (3, 2)), middle])
        early = [own, first, second]
        slots = jnp.array([[0, 1, 2, 3], [3, 0, 4, 1], [1, 4, 0, 3], [3, 2, 1, 0]], jnp.int32)[z]
    else:
        gathered = lax.all_gather(own, "out")
        early, late = [own], [[gathered[k, i:j] for k in range(n)] for i, j in spans]
        slots = jnp.arange(1, n + 1, dtype=jnp.int32)
    while len(made) < len(spans):
        make()

    known, added = None, None
    for part, (start, _) in zip(made, spans):
        terms = ladder_early(early, part, start)
        known = terms if known is None else known + terms
    for part, taus in zip(made[:-1], late):
        added = ladder_early(taus, part, 0)
    if added is None:
        added = jnp.zeros((sum(t.shape[1] for t in late[-1]), BB * a_rows), jnp.float32)
    parts = ladder_late(slots, known, added, late[-1], made[-1], 0, vir)
    swapped = lax.all_to_all(parts, "vir", split_axis=0, concat_axis=0)
    return jnp.sum(swapped, axis=0)


def solution(mesh):
    placed = (P("out", "vir", None), P("out", "vir", None))
    return jax.shard_map(
        body, mesh=mesh, in_specs=placed, out_specs=P(None, "vir", "out"), check_vma=False
    )
```

```python
import functools

import jax
import jax.numpy as jnp
from jax import lax
from jax.experimental import pallas as pl
from jax.experimental.pallas import tpu as pltpu
from jax.sharding import PartitionSpec as P

BB = 2
LANES = 128
NT = (((1,), (1,)), ((), ()))
NN = (((1,), (0,)), ((), ()))
LITTLE = pl.CostEstimate(flops=1024, bytes_accessed=1024, transcendentals=0)
MORE = pl.CostEstimate(flops=24 * 10**9, bytes_accessed=48 * 10**6, transcendentals=0)
MUCH = pl.CostEstimate(flops=2 * 10**10, bytes_accessed=4 * 10**7, transcendentals=0)


def largest_part(extent, limit):
    part = min(extent, limit)
    while extent % part:
        part -= 1
    return part


def call(kernel, inputs, in_specs, out_shape, out_spec, through, grid=(1,), scratch=(), vmem=52):
    n_in, n_thru = len(inputs), len(through)

    def run(*refs):
        outs = refs[n_in + n_thru :]
        kernel(*refs[:n_in], outs[0], *outs[1 + n_thru :])

    anywhere = pl.BlockSpec(memory_space=pl.ANY)
    out = pl.pallas_call(
        run,
        grid=grid,
        in_specs=list(in_specs) + [anywhere] * n_thru,
        out_specs=[out_spec] + [anywhere] * n_thru,
        out_shape=[out_shape] + [jax.ShapeDtypeStruct(t.shape, t.dtype) for t in through],
        input_output_aliases={n_in + k: 1 + k for k in range(n_thru)},
        scratch_shapes=list(scratch),
        compiler_params=pltpu.CompilerParams(vmem_limit_bytes=vmem * 2**20),
        cost_estimate=LITTLE,
    )(*inputs, *through)
    return out[0], list(out[1:])


def fence(arrays, cost=LITTLE):
    anywhere = [pl.BlockSpec(memory_space=pl.ANY)] * len(arrays)
    return pl.pallas_call(
        lambda *refs: None,
        in_specs=anywhere,
        out_specs=anywhere,
        out_shape=[jax.ShapeDtypeStruct(t.shape, t.dtype) for t in arrays],
        input_output_aliases={k: k for k in range(len(arrays))},
        cost_estimate=cost,
    )(*arrays)


def pick_kernel(flag_ref, first_ref, other_ref, out_ref):
    @pl.when(flag_ref[0] == 1)
    def _():
        out_ref[...] = first_ref[...]

    @pl.when(flag_ref[0] == 0)
    def _():
        out_ref[...] = other_ref[...]


def pick(flag, first, other, start, stop, through):
    c_len = largest_part(stop - start, 16)
    begin = start // c_len
    block = (c_len,) + first.shape[1:]
    spec = pl.BlockSpec(block, lambda i: (begin + i, 0, 0))
    return call(
        pick_kernel,
        [flag.astype(jnp.int32).reshape(1), first, other],
        [pl.BlockSpec(memory_space=pltpu.SMEM), spec, spec],
        jax.ShapeDtypeStruct((stop - start,) + first.shape[1:], first.dtype),
        pl.BlockSpec(block, lambda i: (i, 0, 0)),
        through,
        grid=((stop - start) // c_len,),
    )


def pack_kernel(*refs):
    for k, slab in enumerate(refs[:-1]):
        refs[-1][k] = slab[...]


def pack(slabs, through):
    vmem = pl.BlockSpec(memory_space=pltpu.VMEM)
    shape = jax.ShapeDtypeStruct((len(slabs),) + slabs[0].shape, slabs[0].dtype)
    return call(pack_kernel, slabs, [vmem] * len(slabs), shape, vmem, through)


def assemble_kernel(*refs):
    place_ref, packs, out_ref, whole_ref = refs[0], refs[1:-2], refs[-2], refs[-1]
    piece = packs[0].shape[2]
    for i, packed in enumerate(packs):
        for k in range(packed.shape[0]):
            start = pl.multiple_of(place_ref[i * packed.shape[0] + k] * piece, piece)
            whole_ref[:, pl.ds(start, piece), :] = packed[k]
    for b in range(out_ref.shape[0]):
        out_ref[b] = whole_ref[b].T


def assemble(packs, places, through):
    count, bb, piece, aux_len = packs[0].shape
    d_len = piece * count * len(packs)
    vmem = pl.BlockSpec(memory_space=pltpu.VMEM)
    return call(
        assemble_kernel,
        [places] + packs,
        [pl.BlockSpec(memory_space=pltpu.SMEM)] + [vmem] * len(packs),
        jax.ShapeDtypeStruct((bb, aux_len, d_len), jnp.bfloat16),
        vmem,
        through,
        scratch=[pltpu.VMEM((bb, d_len, aux_len), jnp.bfloat16)],
    )


def integral_kernel(factor_ref, batch_ref, out_ref):
    a_len, c_len, aux_len = factor_ref.shape
    d_len = out_ref.shape[3]
    rows = factor_ref[...].reshape(a_len * c_len, aux_len)
    wide = largest_part(d_len // LANES, 2) * LANES
    for b in range(out_ref.shape[1]):
        for j in range(0, d_len, wide):
            tile = lax.dot_general(
                rows, batch_ref[b, :, j : j + wide], NN, preferred_element_type=jnp.float32
            )
            turned = jnp.swapaxes(tile.reshape(a_len, c_len, wide), 0, 1)
            out_ref[:, b, :, j : j + wide] = turned.astype(jnp.bfloat16)


def integrals(factors, batch, start, stop, through):
    a_rows, c_rows, aux_len = factors.shape
    bb, _, d_len = batch.shape
    c_len = largest_part(c_rows, 8)
    first = start // c_len
    return call(
        integral_kernel,
        [factors, batch],
        [
            pl.BlockSpec((a_rows, c_len, aux_len), lambda i: (0, first + i, 0)),
            pl.BlockSpec((bb, aux_len, d_len), lambda i: (0, 0, 0)),
        ],
        jax.ShapeDtypeStruct((stop - start, bb, a_rows, d_len), jnp.bfloat16),
        pl.BlockSpec((c_len, bb, a_rows, d_len), lambda i: (i, 0, 0, 0)),
        through,
        grid=((stop - start) // c_len,),
    )


def sums(tau_of, integral_ref, total_ref):
    c_len, bb, a_rows, d_len = integral_ref.shape

    @pl.when(pl.program_id(0) == 0)
    def _():
        total_ref[...] = jnp.zeros_like(total_ref)

    left = [integral_ref[c].reshape(bb * a_rows, d_len) for c in range(c_len)]
    right = [tau_of(c) for c in range(c_len)]
    total_ref[...] += lax.dot_general(
        jnp.concatenate(left, axis=1),
        jnp.concatenate(right, axis=1),
        NT,
        preferred_element_type=jnp.float32,
    )


def early_kernel(count, *refs):
    tau_refs, (integral_ref, out_ref, total_ref) = refs[:count], refs[count:]
    sums(
        lambda c: jnp.concatenate([r[c] for r in tau_refs], axis=0),
        integral_ref,
        total_ref,
    )

    @pl.when(pl.program_id(0) == pl.num_programs(0) - 1)
    def _():
        out_ref[...] = total_ref[...].T


def late_kernel(count, *refs):
    (slot_ref, early_ref, added_ref), refs = refs[:3], refs[3:]
    tau_refs, (integral_ref, out_ref, total_ref, all_ref) = refs[:count], refs[count:]
    pairs = tau_refs[0].shape[1]
    sums(
        lambda c: jnp.concatenate([r[c] for r in tau_refs], axis=0),
        integral_ref,
        total_ref,
    )

    @pl.when(pl.program_id(0) == pl.num_programs(0) - 1)
    def _():
        known = early_ref.shape[0]
        all_ref[:known] = early_ref[...]
        all_ref[known:] = added_ref[...] + total_ref[...].T
        owners, bb, rows, a_rows = out_ref.shape
        each = pairs // rows
        for j in range(owners):
            start = pl.multiple_of(slot_ref[j // each] * pairs, pairs) + j % each * rows
            for b in range(bb):
                out_ref[j, b] = all_ref[pl.ds(start, rows), b * a_rows : (b + 1) * a_rows]


def ladder_specs(taus, integral):
    _, pairs, d_len = taus[0][0].shape
    c_rows, bb, a_rows, _ = integral.shape
    c_len = largest_part(c_rows, 8)
    specs = [
        pl.BlockSpec((c_len, pairs, d_len), lambda i, k=start // c_len: (k + i, 0, 0))
        for _, start in taus
    ]
    specs.append(pl.BlockSpec((c_len, bb, a_rows, d_len), lambda i: (i, 0, 0, 0)))
    return specs, (bb * a_rows, len(taus) * pairs), (c_rows // c_len,)


def ladder_early(taus, integral):
    specs, shape, grid = ladder_specs(taus, integral)
    return call(
        functools.partial(early_kernel, len(taus)),
        [t for t, _ in taus] + [integral],
        specs,
        jax.ShapeDtypeStruct(shape[::-1], jnp.float32),
        pl.BlockSpec(shape[::-1], lambda i: (0, 0)),
        [],
        grid=grid,
        scratch=[pltpu.VMEM(shape, jnp.float32)],
        vmem=52,
    )[0]


def ladder_late(slots, early, added, taus, integral, owners):
    specs, shape, grid = ladder_specs(taus, integral)
    pairs = taus[0][0].shape[1]
    _, bb, a_rows, _ = integral.shape
    out = (owners, bb, slots.shape[0] * pairs // owners, a_rows)
    return call(
        functools.partial(late_kernel, len(taus)),
        [slots, early, added] + [t for t, _ in taus] + [integral],
        [pl.BlockSpec(memory_space=pltpu.SMEM)]
        + [pl.BlockSpec(t.shape, lambda i: (0, 0)) for t in (early, added)]
        + specs,
        jax.ShapeDtypeStruct(out, jnp.float32),
        pl.BlockSpec(out, lambda i: (0, 0, 0, 0)),
        [],
        grid=grid,
        scratch=[
            pltpu.VMEM(shape, jnp.float32),
            pltpu.VMEM((early.shape[0] + shape[1], shape[0]), jnp.float32),
        ],
        vmem=52,
    )[0]


def spread(rows, n, z):
    heres = [lax.ppermute(rows, "out", [(0, k)]) for k in range(1, n)]
    for k, here in zip(range(1, n), heres):
        rows = jnp.where(z == k, here, rows)
    return rows


def everywhere(shared, vir, through):
    me = lax.axis_index("vir")

    def swap(array, mask):
        return lax.ppermute(array, "vir", [(k, k ^ mask) for k in range(vir)])

    if vir & (vir - 1) == 0 and 2 < vir <= 8:
        masks = list(range(0, vir, 2))
        slabs = [shared] + [swap(shared, m) for m in masks[1:]]
        packed, through = pack(slabs, through)
        packs = [packed, swap(packed, 1)]
        places = jnp.stack([me ^ m ^ core for core in (0, 1) for m in masks])
    else:
        packs = [lax.all_gather(shared, "vir", axis=1, tiled=True)[None]]
        places = jnp.zeros((1,), jnp.int32)
    return assemble(packs, places.astype(jnp.int32), through)


def body(factors, amplitudes):
    a_rows, c_rows, _ = factors.shape
    n = lax.axis_size("out")
    vir = lax.axis_size("vir")
    z = lax.axis_index("out")

    def send(array, *ways):
        return lax.ppermute(array, "out", ways)

    own = amplitudes.transpose(1, 0, 2)
    token = jnp.zeros((8, LANES), jnp.float32)
    shared = spread(factors[:BB], n, z)
    batch, [token] = everywhere(shared, vir, [token])
    cut = 3 * c_rows // 4 if c_rows % 64 == 0 else c_rows
    spans = [(0, cut), (cut, c_rows)] if cut < c_rows else [(0, c_rows)]
    made = []

    def make():
        nonlocal token
        part, [token] = integrals(factors, batch, *spans[len(made)], [token])
        made.append(part)

    make()
    if n == 4:
        inside = (z == 1) | (z == 2)
        second = send(own, (2, 0), (1, 3))
        first = send(own, (3, 1), (1, 0), (0, 2), (2, 3))
        onward, [token] = pick(inside, first, own, 0, c_rows, [token])
        sides = send(onward, (1, 0), (0, 1), (2, 3), (3, 2))
        token, second, *kept = fence([token, second] + [own[i:j] for i, j in spans], MORE)
        [sides] = fence([sides], MUCH)
        early = [own, first, second]
        late = [[(sides, i), (send(t, (2, 1), (1, 2)), 0)] for (i, _), t in zip(spans, kept)]
        slots = jnp.array([[0, 1, 2, 3], [3, 0, 4, 1], [1, 4, 0, 3], [3, 2, 1, 0]], jnp.int32)[z]
    else:
        gathered = lax.all_gather(own, "out")
        early, late = [own], [[(gathered[k], i) for k in range(n)] for i, _ in spans]
        slots = jnp.arange(1, n + 1, dtype=jnp.int32)
    while len(made) < len(spans):
        make()

    known, added = None, None
    for part, (start, _) in zip(made, spans):
        terms = ladder_early([(t, start) for t in early], part)
        known = terms if known is None else known + terms
    for part, taus in zip(made[:-1], late):
        added = ladder_early(taus, part)
    if added is None:
        rows = sum(t.shape[1] for t, _ in late[-1])
        added = jnp.zeros((rows, BB * a_rows), jnp.float32)
    parts = ladder_late(slots, known, added, late[-1], made[-1], vir)
    swapped = lax.all_to_all(parts, "vir", split_axis=0, concat_axis=0)
    return jnp.sum(swapped, axis=0)


def solution(mesh):
    placed = (P("out", "vir", None), P("out", "vir", None))
    return jax.shard_map(
        body, mesh=mesh, in_specs=placed, out_specs=P(None, "vir", "out"), check_vma=False
    )
```

```python
import functools

import jax
import jax.numpy as jnp
from jax import lax
from jax.experimental import pallas as pl
from jax.experimental.pallas import tpu as pltpu
from jax.sharding import PartitionSpec as P

BB = 2
LANES = 128
NT = (((1,), (1,)), ((), ()))
NN = (((1,), (0,)), ((), ()))
LITTLE = pl.CostEstimate(flops=1024, bytes_accessed=1024, transcendentals=0)
MUCH = pl.CostEstimate(flops=2 * 10**10, bytes_accessed=4 * 10**7, transcendentals=0)


def largest_part(extent, limit):
    part = min(extent, limit)
    while extent % part:
        part -= 1
    return part


def call(kernel, inputs, in_specs, out_shape, out_spec, through, grid=(1,), scratch=(), vmem=52):
    n_in, n_thru = len(inputs), len(through)

    def run(*refs):
        outs = refs[n_in + n_thru :]
        kernel(*refs[:n_in], outs[0], *outs[1 + n_thru :])

    anywhere = pl.BlockSpec(memory_space=pl.ANY)
    out = pl.pallas_call(
        run,
        grid=grid,
        in_specs=list(in_specs) + [anywhere] * n_thru,
        out_specs=[out_spec] + [anywhere] * n_thru,
        out_shape=[out_shape] + [jax.ShapeDtypeStruct(t.shape, t.dtype) for t in through],
        input_output_aliases={n_in + k: 1 + k for k in range(n_thru)},
        scratch_shapes=list(scratch),
        compiler_params=pltpu.CompilerParams(vmem_limit_bytes=vmem * 2**20),
        cost_estimate=LITTLE,
    )(*inputs, *through)
    return out[0], list(out[1:])


def fence(arrays, cost=LITTLE):
    anywhere = [pl.BlockSpec(memory_space=pl.ANY)] * len(arrays)
    return pl.pallas_call(
        lambda *refs: None,
        in_specs=anywhere,
        out_specs=anywhere,
        out_shape=[jax.ShapeDtypeStruct(t.shape, t.dtype) for t in arrays],
        input_output_aliases={k: k for k in range(len(arrays))},
        cost_estimate=cost,
    )(*arrays)


def pick_kernel(flag_ref, first_ref, other_ref, out_ref):
    @pl.when(flag_ref[0] == 1)
    def _():
        out_ref[...] = first_ref[...]

    @pl.when(flag_ref[0] == 0)
    def _():
        out_ref[...] = other_ref[...]


def pick(flag, first, other, start, stop, through):
    c_len = largest_part(stop - start, 16)
    begin = start // c_len
    block = (c_len,) + first.shape[1:]
    spec = pl.BlockSpec(block, lambda i: (begin + i, 0, 0))
    return call(
        pick_kernel,
        [flag.astype(jnp.int32).reshape(1), first, other],
        [pl.BlockSpec(memory_space=pltpu.SMEM), spec, spec],
        jax.ShapeDtypeStruct((stop - start,) + first.shape[1:], first.dtype),
        pl.BlockSpec(block, lambda i: (i, 0, 0)),
        through,
        grid=((stop - start) // c_len,),
    )


def pack_kernel(*refs):
    for k, slab in enumerate(refs[:-1]):
        refs[-1][k] = slab[...]


def pack(slabs, through):
    vmem = pl.BlockSpec(memory_space=pltpu.VMEM)
    shape = jax.ShapeDtypeStruct((len(slabs),) + slabs[0].shape, slabs[0].dtype)
    return call(pack_kernel, slabs, [vmem] * len(slabs), shape, vmem, through)


def assemble_kernel(*refs):
    place_ref, packs, out_ref, whole_ref = refs[0], refs[1:-2], refs[-2], refs[-1]
    piece = packs[0].shape[2]
    for i, packed in enumerate(packs):
        for k in range(packed.shape[0]):
            start = pl.multiple_of(place_ref[i * packed.shape[0] + k] * piece, piece)
            whole_ref[:, pl.ds(start, piece), :] = packed[k]
    for b in range(out_ref.shape[0]):
        out_ref[b] = whole_ref[b].T


def assemble(packs, places, through):
    count, bb, piece, aux_len = packs[0].shape
    d_len = piece * count * len(packs)
    vmem = pl.BlockSpec(memory_space=pltpu.VMEM)
    return call(
        assemble_kernel,
        [places] + packs,
        [pl.BlockSpec(memory_space=pltpu.SMEM)] + [vmem] * len(packs),
        jax.ShapeDtypeStruct((bb, aux_len, d_len), jnp.bfloat16),
        vmem,
        through,
        scratch=[pltpu.VMEM((bb, d_len, aux_len), jnp.bfloat16)],
    )


def integral_kernel(factor_ref, batch_ref, out_ref):
    a_len, c_len, aux_len = factor_ref.shape
    d_len = out_ref.shape[3]
    rows = factor_ref[...].reshape(a_len * c_len, aux_len)
    wide = largest_part(d_len // LANES, 2) * LANES
    for b in range(out_ref.shape[1]):
        for j in range(0, d_len, wide):
            tile = lax.dot_general(
                rows, batch_ref[b, :, j : j + wide], NN, preferred_element_type=jnp.float32
            )
            turned = jnp.swapaxes(tile.reshape(a_len, c_len, wide), 0, 1)
            out_ref[:, b, :, j : j + wide] = turned.astype(jnp.bfloat16)


def integrals(factors, batch, start, stop, through):
    a_rows, c_rows, aux_len = factors.shape
    bb, _, d_len = batch.shape
    c_len = largest_part(c_rows, 8)
    first = start // c_len
    return call(
        integral_kernel,
        [factors, batch],
        [
            pl.BlockSpec((a_rows, c_len, aux_len), lambda i: (0, first + i, 0)),
            pl.BlockSpec((bb, aux_len, d_len), lambda i: (0, 0, 0)),
        ],
        jax.ShapeDtypeStruct((stop - start, bb, a_rows, d_len), jnp.bfloat16),
        pl.BlockSpec((c_len, bb, a_rows, d_len), lambda i: (i, 0, 0, 0)),
        through,
        grid=((stop - start) // c_len,),
    )


def sums(tau_of, integral_ref, total_ref):
    c_len, bb, a_rows, d_len = integral_ref.shape

    @pl.when(pl.program_id(0) == 0)
    def _():
        total_ref[...] = jnp.zeros_like(total_ref)

    left = [integral_ref[c].reshape(bb * a_rows, d_len) for c in range(c_len)]
    right = [tau_of(c) for c in range(c_len)]
    total_ref[...] += lax.dot_general(
        jnp.concatenate(left, axis=1),
        jnp.concatenate(right, axis=1),
        NT,
        preferred_element_type=jnp.float32,
    )


def early_kernel(count, *refs):
    tau_refs, (integral_ref, out_ref, total_ref) = refs[:count], refs[count:]
    sums(
        lambda c: jnp.concatenate([r[c] for r in tau_refs], axis=0),
        integral_ref,
        total_ref,
    )

    @pl.when(pl.program_id(0) == pl.num_programs(0) - 1)
    def _():
        out_ref[...] = total_ref[...].T


def late_kernel(count, *refs):
    (slot_ref, early_ref, added_ref), refs = refs[:3], refs[3:]
    tau_refs, (integral_ref, out_ref, total_ref, all_ref) = refs[:count], refs[count:]
    pairs = tau_refs[0].shape[1]
    sums(
        lambda c: jnp.concatenate([r[c] for r in tau_refs], axis=0),
        integral_ref,
        total_ref,
    )

    @pl.when(pl.program_id(0) == pl.num_programs(0) - 1)
    def _():
        known = early_ref.shape[0]
        all_ref[:known] = early_ref[...]
        all_ref[known:] = added_ref[...] + total_ref[...].T
        owners, bb, rows, a_rows = out_ref.shape
        each = pairs // rows
        for j in range(owners):
            start = pl.multiple_of(slot_ref[j // each] * pairs, pairs) + j % each * rows
            for b in range(bb):
                out_ref[j, b] = all_ref[pl.ds(start, rows), b * a_rows : (b + 1) * a_rows]


def ladder_specs(taus, integral):
    _, pairs, d_len = taus[0][0].shape
    c_rows, bb, a_rows, _ = integral.shape
    c_len = largest_part(c_rows, 8)
    specs = [
        pl.BlockSpec((c_len, pairs, d_len), lambda i, k=start // c_len: (k + i, 0, 0))
        for _, start in taus
    ]
    specs.append(pl.BlockSpec((c_len, bb, a_rows, d_len), lambda i: (i, 0, 0, 0)))
    return specs, (bb * a_rows, len(taus) * pairs), (c_rows // c_len,)


def ladder_early(taus, integral):
    specs, shape, grid = ladder_specs(taus, integral)
    return call(
        functools.partial(early_kernel, len(taus)),
        [t for t, _ in taus] + [integral],
        specs,
        jax.ShapeDtypeStruct(shape[::-1], jnp.float32),
        pl.BlockSpec(shape[::-1], lambda i: (0, 0)),
        [],
        grid=grid,
        scratch=[pltpu.VMEM(shape, jnp.float32)],
        vmem=52,
    )[0]


def ladder_late(slots, early, added, taus, integral, owners):
    specs, shape, grid = ladder_specs(taus, integral)
    pairs = taus[0][0].shape[1]
    _, bb, a_rows, _ = integral.shape
    out = (owners, bb, slots.shape[0] * pairs // owners, a_rows)
    return call(
        functools.partial(late_kernel, len(taus)),
        [slots, early, added] + [t for t, _ in taus] + [integral],
        [pl.BlockSpec(memory_space=pltpu.SMEM)]
        + [pl.BlockSpec(t.shape, lambda i: (0, 0)) for t in (early, added)]
        + specs,
        jax.ShapeDtypeStruct(out, jnp.float32),
        pl.BlockSpec(out, lambda i: (0, 0, 0, 0)),
        [],
        grid=grid,
        scratch=[
            pltpu.VMEM(shape, jnp.float32),
            pltpu.VMEM((early.shape[0] + shape[1], shape[0]), jnp.float32),
        ],
        vmem=52,
    )[0]


def spread(rows, n, z):
    heres = [lax.ppermute(rows, "out", [(0, k)]) for k in range(1, n)]
    for k, here in zip(range(1, n), heres):
        rows = jnp.where(z == k, here, rows)
    return rows


def everywhere(shared, vir, through):
    me = lax.axis_index("vir")

    def swap(array, mask):
        return lax.ppermute(array, "vir", [(k, k ^ mask) for k in range(vir)])

    if vir & (vir - 1) == 0 and 2 < vir <= 8:
        masks = list(range(0, vir, 2))
        slabs = [shared] + [swap(shared, m) for m in masks[1:]]
        packed, through = pack(slabs, through)
        packs = [packed, swap(packed, 1)]
        places = jnp.stack([me ^ m ^ core for core in (0, 1) for m in masks])
    else:
        packs = [lax.all_gather(shared, "vir", axis=1, tiled=True)[None]]
        places = jnp.zeros((1,), jnp.int32)
    return assemble(packs, places.astype(jnp.int32), through)


def body(factors, amplitudes):
    a_rows, c_rows, _ = factors.shape
    n = lax.axis_size("out")
    vir = lax.axis_size("vir")
    z = lax.axis_index("out")

    def send(array, *ways):
        return lax.ppermute(array, "out", ways)

    own = amplitudes.transpose(1, 0, 2)
    token = jnp.zeros((8, LANES), jnp.float32)
    shared = spread(factors[:BB], n, z)
    batch, [token] = everywhere(shared, vir, [token])
    cut = 3 * c_rows // 4 if c_rows % 64 == 0 else c_rows
    spans = [(0, cut), (cut, c_rows)] if cut < c_rows else [(0, c_rows)]
    made = []

    def make():
        nonlocal token
        part, [token] = integrals(factors, batch, *spans[len(made)], [token])
        made.append(part)

    make()
    if n == 4:
        inside = (z == 1) | (z == 2)
        second = send(own, (2, 0), (1, 3))
        first = send(own, (3, 1), (1, 0), (0, 2), (2, 3))
        onward = []
        for span in spans:
            part, [token] = pick(inside, first, own, *span, [token])
            onward.append(part)
        sides = [send(t, (1, 0), (0, 1), (2, 3), (3, 2)) for t in onward]
        token, second, *kept = fence([token, second] + [own[i:j] for i, j in spans], MUCH)
        middle = [send(t, (2, 1), (1, 2)) for t in kept]
        [sides[0]] = fence(sides[:1], MUCH)
        late = [[(t, 0) for t in pair] for pair in zip(sides, middle)]
        early = [own, first, second]
        slots = jnp.array([[0, 1, 2, 3], [3, 0, 4, 1], [1, 4, 0, 3], [3, 2, 1, 0]], jnp.int32)[z]
    else:
        gathered = lax.all_gather(own, "out")
        early, late = [own], [[(gathered[k], i) for k in range(n)] for i, _ in spans]
        slots = jnp.arange(1, n + 1, dtype=jnp.int32)
    while len(made) < len(spans):
        make()

    known, added = None, None
    for part, (start, _) in zip(made, spans):
        terms = ladder_early([(t, start) for t in early], part)
        known = terms if known is None else known + terms
    for part, taus in zip(made[:-1], late):
        added = ladder_early(taus, part)
    if added is None:
        rows = sum(t.shape[1] for t, _ in late[-1])
        added = jnp.zeros((rows, BB * a_rows), jnp.float32)
    parts = ladder_late(slots, known, added, late[-1], made[-1], vir)
    swapped = lax.all_to_all(parts, "vir", split_axis=0, concat_axis=0)
    return jnp.sum(swapped, axis=0)


def solution(mesh):
    placed = (P("out", "vir", None), P("out", "vir", None))
    return jax.shard_map(
        body, mesh=mesh, in_specs=placed, out_specs=P(None, "vir", "out"), check_vma=False
    )
```

```python
import functools

import jax
import jax.numpy as jnp
from jax import lax
from jax.experimental import pallas as pl
from jax.experimental.pallas import tpu as pltpu
from jax.sharding import PartitionSpec as P

BB = 2
LANES = 128
NT = (((1,), (1,)), ((), ()))
NN = (((1,), (0,)), ((), ()))
LITTLE = pl.CostEstimate(flops=1024, bytes_accessed=1024, transcendentals=0)
MUCH = pl.CostEstimate(flops=2 * 10**10, bytes_accessed=4 * 10**7, transcendentals=0)


def largest_part(extent, limit):
    part = min(extent, limit)
    while extent % part:
        part -= 1
    return part


def call(kernel, inputs, in_specs, out_shape, out_spec, through, grid=(1,), scratch=(), vmem=52):
    n_in, n_thru = len(inputs), len(through)

    def run(*refs):
        outs = refs[n_in + n_thru :]
        kernel(*refs[:n_in], outs[0], *outs[1 + n_thru :])

    anywhere = pl.BlockSpec(memory_space=pl.ANY)
    out = pl.pallas_call(
        run,
        grid=grid,
        in_specs=list(in_specs) + [anywhere] * n_thru,
        out_specs=[out_spec] + [anywhere] * n_thru,
        out_shape=[out_shape] + [jax.ShapeDtypeStruct(t.shape, t.dtype) for t in through],
        input_output_aliases={n_in + k: 1 + k for k in range(n_thru)},
        scratch_shapes=list(scratch),
        compiler_params=pltpu.CompilerParams(vmem_limit_bytes=vmem * 2**20),
        cost_estimate=LITTLE,
    )(*inputs, *through)
    return out[0], list(out[1:])


def fence(arrays, cost=LITTLE):
    anywhere = [pl.BlockSpec(memory_space=pl.ANY)] * len(arrays)
    return pl.pallas_call(
        lambda *refs: None,
        in_specs=anywhere,
        out_specs=anywhere,
        out_shape=[jax.ShapeDtypeStruct(t.shape, t.dtype) for t in arrays],
        input_output_aliases={k: k for k in range(len(arrays))},
        cost_estimate=cost,
    )(*arrays)


def pick_kernel(flag_ref, first_ref, other_ref, out_ref):
    @pl.when(flag_ref[0] == 1)
    def _():
        out_ref[...] = first_ref[...]

    @pl.when(flag_ref[0] == 0)
    def _():
        out_ref[...] = other_ref[...]


def pick(flag, first, other, start, stop, through):
    c_len = largest_part(stop - start, 16)
    begin = start // c_len
    block = (c_len,) + first.shape[1:]
    spec = pl.BlockSpec(block, lambda i: (begin + i, 0, 0))
    return call(
        pick_kernel,
        [flag.astype(jnp.int32).reshape(1), first, other],
        [pl.BlockSpec(memory_space=pltpu.SMEM), spec, spec],
        jax.ShapeDtypeStruct((stop - start,) + first.shape[1:], first.dtype),
        pl.BlockSpec(block, lambda i: (i, 0, 0)),
        through,
        grid=((stop - start) // c_len,),
    )


def pack_kernel(*refs):
    for k, slab in enumerate(refs[:-1]):
        refs[-1][k] = slab[...]


def pack(slabs, through):
    vmem = pl.BlockSpec(memory_space=pltpu.VMEM)
    shape = jax.ShapeDtypeStruct((len(slabs),) + slabs[0].shape, slabs[0].dtype)
    return call(pack_kernel, slabs, [vmem] * len(slabs), shape, vmem, through)


def assemble_kernel(*refs):
    place_ref, packs, out_ref, whole_ref = refs[0], refs[1:-2], refs[-2], refs[-1]
    piece = packs[0].shape[2]
    for i, packed in enumerate(packs):
        for k in range(packed.shape[0]):
            start = pl.multiple_of(place_ref[i * packed.shape[0] + k] * piece, piece)
            whole_ref[:, pl.ds(start, piece), :] = packed[k]
    for b in range(out_ref.shape[0]):
        out_ref[b] = whole_ref[b].T


def assemble(packs, places, through):
    count, bb, piece, aux_len = packs[0].shape
    d_len = piece * count * len(packs)
    vmem = pl.BlockSpec(memory_space=pltpu.VMEM)
    return call(
        assemble_kernel,
        [places] + packs,
        [pl.BlockSpec(memory_space=pltpu.SMEM)] + [vmem] * len(packs),
        jax.ShapeDtypeStruct((bb, aux_len, d_len), jnp.bfloat16),
        vmem,
        through,
        scratch=[pltpu.VMEM((bb, d_len, aux_len), jnp.bfloat16)],
    )


def integral_kernel(factor_ref, batch_ref, out_ref):
    a_len, c_len, aux_len = factor_ref.shape
    d_len = out_ref.shape[3]
    rows = factor_ref[...].reshape(a_len * c_len, aux_len)
    wide = largest_part(d_len // LANES, 2) * LANES
    for b in range(out_ref.shape[1]):
        for j in range(0, d_len, wide):
            tile = lax.dot_general(
                rows, batch_ref[b, :, j : j + wide], NN, preferred_element_type=jnp.float32
            )
            turned = jnp.swapaxes(tile.reshape(a_len, c_len, wide), 0, 1)
            out_ref[:, b, :, j : j + wide] = turned.astype(jnp.bfloat16)


def integrals(factors, batch, start, stop, through):
    a_rows, c_rows, aux_len = factors.shape
    bb, _, d_len = batch.shape
    c_len = largest_part(c_rows, 8)
    first = start // c_len
    return call(
        integral_kernel,
        [factors, batch],
        [
            pl.BlockSpec((a_rows, c_len, aux_len), lambda i: (0, first + i, 0)),
            pl.BlockSpec((bb, aux_len, d_len), lambda i: (0, 0, 0)),
        ],
        jax.ShapeDtypeStruct((stop - start, bb, a_rows, d_len), jnp.bfloat16),
        pl.BlockSpec((c_len, bb, a_rows, d_len), lambda i: (i, 0, 0, 0)),
        through,
        grid=((stop - start) // c_len,),
    )


def sums(tau_of, integral_refs, total_ref):
    c_len = integral_refs[0].shape[0]

    @pl.when(pl.program_id(0) == 0)
    def _():
        total_ref[...] = jnp.zeros_like(total_ref)

    left = [jnp.concatenate([r[c, 0] for r in integral_refs], axis=0) for c in range(c_len)]
    right = [tau_of(c) for c in range(c_len)]
    total_ref[...] += lax.dot_general(
        jnp.concatenate(left, axis=1),
        jnp.concatenate(right, axis=1),
        NT,
        preferred_element_type=jnp.float32,
    )


def early_kernel(count, *refs):
    tau_refs, integral_refs, (out_ref, total_ref) = refs[:count], refs[count:-2], refs[-2:]
    sums(
        lambda c: jnp.concatenate([r[c] for r in tau_refs], axis=0),
        integral_refs,
        total_ref,
    )

    @pl.when(pl.program_id(0) == pl.num_programs(0) - 1)
    def _():
        out_ref[...] = total_ref[...].T


def late_kernel(count, *refs):
    (slot_ref, early_ref, added_ref), refs = refs[:3], refs[3:]
    tau_refs, integral_refs = refs[:count], refs[count:-3]
    out_ref, total_ref, all_ref = refs[-3:]
    pairs = tau_refs[0].shape[1]
    sums(
        lambda c: jnp.concatenate([r[c] for r in tau_refs], axis=0),
        integral_refs,
        total_ref,
    )

    @pl.when(pl.program_id(0) == pl.num_programs(0) - 1)
    def _():
        known = early_ref.shape[0]
        all_ref[:known] = early_ref[...]
        all_ref[known:] = added_ref[...] + total_ref[...].T
        owners, bb, rows, a_rows = out_ref.shape
        each = pairs // rows
        for j in range(owners):
            start = pl.multiple_of(slot_ref[j // each] * pairs, pairs) + j % each * rows
            for b in range(bb):
                out_ref[j, b] = all_ref[pl.ds(start, rows), b * a_rows : (b + 1) * a_rows]


def ladder_specs(taus, integral):
    _, pairs, d_len = taus[0][0].shape
    c_rows, bb, a_rows, _ = integral.shape
    c_len = largest_part(c_rows, 8)
    specs = [
        pl.BlockSpec((c_len, pairs, d_len), lambda i, k=start // c_len: (k + i, 0, 0))
        for _, start in taus
    ]
    for b in range(bb):
        specs.append(pl.BlockSpec((c_len, 1, a_rows, d_len), lambda i, b=b: (i, b, 0, 0)))
    return specs, (bb * a_rows, len(taus) * pairs), (c_rows // c_len,)


def ladder_early(taus, integral):
    specs, shape, grid = ladder_specs(taus, integral)
    return call(
        functools.partial(early_kernel, len(taus)),
        [t for t, _ in taus] + [integral] * integral.shape[1],
        specs,
        jax.ShapeDtypeStruct(shape[::-1], jnp.float32),
        pl.BlockSpec(shape[::-1], lambda i: (0, 0)),
        [],
        grid=grid,
        scratch=[pltpu.VMEM(shape, jnp.float32)],
        vmem=60,
    )[0]


def ladder_late(slots, early, added, taus, integral, owners):
    specs, shape, grid = ladder_specs(taus, integral)
    pairs = taus[0][0].shape[1]
    _, bb, a_rows, _ = integral.shape
    out = (owners, bb, slots.shape[0] * pairs // owners, a_rows)
    return call(
        functools.partial(late_kernel, len(taus)),
        [slots, early, added] + [t for t, _ in taus] + [integral] * integral.shape[1],
        [pl.BlockSpec(memory_space=pltpu.SMEM)]
        + [pl.BlockSpec(t.shape, lambda i: (0, 0)) for t in (early, added)]
        + specs,
        jax.ShapeDtypeStruct(out, jnp.float32),
        pl.BlockSpec(out, lambda i: (0, 0, 0, 0)),
        [],
        grid=grid,
        scratch=[
            pltpu.VMEM(shape, jnp.float32),
            pltpu.VMEM((early.shape[0] + shape[1], shape[0]), jnp.float32),
        ],
        vmem=60,
    )[0]


def spread(rows, n, z):
    heres = [lax.ppermute(rows, "out", [(0, k)]) for k in range(n - 1, 0, -1)]
    for k, here in zip(range(n - 1, 0, -1), heres):
        rows = jnp.where(z == k, here, rows)
    return rows


def everywhere(shared, vir, through):
    me = lax.axis_index("vir")

    def swap(array, mask):
        return lax.ppermute(array, "vir", [(k, k ^ mask) for k in range(vir)])

    if vir & (vir - 1) == 0 and 2 < vir <= 8:
        masks = list(range(0, vir, 2))
        slabs = [shared] + [swap(shared, m) for m in masks[1:]]
        packed, through = pack(slabs, through)
        packs = [packed, swap(packed, 1)]
        places = jnp.stack([me ^ m ^ core for core in (0, 1) for m in masks])
    else:
        packs = [lax.all_gather(shared, "vir", axis=1, tiled=True)[None]]
        places = jnp.zeros((1,), jnp.int32)
    return assemble(packs, places.astype(jnp.int32), through)


def body(factors, amplitudes):
    a_rows, c_rows, _ = factors.shape
    n = lax.axis_size("out")
    vir = lax.axis_size("vir")
    z = lax.axis_index("out")

    def send(array, *ways):
        return lax.ppermute(array, "out", ways)

    own = amplitudes.transpose(1, 0, 2)
    token = jnp.zeros((8, LANES), jnp.float32)
    shared = spread(factors[:BB], n, z)
    batch, [token] = everywhere(shared, vir, [token])
    cut = 3 * c_rows // 4 if c_rows % 64 == 0 else c_rows
    spans = [(0, cut), (cut, c_rows)] if cut < c_rows else [(0, c_rows)]
    made = []

    def make():
        nonlocal token
        part, [token] = integrals(factors, batch, *spans[len(made)], [token])
        made.append(part)

    make()
    if n == 4:
        inside = (z == 1) | (z == 2)
        second = send(amplitudes, (2, 0), (1, 3))
        first = send(amplitudes, (3, 1), (1, 0), (0, 2), (2, 3)).transpose(1, 0, 2)
        onward = []
        for span in spans:
            part, [token] = pick(inside, first, own, *span, [token])
            onward.append(part)
        sides = [send(t, (1, 0), (0, 1), (2, 3), (3, 2)) for t in onward]
        token, second, *kept = fence([token, second] + [own[i:j] for i, j in spans], MUCH)
        middle = [send(t, (2, 1), (1, 2)) for t in kept]
        [sides[0]] = fence(sides[:1], MUCH)
        late = [[(t, 0) for t in pair] for pair in zip(sides, middle)]
        early = [own, first, second.transpose(1, 0, 2)]
        slots = jnp.array([[0, 1, 2, 3], [3, 0, 4, 1], [1, 4, 0, 3], [3, 2, 1, 0]], jnp.int32)[z]
    else:
        gathered = lax.all_gather(own, "out")
        early, late = [own], [[(gathered[k], i) for k in range(n)] for i, _ in spans]
        slots = jnp.arange(1, n + 1, dtype=jnp.int32)
    while len(made) < len(spans):
        make()

    known, added = None, None
    for part, (start, _) in zip(made, spans):
        terms = ladder_early([(t, start) for t in early], part)
        known = terms if known is None else known + terms
    for part, taus in zip(made[:-1], late):
        added = ladder_early(taus, part)
    if added is None:
        rows = sum(t.shape[1] for t, _ in late[-1])
        added = jnp.zeros((rows, BB * a_rows), jnp.float32)
    parts = ladder_late(slots, known, added, late[-1], made[-1], vir)
    swapped = lax.all_to_all(parts, "vir", split_axis=0, concat_axis=0)
    return jnp.sum(swapped, axis=0)


def solution(mesh):
    placed = (P("out", "vir", None), P("out", "vir", None))
    return jax.shard_map(
        body, mesh=mesh, in_specs=placed, out_specs=P(None, "vir", "out"), check_vma=False
    )
```

```python
import functools

import jax
import jax.numpy as jnp
from jax import lax
from jax.experimental import pallas as pl
from jax.experimental.pallas import tpu as pltpu
from jax.sharding import PartitionSpec as P

BB = 2
LANES = 128
NT = (((1,), (1,)), ((), ()))
NN = (((1,), (0,)), ((), ()))
LITTLE = pl.CostEstimate(flops=1024, bytes_accessed=1024, transcendentals=0)
MUCH = pl.CostEstimate(flops=2 * 10**10, bytes_accessed=4 * 10**7, transcendentals=0)


def largest_part(extent, limit):
    part = min(extent, limit)
    while extent % part:
        part -= 1
    return part


def call(kernel, inputs, in_specs, out_shape, out_spec, through, grid=(1,), scratch=(), vmem=52):
    n_in, n_thru = len(inputs), len(through)

    def run(*refs):
        outs = refs[n_in + n_thru :]
        kernel(*refs[:n_in], outs[0], *outs[1 + n_thru :])

    anywhere = pl.BlockSpec(memory_space=pl.ANY)
    out = pl.pallas_call(
        run,
        grid=grid,
        in_specs=list(in_specs) + [anywhere] * n_thru,
        out_specs=[out_spec] + [anywhere] * n_thru,
        out_shape=[out_shape] + [jax.ShapeDtypeStruct(t.shape, t.dtype) for t in through],
        input_output_aliases={n_in + k: 1 + k for k in range(n_thru)},
        scratch_shapes=list(scratch),
        compiler_params=pltpu.CompilerParams(vmem_limit_bytes=vmem * 2**20),
        cost_estimate=LITTLE,
    )(*inputs, *through)
    return out[0], list(out[1:])


def fence(arrays, cost=LITTLE):
    anywhere = [pl.BlockSpec(memory_space=pl.ANY)] * len(arrays)
    return pl.pallas_call(
        lambda *refs: None,
        in_specs=anywhere,
        out_specs=anywhere,
        out_shape=[jax.ShapeDtypeStruct(t.shape, t.dtype) for t in arrays],
        input_output_aliases={k: k for k in range(len(arrays))},
        cost_estimate=cost,
    )(*arrays)


def pick_kernel(flag_ref, first_ref, other_ref, out_ref):
    @pl.when(flag_ref[0] == 1)
    def _():
        out_ref[...] = first_ref[...]

    @pl.when(flag_ref[0] == 0)
    def _():
        out_ref[...] = other_ref[...]


def pick(flag, first, other, start, stop, through):
    c_len = largest_part(stop - start, 16)
    begin = start // c_len
    block = (c_len,) + first.shape[1:]
    spec = pl.BlockSpec(block, lambda i: (begin + i, 0, 0))
    return call(
        pick_kernel,
        [flag.astype(jnp.int32).reshape(1), first, other],
        [pl.BlockSpec(memory_space=pltpu.SMEM), spec, spec],
        jax.ShapeDtypeStruct((stop - start,) + first.shape[1:], first.dtype),
        pl.BlockSpec(block, lambda i: (i, 0, 0)),
        through,
        grid=((stop - start) // c_len,),
    )


def pack_kernel(*refs):
    for k, slab in enumerate(refs[:-1]):
        refs[-1][k] = slab[...]


def pack(slabs, through):
    vmem = pl.BlockSpec(memory_space=pltpu.VMEM)
    shape = jax.ShapeDtypeStruct((len(slabs),) + slabs[0].shape, slabs[0].dtype)
    return call(pack_kernel, slabs, [vmem] * len(slabs), shape, vmem, through)


def turn_kernel(in_ref, out_ref):
    whole = in_ref[...].astype(jnp.float32)
    out_ref[...] = jnp.swapaxes(whole, 0, 1).astype(out_ref.dtype)


def turn(array, through):
    pairs, c_rows, d_len = array.shape
    c_len = largest_part(c_rows, 16)
    return call(
        turn_kernel,
        [array],
        [pl.BlockSpec((pairs, c_len, d_len), lambda i: (0, i, 0))],
        jax.ShapeDtypeStruct((c_rows, pairs, d_len), array.dtype),
        pl.BlockSpec((c_len, pairs, d_len), lambda i: (i, 0, 0)),
        through,
        grid=(c_rows // c_len,),
    )


def assemble_kernel(*refs):
    place_ref, packs, out_ref, whole_ref = refs[0], refs[1:-2], refs[-2], refs[-1]
    piece = packs[0].shape[2]
    for i, packed in enumerate(packs):
        for k in range(packed.shape[0]):
            start = pl.multiple_of(place_ref[i * packed.shape[0] + k] * piece, piece)
            whole_ref[:, pl.ds(start, piece), :] = packed[k]
    for b in range(out_ref.shape[0]):
        out_ref[b] = whole_ref[b].T


def assemble(packs, places, through):
    count, bb, piece, aux_len = packs[0].shape
    d_len = piece * count * len(packs)
    vmem = pl.BlockSpec(memory_space=pltpu.VMEM)
    return call(
        assemble_kernel,
        [places] + packs,
        [pl.BlockSpec(memory_space=pltpu.SMEM)] + [vmem] * len(packs),
        jax.ShapeDtypeStruct((bb, aux_len, d_len), jnp.bfloat16),
        vmem,
        through,
        scratch=[pltpu.VMEM((bb, d_len, aux_len), jnp.bfloat16)],
    )


def integral_kernel(factor_ref, batch_ref, out_ref):
    a_len, c_len, aux_len = factor_ref.shape
    d_len = out_ref.shape[3]
    rows = factor_ref[...].reshape(a_len * c_len, aux_len)
    wide = largest_part(d_len // LANES, 2) * LANES
    for b in range(out_ref.shape[1]):
        for j in range(0, d_len, wide):
            tile = lax.dot_general(
                rows, batch_ref[b, :, j : j + wide], NN, preferred_element_type=jnp.float32
            )
            turned = jnp.swapaxes(tile.reshape(a_len, c_len, wide), 0, 1)
            out_ref[:, b, :, j : j + wide] = turned.astype(jnp.bfloat16)


def integrals(factors, batch, start, stop, through):
    a_rows, c_rows, aux_len = factors.shape
    bb, _, d_len = batch.shape
    c_len = largest_part(c_rows, 8)
    first = start // c_len
    return call(
        integral_kernel,
        [factors, batch],
        [
            pl.BlockSpec((a_rows, c_len, aux_len), lambda i: (0, first + i, 0)),
            pl.BlockSpec((bb, aux_len, d_len), lambda i: (0, 0, 0)),
        ],
        jax.ShapeDtypeStruct((stop - start, bb, a_rows, d_len), jnp.bfloat16),
        pl.BlockSpec((c_len, bb, a_rows, d_len), lambda i: (i, 0, 0, 0)),
        through,
        grid=((stop - start) // c_len,),
    )


def sums(tau_of, integral_ref, total_ref):
    c_len, bb, a_rows, d_len = integral_ref.shape

    @pl.when(pl.program_id(0) == 0)
    def _():
        total_ref[...] = jnp.zeros_like(total_ref)

    left = [integral_ref[c].reshape(bb * a_rows, d_len) for c in range(c_len)]
    right = [tau_of(c) for c in range(c_len)]
    total_ref[...] += lax.dot_general(
        jnp.concatenate(left, axis=1),
        jnp.concatenate(right, axis=1),
        NT,
        preferred_element_type=jnp.float32,
    )


def early_kernel(count, *refs):
    tau_refs, (integral_ref, out_ref, total_ref) = refs[:count], refs[count:]
    sums(
        lambda c: jnp.concatenate([r[c] for r in tau_refs], axis=0),
        integral_ref,
        total_ref,
    )

    @pl.when(pl.program_id(0) == pl.num_programs(0) - 1)
    def _():
        out_ref[...] = total_ref[...].T


def late_kernel(count, *refs):
    (slot_ref, early_ref, added_ref), refs = refs[:3], refs[3:]
    tau_refs, (integral_ref, out_ref, total_ref, all_ref) = refs[:count], refs[count:]
    pairs = tau_refs[0].shape[1]
    sums(
        lambda c: jnp.concatenate([r[c] for r in tau_refs], axis=0),
        integral_ref,
        total_ref,
    )

    @pl.when(pl.program_id(0) == pl.num_programs(0) - 1)
    def _():
        known = early_ref.shape[0]
        all_ref[:known] = early_ref[...]
        all_ref[known:] = added_ref[...] + total_ref[...].T
        owners, bb, rows, a_rows = out_ref.shape
        each = pairs // rows
        for j in range(owners):
            start = pl.multiple_of(slot_ref[j // each] * pairs, pairs) + j % each * rows
            for b in range(bb):
                out_ref[j, b] = all_ref[pl.ds(start, rows), b * a_rows : (b + 1) * a_rows]


def ladder_specs(taus, integral):
    _, pairs, d_len = taus[0][0].shape
    c_rows, bb, a_rows, _ = integral.shape
    c_len = largest_part(c_rows, 8)
    specs = [
        pl.BlockSpec((c_len, pairs, d_len), lambda i, k=start // c_len: (k + i, 0, 0))
        for _, start in taus
    ]
    specs.append(pl.BlockSpec((c_len, bb, a_rows, d_len), lambda i: (i, 0, 0, 0)))
    return specs, (bb * a_rows, len(taus) * pairs), (c_rows // c_len,)


def ladder_early(taus, integral):
    specs, shape, grid = ladder_specs(taus, integral)
    return call(
        functools.partial(early_kernel, len(taus)),
        [t for t, _ in taus] + [integral],
        specs,
        jax.ShapeDtypeStruct(shape[::-1], jnp.float32),
        pl.BlockSpec(shape[::-1], lambda i: (0, 0)),
        [],
        grid=grid,
        scratch=[pltpu.VMEM(shape, jnp.float32)],
        vmem=52,
    )[0]


def ladder_late(slots, early, added, taus, integral, owners):
    specs, shape, grid = ladder_specs(taus, integral)
    pairs = taus[0][0].shape[1]
    _, bb, a_rows, _ = integral.shape
    out = (owners, bb, slots.shape[0] * pairs // owners, a_rows)
    return call(
        functools.partial(late_kernel, len(taus)),
        [slots, early, added] + [t for t, _ in taus] + [integral],
        [pl.BlockSpec(memory_space=pltpu.SMEM)]
        + [pl.BlockSpec(t.shape, lambda i: (0, 0)) for t in (early, added)]
        + specs,
        jax.ShapeDtypeStruct(out, jnp.float32),
        pl.BlockSpec(out, lambda i: (0, 0, 0, 0)),
        [],
        grid=grid,
        scratch=[
            pltpu.VMEM(shape, jnp.float32),
            pltpu.VMEM((early.shape[0] + shape[1], shape[0]), jnp.float32),
        ],
        vmem=52,
    )[0]


def spread(rows, n, z):
    heres = [lax.ppermute(rows, "out", [(0, k)]) for k in range(1, n)]
    for k, here in zip(range(1, n), heres):
        rows = jnp.where(z == k, here, rows)
    return rows


def everywhere(shared, vir, through):
    me = lax.axis_index("vir")

    def swap(array, mask):
        return lax.ppermute(array, "vir", [(k, k ^ mask) for k in range(vir)])

    if vir & (vir - 1) == 0 and 2 < vir <= 8:
        masks = list(range(0, vir, 2))
        slabs = [shared] + [swap(shared, m) for m in masks[1:]]
        packed, through = pack(slabs, through)
        packs = [packed, swap(packed, 1)]
        places = jnp.stack([me ^ m ^ core for core in (0, 1) for m in masks])
    else:
        packs = [lax.all_gather(shared, "vir", axis=1, tiled=True)[None]]
        places = jnp.zeros((1,), jnp.int32)
    return assemble(packs, places.astype(jnp.int32), through)


def body(factors, amplitudes):
    a_rows, c_rows, _ = factors.shape
    n = lax.axis_size("out")
    vir = lax.axis_size("vir")
    z = lax.axis_index("out")

    def send(array, *ways):
        return lax.ppermute(array, "out", ways)

    own = amplitudes.transpose(1, 0, 2)
    token = jnp.zeros((8, LANES), jnp.float32)
    shared = spread(factors[:BB], n, z)
    batch, [token] = everywhere(shared, vir, [token])
    cut = 3 * c_rows // 4 if c_rows % 64 == 0 else c_rows
    spans = [(0, cut), (cut, c_rows)] if cut < c_rows else [(0, c_rows)]
    made = []

    def make():
        nonlocal token
        part, [token] = integrals(factors, batch, *spans[len(made)], [token])
        made.append(part)

    make()
    if n == 4:
        inside = (z == 1) | (z == 2)
        second = send(amplitudes, (2, 0), (1, 3))
        first = send(own, (3, 1), (1, 0), (0, 2), (2, 3))
        onward, kept = [], [own[i:j] for i, j in spans]
        for span in spans:
            part, [token] = pick(inside, first, own, *span, [token])
            onward.append(part)
        sides, middle = [], []
        for k in range(len(spans)):
            if k:
                make()
            token, onward[k], kept[k] = fence([token, onward[k], kept[k]])
            middle.append(send(kept[k], (2, 1), (1, 2)))
            sides.append(send(onward[k], (1, 0), (0, 1), (2, 3), (3, 2)))
        token, second = fence([token, second], MUCH)
        [sides[0]] = fence(sides[:1], MUCH)
        second, [token] = turn(second, [token])
        late = [[(t, 0) for t in pair] for pair in zip(sides, middle)]
        early = [own, first, second]
        slots = jnp.array([[0, 1, 2, 3], [3, 0, 4, 1], [1, 4, 0, 3], [3, 2, 1, 0]], jnp.int32)[z]
    else:
        gathered = lax.all_gather(own, "out")
        early, late = [own], [[(gathered[k], i) for k in range(n)] for i, _ in spans]
        slots = jnp.arange(1, n + 1, dtype=jnp.int32)
    while len(made) < len(spans):
        make()

    known, added = None, None
    for part, (start, _) in zip(made, spans):
        terms = ladder_early([(t, start) for t in early], part)
        known = terms if known is None else known + terms
    for part, taus in zip(made[:-1], late):
        added = ladder_early(taus, part)
    if added is None:
        rows = sum(t.shape[1] for t, _ in late[-1])
        added = jnp.zeros((rows, BB * a_rows), jnp.float32)
    parts = ladder_late(slots, known, added, late[-1], made[-1], vir)
    swapped = lax.all_to_all(parts, "vir", split_axis=0, concat_axis=0)
    return jnp.sum(swapped, axis=0)


def solution(mesh):
    placed = (P("out", "vir", None), P("out", "vir", None))
    return jax.shard_map(
        body, mesh=mesh, in_specs=placed, out_specs=P(None, "vir", "out"), check_vma=False
    )
```

```python
import functools

import jax
import jax.numpy as jnp
from jax import lax
from jax.experimental import pallas as pl
from jax.experimental.pallas import tpu as pltpu
from jax.sharding import PartitionSpec as P

BB = 2
LANES = 128
NT = (((1,), (1,)), ((), ()))
NN = (((1,), (0,)), ((), ()))
LITTLE = pl.CostEstimate(flops=1024, bytes_accessed=1024, transcendentals=0)
MUCH = pl.CostEstimate(flops=2 * 10**10, bytes_accessed=4 * 10**7, transcendentals=0)


def largest_part(extent, limit):
    part = min(extent, limit)
    while extent % part:
        part -= 1
    return part


def call(kernel, inputs, in_specs, out_shape, out_spec, through, grid=(1,), scratch=(), vmem=52):
    n_in, n_thru = len(inputs), len(through)

    def run(*refs):
        outs = refs[n_in + n_thru :]
        kernel(*refs[:n_in], outs[0], *outs[1 + n_thru :])

    anywhere = pl.BlockSpec(memory_space=pl.ANY)
    out = pl.pallas_call(
        run,
        grid=grid,
        in_specs=list(in_specs) + [anywhere] * n_thru,
        out_specs=[out_spec] + [anywhere] * n_thru,
        out_shape=[out_shape] + [jax.ShapeDtypeStruct(t.shape, t.dtype) for t in through],
        input_output_aliases={n_in + k: 1 + k for k in range(n_thru)},
        scratch_shapes=list(scratch),
        compiler_params=pltpu.CompilerParams(vmem_limit_bytes=vmem * 2**20),
        cost_estimate=LITTLE,
    )(*inputs, *through)
    return out[0], list(out[1:])


def fence(arrays, cost=LITTLE):
    anywhere = [pl.BlockSpec(memory_space=pl.ANY)] * len(arrays)
    return pl.pallas_call(
        lambda *refs: None,
        in_specs=anywhere,
        out_specs=anywhere,
        out_shape=[jax.ShapeDtypeStruct(t.shape, t.dtype) for t in arrays],
        input_output_aliases={k: k for k in range(len(arrays))},
        cost_estimate=cost,
    )(*arrays)


def pick_kernel(flag_ref, first_ref, other_ref, out_ref):
    @pl.when(flag_ref[0] == 1)
    def _():
        out_ref[...] = first_ref[...]

    @pl.when(flag_ref[0] == 0)
    def _():
        out_ref[...] = other_ref[...]


def pick(flag, first, other, start, stop, through):
    c_len = largest_part(stop - start, 16)
    begin = start // c_len
    block = (c_len,) + first.shape[1:]
    spec = pl.BlockSpec(block, lambda i: (begin + i, 0, 0))
    return call(
        pick_kernel,
        [flag.astype(jnp.int32).reshape(1), first, other],
        [pl.BlockSpec(memory_space=pltpu.SMEM), spec, spec],
        jax.ShapeDtypeStruct((stop - start,) + first.shape[1:], first.dtype),
        pl.BlockSpec(block, lambda i: (i, 0, 0)),
        through,
        grid=((stop - start) // c_len,),
    )


def pack_kernel(*refs):
    for k, slab in enumerate(refs[:-1]):
        refs[-1][k] = slab[...]


def pack(slabs, through):
    vmem = pl.BlockSpec(memory_space=pltpu.VMEM)
    shape = jax.ShapeDtypeStruct((len(slabs),) + slabs[0].shape, slabs[0].dtype)
    return call(pack_kernel, slabs, [vmem] * len(slabs), shape, vmem, through)


def turn_kernel(in_ref, out_ref):
    whole = in_ref[...].astype(jnp.float32)
    out_ref[...] = jnp.swapaxes(whole, 0, 1).astype(out_ref.dtype)


def turn(array, through):
    pairs, c_rows, d_len = array.shape
    c_len = largest_part(c_rows, 16)
    return call(
        turn_kernel,
        [array],
        [pl.BlockSpec((pairs, c_len, d_len), lambda i: (0, i, 0))],
        jax.ShapeDtypeStruct((c_rows, pairs, d_len), array.dtype),
        pl.BlockSpec((c_len, pairs, d_len), lambda i: (i, 0, 0)),
        through,
        grid=(c_rows // c_len,),
    )


def assemble_kernel(*refs):
    place_ref, packs, out_ref, whole_ref = refs[0], refs[1:-2], refs[-2], refs[-1]
    piece = packs[0].shape[2]
    for i, packed in enumerate(packs):
        for k in range(packed.shape[0]):
            start = pl.multiple_of(place_ref[i * packed.shape[0] + k] * piece, piece)
            whole_ref[:, pl.ds(start, piece), :] = packed[k]
    for b in range(out_ref.shape[0]):
        out_ref[b] = whole_ref[b].T


def assemble(packs, places, through):
    count, bb, piece, aux_len = packs[0].shape
    d_len = piece * count * len(packs)
    vmem = pl.BlockSpec(memory_space=pltpu.VMEM)
    return call(
        assemble_kernel,
        [places] + packs,
        [pl.BlockSpec(memory_space=pltpu.SMEM)] + [vmem] * len(packs),
        jax.ShapeDtypeStruct((bb, aux_len, d_len), jnp.bfloat16),
        vmem,
        through,
        scratch=[pltpu.VMEM((bb, d_len, aux_len), jnp.bfloat16)],
    )


def integral_kernel(factor_ref, batch_ref, out_ref):
    a_len, c_len, aux_len = factor_ref.shape
    d_len = out_ref.shape[3]
    rows = factor_ref[...].reshape(a_len * c_len, aux_len)
    wide = largest_part(d_len // LANES, 2) * LANES
    for b in range(out_ref.shape[1]):
        for j in range(0, d_len, wide):
            tile = lax.dot_general(
                rows, batch_ref[b, :, j : j + wide], NN, preferred_element_type=jnp.float32
            )
            turned = jnp.swapaxes(tile.reshape(a_len, c_len, wide), 0, 1)
            out_ref[:, b, :, j : j + wide] = turned.astype(jnp.bfloat16)


def integrals(factors, batch, start, stop, through):
    a_rows, c_rows, aux_len = factors.shape
    bb, _, d_len = batch.shape
    c_len = largest_part(c_rows, 8)
    first = start // c_len
    return call(
        integral_kernel,
        [factors, batch],
        [
            pl.BlockSpec((a_rows, c_len, aux_len), lambda i: (0, first + i, 0)),
            pl.BlockSpec((bb, aux_len, d_len), lambda i: (0, 0, 0)),
        ],
        jax.ShapeDtypeStruct((stop - start, bb, a_rows, d_len), jnp.bfloat16),
        pl.BlockSpec((c_len, bb, a_rows, d_len), lambda i: (i, 0, 0, 0)),
        through,
        grid=((stop - start) // c_len,),
    )


def sums(tau_of, integral_ref, total_ref):
    c_len, bb, a_rows, d_len = integral_ref.shape

    @pl.when(pl.program_id(0) == 0)
    def _():
        total_ref[...] = jnp.zeros_like(total_ref)

    left = [integral_ref[c].reshape(bb * a_rows, d_len) for c in range(c_len)]
    right = [tau_of(c) for c in range(c_len)]
    total_ref[...] += lax.dot_general(
        jnp.concatenate(left, axis=1),
        jnp.concatenate(right, axis=1),
        NT,
        preferred_element_type=jnp.float32,
    )


def early_kernel(count, *refs):
    tau_refs, (integral_ref, out_ref, total_ref) = refs[:count], refs[count:]
    sums(
        lambda c: jnp.concatenate([r[c] for r in tau_refs], axis=0),
        integral_ref,
        total_ref,
    )

    @pl.when(pl.program_id(0) == pl.num_programs(0) - 1)
    def _():
        out_ref[...] = total_ref[...].T


def late_kernel(count, *refs):
    (slot_ref, early_ref, added_ref), refs = refs[:3], refs[3:]
    tau_refs, (integral_ref, out_ref, total_ref, all_ref) = refs[:count], refs[count:]
    pairs = tau_refs[0].shape[1]
    sums(
        lambda c: jnp.concatenate([r[c] for r in tau_refs], axis=0),
        integral_ref,
        total_ref,
    )

    @pl.when(pl.program_id(0) == pl.num_programs(0) - 1)
    def _():
        known = early_ref.shape[0]
        all_ref[:known] = early_ref[...]
        all_ref[known:] = added_ref[...] + total_ref[...].T
        owners, bb, rows, a_rows = out_ref.shape
        each = pairs // rows
        for j in range(owners):
            start = pl.multiple_of(slot_ref[j // each] * pairs, pairs) + j % each * rows
            for b in range(bb):
                out_ref[j, b] = all_ref[pl.ds(start, rows), b * a_rows : (b + 1) * a_rows]


def ladder_specs(taus, integral):
    _, pairs, d_len = taus[0][0].shape
    c_rows, bb, a_rows, _ = integral.shape
    c_len = largest_part(c_rows, 8)
    specs = [
        pl.BlockSpec((c_len, pairs, d_len), lambda i, k=start // c_len: (k + i, 0, 0))
        for _, start in taus
    ]
    specs.append(pl.BlockSpec((c_len, bb, a_rows, d_len), lambda i: (i, 0, 0, 0)))
    return specs, (bb * a_rows, len(taus) * pairs), (c_rows // c_len,)


def ladder_early(taus, integral):
    specs, shape, grid = ladder_specs(taus, integral)
    return call(
        functools.partial(early_kernel, len(taus)),
        [t for t, _ in taus] + [integral],
        specs,
        jax.ShapeDtypeStruct(shape[::-1], jnp.float32),
        pl.BlockSpec(shape[::-1], lambda i: (0, 0)),
        [],
        grid=grid,
        scratch=[pltpu.VMEM(shape, jnp.float32)],
        vmem=52,
    )[0]


def ladder_late(slots, early, added, taus, integral, owners):
    specs, shape, grid = ladder_specs(taus, integral)
    pairs = taus[0][0].shape[1]
    _, bb, a_rows, _ = integral.shape
    out = (owners, bb, slots.shape[0] * pairs // owners, a_rows)
    return call(
        functools.partial(late_kernel, len(taus)),
        [slots, early, added] + [t for t, _ in taus] + [integral],
        [pl.BlockSpec(memory_space=pltpu.SMEM)]
        + [pl.BlockSpec(t.shape, lambda i: (0, 0)) for t in (early, added)]
        + specs,
        jax.ShapeDtypeStruct(out, jnp.float32),
        pl.BlockSpec(out, lambda i: (0, 0, 0, 0)),
        [],
        grid=grid,
        scratch=[
            pltpu.VMEM(shape, jnp.float32),
            pltpu.VMEM((early.shape[0] + shape[1], shape[0]), jnp.float32),
        ],
        vmem=52,
    )[0]


def spread(rows, n, z):
    heres = [lax.ppermute(rows, "out", [(0, k)]) for k in range(n - 1, 0, -1)]
    for k, here in zip(range(n - 1, 0, -1), heres):
        rows = jnp.where(z == k, here, rows)
    return rows


def everywhere(shared, vir, through):
    me = lax.axis_index("vir")

    def swap(array, mask):
        return lax.ppermute(array, "vir", [(k, k ^ mask) for k in range(vir)])

    if vir & (vir - 1) == 0 and 2 < vir <= 8:
        masks = list(range(0, vir, 2))
        slabs = [shared] + [swap(shared, m) for m in masks[1:]]
        packed, through = pack(slabs, through)
        packs = [packed, swap(packed, 1)]
        places = jnp.stack([me ^ m ^ core for core in (0, 1) for m in masks])
    else:
        packs = [lax.all_gather(shared, "vir", axis=1, tiled=True)[None]]
        places = jnp.zeros((1,), jnp.int32)
    return assemble(packs, places.astype(jnp.int32), through)


def body(factors, amplitudes):
    a_rows, c_rows, _ = factors.shape
    n = lax.axis_size("out")
    vir = lax.axis_size("vir")
    z = lax.axis_index("out")

    def send(array, *ways):
        return lax.ppermute(array, "out", ways)

    own = amplitudes.transpose(1, 0, 2)
    token = jnp.zeros((8, LANES), jnp.float32)
    shared = spread(factors[:BB], n, z)
    batch, [token] = everywhere(shared, vir, [token])
    cut = 3 * c_rows // 4 if c_rows % 64 == 0 else c_rows
    spans = [(0, cut), (cut, c_rows)] if cut < c_rows else [(0, c_rows)]
    made = []

    def make():
        nonlocal token
        part, [token] = integrals(factors, batch, *spans[len(made)], [token])
        made.append(part)

    make()
    if n == 4:
        inside = (z == 1) | (z == 2)
        second = send(amplitudes, (2, 0), (1, 3))
        first = send(own, (3, 1), (1, 0), (0, 2), (2, 3))
        onward, kept = [], [own[i:j] for i, j in spans]
        for span in spans:
            part, [token] = pick(inside, first, own, *span, [token])
            onward.append(part)
        sides, middle = [], []
        for k in range(len(spans)):
            if k:
                make()
            token, onward[k], kept[k] = fence([token, onward[k], kept[k]])
            middle.append(send(kept[k], (2, 1), (1, 2)))
            sides.append(send(onward[k], (1, 0), (0, 1), (2, 3), (3, 2)))
        token, second = fence([token, second], MUCH)
        [sides[0]] = fence(sides[:1], MUCH)
        second, [token] = turn(second, [token])
        late = [[(t, 0) for t in pair] for pair in zip(sides, middle)]
        early = [own, first, second]
        slots = jnp.array([[0, 1, 2, 3], [3, 0, 4, 1], [1, 4, 0, 3], [3, 2, 1, 0]], jnp.int32)[z]
    else:
        gathered = lax.all_gather(own, "out")
        early, late = [own], [[(gathered[k], i) for k in range(n)] for i, _ in spans]
        slots = jnp.arange(1, n + 1, dtype=jnp.int32)
    while len(made) < len(spans):
        make()

    known, added = None, None
    for part, (start, _) in zip(made, spans):
        terms = ladder_early([(t, start) for t in early], part)
        known = terms if known is None else known + terms
    for part, taus in zip(made[:-1], late):
        added = ladder_early(taus, part)
    if added is None:
        rows = sum(t.shape[1] for t, _ in late[-1])
        added = jnp.zeros((rows, BB * a_rows), jnp.float32)
    parts = ladder_late(slots, known, added, late[-1], made[-1], vir)
    swapped = lax.all_to_all(parts, "vir", split_axis=0, concat_axis=0)
    return jnp.sum(swapped, axis=0)


def solution(mesh):
    placed = (P("out", "vir", None), P("out", "vir", None))
    return jax.shard_map(
        body, mesh=mesh, in_specs=placed, out_specs=P(None, "vir", "out"), check_vma=False
    )
```

```python
import functools

import jax
import jax.numpy as jnp
from jax import lax
from jax.experimental import pallas as pl
from jax.experimental.pallas import tpu as pltpu
from jax.sharding import PartitionSpec as P

BB = 2
LANES = 128
NT = (((1,), (1,)), ((), ()))
NN = (((1,), (0,)), ((), ()))
LITTLE = pl.CostEstimate(flops=1024, bytes_accessed=1024, transcendentals=0)
MUCH = pl.CostEstimate(flops=2 * 10**10, bytes_accessed=4 * 10**7, transcendentals=0)


def largest_part(extent, limit):
    part = min(extent, limit)
    while extent % part:
        part -= 1
    return part


def call(kernel, inputs, in_specs, out_shape, out_spec, through, grid=(1,), scratch=(), vmem=52):
    n_in, n_thru = len(inputs), len(through)

    def run(*refs):
        outs = refs[n_in + n_thru :]
        kernel(*refs[:n_in], outs[0], *outs[1 + n_thru :])

    anywhere = pl.BlockSpec(memory_space=pl.ANY)
    out = pl.pallas_call(
        run,
        grid=grid,
        in_specs=list(in_specs) + [anywhere] * n_thru,
        out_specs=[out_spec] + [anywhere] * n_thru,
        out_shape=[out_shape] + [jax.ShapeDtypeStruct(t.shape, t.dtype) for t in through],
        input_output_aliases={n_in + k: 1 + k for k in range(n_thru)},
        scratch_shapes=list(scratch),
        compiler_params=pltpu.CompilerParams(vmem_limit_bytes=vmem * 2**20),
        cost_estimate=LITTLE,
    )(*inputs, *through)
    return out[0], list(out[1:])


def fence(arrays, cost=LITTLE):
    anywhere = [pl.BlockSpec(memory_space=pl.ANY)] * len(arrays)
    return pl.pallas_call(
        lambda *refs: None,
        in_specs=anywhere,
        out_specs=anywhere,
        out_shape=[jax.ShapeDtypeStruct(t.shape, t.dtype) for t in arrays],
        input_output_aliases={k: k for k in range(len(arrays))},
        cost_estimate=cost,
    )(*arrays)


def pick_kernel(flag_ref, first_ref, other_ref, out_ref):
    @pl.when(flag_ref[0] == 1)
    def _():
        out_ref[...] = first_ref[...]

    @pl.when(flag_ref[0] == 0)
    def _():
        out_ref[...] = other_ref[...]


def pick(flag, first, other, start, stop, through):
    c_len = largest_part(stop - start, 16)
    begin = start // c_len
    block = (c_len,) + first.shape[1:]
    spec = pl.BlockSpec(block, lambda i: (begin + i, 0, 0))
    return call(
        pick_kernel,
        [flag.astype(jnp.int32).reshape(1), first, other],
        [pl.BlockSpec(memory_space=pltpu.SMEM), spec, spec],
        jax.ShapeDtypeStruct((stop - start,) + first.shape[1:], first.dtype),
        pl.BlockSpec(block, lambda i: (i, 0, 0)),
        through,
        grid=((stop - start) // c_len,),
    )


def pack_kernel(*refs):
    for k, slab in enumerate(refs[:-1]):
        refs[-1][k] = slab[...]


def pack(slabs, through):
    vmem = pl.BlockSpec(memory_space=pltpu.VMEM)
    shape = jax.ShapeDtypeStruct((len(slabs),) + slabs[0].shape, slabs[0].dtype)
    return call(pack_kernel, slabs, [vmem] * len(slabs), shape, vmem, through)


def turn_kernel(in_ref, out_ref):
    whole = in_ref[...].astype(jnp.float32)
    out_ref[...] = jnp.swapaxes(whole, 0, 1).astype(out_ref.dtype)


def turn(array, through):
    pairs, c_rows, d_len = array.shape
    c_len = largest_part(c_rows, 16)
    return call(
        turn_kernel,
        [array],
        [pl.BlockSpec((pairs, c_len, d_len), lambda i: (0, i, 0))],
        jax.ShapeDtypeStruct((c_rows, pairs, d_len), array.dtype),
        pl.BlockSpec((c_len, pairs, d_len), lambda i: (i, 0, 0)),
        through,
        grid=(c_rows // c_len,),
    )


def assemble_kernel(*refs):
    place_ref, packs, out_ref, whole_ref = refs[0], refs[1:-2], refs[-2], refs[-1]
    piece = packs[0].shape[2]
    for i, packed in enumerate(packs):
        for k in range(packed.shape[0]):
            start = pl.multiple_of(place_ref[i * packed.shape[0] + k] * piece, piece)
            whole_ref[:, pl.ds(start, piece), :] = packed[k]
    for b in range(out_ref.shape[0]):
        out_ref[b] = whole_ref[b].T


def assemble(packs, places, through):
    count, bb, piece, aux_len = packs[0].shape
    d_len = piece * count * len(packs)
    vmem = pl.BlockSpec(memory_space=pltpu.VMEM)
    return call(
        assemble_kernel,
        [places] + packs,
        [pl.BlockSpec(memory_space=pltpu.SMEM)] + [vmem] * len(packs),
        jax.ShapeDtypeStruct((bb, aux_len, d_len), jnp.bfloat16),
        vmem,
        through,
        scratch=[pltpu.VMEM((bb, d_len, aux_len), jnp.bfloat16)],
    )


def integral_kernel(factor_ref, batch_ref, out_ref):
    a_len, c_len, aux_len = factor_ref.shape
    d_len = out_ref.shape[3]
    rows = factor_ref[...].reshape(a_len * c_len, aux_len)
    wide = largest_part(d_len // LANES, 2) * LANES
    for b in range(out_ref.shape[1]):
        for j in range(0, d_len, wide):
            tile = lax.dot_general(
                rows, batch_ref[b, :, j : j + wide], NN, preferred_element_type=jnp.float32
            )
            turned = jnp.swapaxes(tile.reshape(a_len, c_len, wide), 0, 1)
            out_ref[:, b, :, j : j + wide] = turned.astype(jnp.bfloat16)


def integrals(factors, batch, start, stop, through):
    a_rows, c_rows, aux_len = factors.shape
    bb, _, d_len = batch.shape
    c_len = largest_part(c_rows, 8)
    first = start // c_len
    return call(
        integral_kernel,
        [factors, batch],
        [
            pl.BlockSpec((a_rows, c_len, aux_len), lambda i: (0, first + i, 0)),
            pl.BlockSpec((bb, aux_len, d_len), lambda i: (0, 0, 0)),
        ],
        jax.ShapeDtypeStruct((stop - start, bb, a_rows, d_len), jnp.bfloat16),
        pl.BlockSpec((c_len, bb, a_rows, d_len), lambda i: (i, 0, 0, 0)),
        through,
        grid=((stop - start) // c_len,),
    )


def sums(tau_of, integral_ref, total_ref):
    c_len, bb, a_rows, d_len = integral_ref.shape

    @pl.when(pl.program_id(0) == 0)
    def _():
        total_ref[...] = jnp.zeros_like(total_ref)

    left = [integral_ref[c].reshape(bb * a_rows, d_len) for c in range(c_len)]
    right = [tau_of(c) for c in range(c_len)]
    total_ref[...] += lax.dot_general(
        jnp.concatenate(left, axis=1),
        jnp.concatenate(right, axis=1),
        NT,
        preferred_element_type=jnp.float32,
    )


def early_kernel(count, *refs):
    tau_refs, (integral_ref, out_ref, total_ref) = refs[:count], refs[count:]
    sums(
        lambda c: jnp.concatenate([r[c] for r in tau_refs], axis=0),
        integral_ref,
        total_ref,
    )

    @pl.when(pl.program_id(0) == pl.num_programs(0) - 1)
    def _():
        out_ref[...] = total_ref[...].T


def late_kernel(count, *refs):
    (slot_ref, early_ref, added_ref), refs = refs[:3], refs[3:]
    tau_refs, (integral_ref, out_ref, total_ref, all_ref) = refs[:count], refs[count:]
    pairs = tau_refs[0].shape[1]
    sums(
        lambda c: jnp.concatenate([r[c] for r in tau_refs], axis=0),
        integral_ref,
        total_ref,
    )

    @pl.when(pl.program_id(0) == pl.num_programs(0) - 1)
    def _():
        known = early_ref.shape[0]
        all_ref[:known] = early_ref[...]
        all_ref[known:] = added_ref[...] + total_ref[...].T
        owners, bb, rows, a_rows = out_ref.shape
        each = pairs // rows
        for j in range(owners):
            start = pl.multiple_of(slot_ref[j // each] * pairs, pairs) + j % each * rows
            for b in range(bb):
                out_ref[j, b] = all_ref[pl.ds(start, rows), b * a_rows : (b + 1) * a_rows]


def ladder_specs(taus, integral, limit=8):
    _, pairs, d_len = taus[0][0].shape
    c_rows, bb, a_rows, _ = integral.shape
    c_len = largest_part(c_rows, limit)
    specs = [
        pl.BlockSpec((c_len, pairs, d_len), lambda i, k=start // c_len: (k + i, 0, 0))
        for _, start in taus
    ]
    specs.append(pl.BlockSpec((c_len, bb, a_rows, d_len), lambda i: (i, 0, 0, 0)))
    return specs, (bb * a_rows, len(taus) * pairs), (c_rows // c_len,)


def ladder_early(taus, integral):
    specs, shape, grid = ladder_specs(taus, integral)
    return call(
        functools.partial(early_kernel, len(taus)),
        [t for t, _ in taus] + [integral],
        specs,
        jax.ShapeDtypeStruct(shape[::-1], jnp.float32),
        pl.BlockSpec(shape[::-1], lambda i: (0, 0)),
        [],
        grid=grid,
        scratch=[pltpu.VMEM(shape, jnp.float32)],
        vmem=52,
    )[0]


def ladder_late(slots, early, added, taus, integral, owners):
    specs, shape, grid = ladder_specs(taus, integral, 4)
    pairs = taus[0][0].shape[1]
    _, bb, a_rows, _ = integral.shape
    out = (owners, bb, slots.shape[0] * pairs // owners, a_rows)
    return call(
        functools.partial(late_kernel, len(taus)),
        [slots, early, added] + [t for t, _ in taus] + [integral],
        [pl.BlockSpec(memory_space=pltpu.SMEM)]
        + [pl.BlockSpec(t.shape, lambda i: (0, 0)) for t in (early, added)]
        + specs,
        jax.ShapeDtypeStruct(out, jnp.float32),
        pl.BlockSpec(out, lambda i: (0, 0, 0, 0)),
        [],
        grid=grid,
        scratch=[
            pltpu.VMEM(shape, jnp.float32),
            pltpu.VMEM((early.shape[0] + shape[1], shape[0]), jnp.float32),
        ],
        vmem=52,
    )[0]


def spread(rows, n, z):
    heres = [lax.ppermute(rows, "out", [(0, k)]) for k in range(1, n)]
    for k, here in zip(range(1, n), heres):
        rows = jnp.where(z == k, here, rows)
    return rows


def everywhere(shared, vir, through):
    me = lax.axis_index("vir")

    def swap(array, mask):
        return lax.ppermute(array, "vir", [(k, k ^ mask) for k in range(vir)])

    if vir & (vir - 1) == 0 and 2 < vir <= 8:
        masks = list(range(0, vir, 2))
        slabs = [shared] + [swap(shared, m) for m in masks[1:]]
        packed, through = pack(slabs, through)
        packs = [packed, swap(packed, 1)]
        places = jnp.stack([me ^ m ^ core for core in (0, 1) for m in masks])
    else:
        packs = [lax.all_gather(shared, "vir", axis=1, tiled=True)[None]]
        places = jnp.zeros((1,), jnp.int32)
    return assemble(packs, places.astype(jnp.int32), through)


def body(factors, amplitudes):
    a_rows, c_rows, _ = factors.shape
    n = lax.axis_size("out")
    vir = lax.axis_size("vir")
    z = lax.axis_index("out")

    def send(array, *ways):
        return lax.ppermute(array, "out", ways)

    own = amplitudes.transpose(1, 0, 2)
    token = jnp.zeros((8, LANES), jnp.float32)
    shared = spread(factors[:BB], n, z)
    batch, [token] = everywhere(shared, vir, [token])
    cut = 3 * c_rows // 4 if c_rows % 64 == 0 else c_rows
    spans = [(0, cut), (cut, c_rows)] if cut < c_rows else [(0, c_rows)]
    made = []

    def make():
        nonlocal token
        part, [token] = integrals(factors, batch, *spans[len(made)], [token])
        made.append(part)

    make()
    if n == 4:
        inside = (z == 1) | (z == 2)
        second = send(amplitudes, (2, 0), (1, 3))
        first = send(own, (3, 1), (1, 0), (0, 2), (2, 3))
        onward, kept = [], [own[i:j] for i, j in spans]
        for span in spans:
            part, [token] = pick(inside, first, own, *span, [token])
            onward.append(part)
        sides, middle = [], []
        for k in range(len(spans)):
            if k:
                make()
            token, onward[k], kept[k] = fence([token, onward[k], kept[k]])
            middle.append(send(kept[k], (2, 1), (1, 2)))
            sides.append(send(onward[k], (1, 0), (0, 1), (2, 3), (3, 2)))
        token, second = fence([token, second], MUCH)
        [sides[0]] = fence(sides[:1], MUCH)
        second, [token] = turn(second, [token])
        late = [[(t, 0) for t in pair] for pair in zip(sides, middle)]
        early = [own, first, second]
        slots = jnp.array([[0, 1, 2, 3], [3, 0, 4, 1], [1, 4, 0, 3], [3, 2, 1, 0]], jnp.int32)[z]
    else:
        gathered = lax.all_gather(own, "out")
        early, late = [own], [[(gathered[k], i) for k in range(n)] for i, _ in spans]
        slots = jnp.arange(1, n + 1, dtype=jnp.int32)
    while len(made) < len(spans):
        make()

    known, added = None, None
    for part, (start, _) in zip(made, spans):
        terms = ladder_early([(t, start) for t in early], part)
        known = terms if known is None else known + terms
    for part, taus in zip(made[:-1], late):
        added = ladder_early(taus, part)
    if added is None:
        rows = sum(t.shape[1] for t, _ in late[-1])
        added = jnp.zeros((rows, BB * a_rows), jnp.float32)
    parts = ladder_late(slots, known, added, late[-1], made[-1], vir)
    swapped = lax.all_to_all(parts, "vir", split_axis=0, concat_axis=0)
    return jnp.sum(swapped, axis=0)


def solution(mesh):
    placed = (P("out", "vir", None), P("out", "vir", None))
    return jax.shard_map(
        body, mesh=mesh, in_specs=placed, out_specs=P(None, "vir", "out"), check_vma=False
    )
```

```python
import functools

import jax
import jax.numpy as jnp
from jax import lax
from jax.experimental import pallas as pl
from jax.experimental.pallas import tpu as pltpu
from jax.sharding import PartitionSpec as P

BB = 2
LANES = 128
NT = (((1,), (1,)), ((), ()))
NN = (((1,), (0,)), ((), ()))
LITTLE = pl.CostEstimate(flops=1024, bytes_accessed=1024, transcendentals=0)
MUCH = pl.CostEstimate(flops=2 * 10**10, bytes_accessed=4 * 10**7, transcendentals=0)


def largest_part(extent, limit):
    part = min(extent, limit)
    while extent % part:
        part -= 1
    return part


def call(kernel, inputs, in_specs, out_shape, out_spec, through, grid=(1,), scratch=(), vmem=52):
    n_in, n_thru = len(inputs), len(through)

    def run(*refs):
        outs = refs[n_in + n_thru :]
        kernel(*refs[:n_in], outs[0], *outs[1 + n_thru :])

    anywhere = pl.BlockSpec(memory_space=pl.ANY)
    out = pl.pallas_call(
        run,
        grid=grid,
        in_specs=list(in_specs) + [anywhere] * n_thru,
        out_specs=[out_spec] + [anywhere] * n_thru,
        out_shape=[out_shape] + [jax.ShapeDtypeStruct(t.shape, t.dtype) for t in through],
        input_output_aliases={n_in + k: 1 + k for k in range(n_thru)},
        scratch_shapes=list(scratch),
        compiler_params=pltpu.CompilerParams(vmem_limit_bytes=vmem * 2**20),
        cost_estimate=LITTLE,
    )(*inputs, *through)
    return out[0], list(out[1:])


def fence(arrays, cost=LITTLE):
    anywhere = [pl.BlockSpec(memory_space=pl.ANY)] * len(arrays)
    return pl.pallas_call(
        lambda *refs: None,
        in_specs=anywhere,
        out_specs=anywhere,
        out_shape=[jax.ShapeDtypeStruct(t.shape, t.dtype) for t in arrays],
        input_output_aliases={k: k for k in range(len(arrays))},
        cost_estimate=cost,
    )(*arrays)


def pick_kernel(flag_ref, first_ref, other_ref, out_ref):
    @pl.when(flag_ref[0] == 1)
    def _():
        out_ref[...] = first_ref[...]

    @pl.when(flag_ref[0] == 0)
    def _():
        out_ref[...] = other_ref[...]


def pick(flag, first, other, start, stop, through):
    c_len = largest_part(stop - start, 16)
    begin = start // c_len
    block = (c_len,) + first.shape[1:]
    spec = pl.BlockSpec(block, lambda i: (begin + i, 0, 0))
    return call(
        pick_kernel,
        [flag.astype(jnp.int32).reshape(1), first, other],
        [pl.BlockSpec(memory_space=pltpu.SMEM), spec, spec],
        jax.ShapeDtypeStruct((stop - start,) + first.shape[1:], first.dtype),
        pl.BlockSpec(block, lambda i: (i, 0, 0)),
        through,
        grid=((stop - start) // c_len,),
    )


def pack_kernel(*refs):
    for k, slab in enumerate(refs[:-1]):
        refs[-1][k] = slab[...]


def pack(slabs, through):
    vmem = pl.BlockSpec(memory_space=pltpu.VMEM)
    shape = jax.ShapeDtypeStruct((len(slabs),) + slabs[0].shape, slabs[0].dtype)
    return call(pack_kernel, slabs, [vmem] * len(slabs), shape, vmem, through)


def turn_kernel(in_ref, out_ref):
    whole = in_ref[...].astype(jnp.float32)
    out_ref[...] = jnp.swapaxes(whole, 0, 1).astype(out_ref.dtype)


def turn(array, through):
    pairs, c_rows, d_len = array.shape
    c_len = largest_part(c_rows, 16)
    return call(
        turn_kernel,
        [array],
        [pl.BlockSpec((pairs, c_len, d_len), lambda i: (0, i, 0))],
        jax.ShapeDtypeStruct((c_rows, pairs, d_len), array.dtype),
        pl.BlockSpec((c_len, pairs, d_len), lambda i: (i, 0, 0)),
        through,
        grid=(c_rows // c_len,),
    )


def assemble_kernel(*refs):
    place_ref, packs, out_ref, whole_ref = refs[0], refs[1:-2], refs[-2], refs[-1]
    piece = packs[0].shape[2]
    for i, packed in enumerate(packs):
        for k in range(packed.shape[0]):
            start = pl.multiple_of(place_ref[i * packed.shape[0] + k] * piece, piece)
            whole_ref[:, pl.ds(start, piece), :] = packed[k]
    for b in range(out_ref.shape[0]):
        out_ref[b] = whole_ref[b].T


def assemble(packs, places, through):
    count, bb, piece, aux_len = packs[0].shape
    d_len = piece * count * len(packs)
    vmem = pl.BlockSpec(memory_space=pltpu.VMEM)
    return call(
        assemble_kernel,
        [places] + packs,
        [pl.BlockSpec(memory_space=pltpu.SMEM)] + [vmem] * len(packs),
        jax.ShapeDtypeStruct((bb, aux_len, d_len), jnp.bfloat16),
        vmem,
        through,
        scratch=[pltpu.VMEM((bb, d_len, aux_len), jnp.bfloat16)],
    )


def integral_kernel(factor_ref, batch_ref, out_ref):
    a_len, c_len, aux_len = factor_ref.shape
    d_len = out_ref.shape[3]
    rows = factor_ref[...].reshape(a_len * c_len, aux_len)
    wide = largest_part(d_len // LANES, 2) * LANES
    for b in range(out_ref.shape[1]):
        for j in range(0, d_len, wide):
            tile = lax.dot_general(
                rows, batch_ref[b, :, j : j + wide], NN, preferred_element_type=jnp.float32
            )
            turned = jnp.swapaxes(tile.reshape(a_len, c_len, wide), 0, 1)
            out_ref[:, b, :, j : j + wide] = turned.astype(jnp.bfloat16)


def integrals(factors, batch, start, stop, through):
    a_rows, c_rows, aux_len = factors.shape
    bb, _, d_len = batch.shape
    c_len = largest_part(c_rows, 8)
    first = start // c_len
    return call(
        integral_kernel,
        [factors, batch],
        [
            pl.BlockSpec((a_rows, c_len, aux_len), lambda i: (0, first + i, 0)),
            pl.BlockSpec((bb, aux_len, d_len), lambda i: (0, 0, 0)),
        ],
        jax.ShapeDtypeStruct((stop - start, bb, a_rows, d_len), jnp.bfloat16),
        pl.BlockSpec((c_len, bb, a_rows, d_len), lambda i: (i, 0, 0, 0)),
        through,
        grid=((stop - start) // c_len,),
    )


def sums(tau_of, integral_ref, total_ref):
    c_len, bb, a_rows, d_len = integral_ref.shape

    @pl.when(pl.program_id(0) == 0)
    def _():
        total_ref[...] = jnp.zeros_like(total_ref)

    left = [integral_ref[c].reshape(bb * a_rows, d_len) for c in range(c_len)]
    right = [tau_of(c) for c in range(c_len)]
    total_ref[...] += lax.dot_general(
        jnp.concatenate(left, axis=1),
        jnp.concatenate(right, axis=1),
        NT,
        preferred_element_type=jnp.float32,
    )


def early_kernel(count, *refs):
    tau_refs, (integral_ref, out_ref, total_ref) = refs[:count], refs[count:]
    sums(
        lambda c: jnp.concatenate([r[c] for r in tau_refs], axis=0),
        integral_ref,
        total_ref,
    )

    @pl.when(pl.program_id(0) == pl.num_programs(0) - 1)
    def _():
        out_ref[...] = total_ref[...].T


def late_kernel(count, *refs):
    (slot_ref, early_ref, added_ref), refs = refs[:3], refs[3:]
    tau_refs, (integral_ref, out_ref, total_ref, all_ref) = refs[:count], refs[count:]
    pairs = tau_refs[0].shape[1]
    sums(
        lambda c: jnp.concatenate([r[c] for r in tau_refs], axis=0),
        integral_ref,
        total_ref,
    )

    @pl.when(pl.program_id(0) == pl.num_programs(0) - 1)
    def _():
        known = early_ref.shape[0]
        all_ref[:known] = early_ref[...]
        all_ref[known:] = added_ref[...] + total_ref[...].T
        owners, bb, rows, a_rows = out_ref.shape
        each = pairs // rows
        for j in range(owners):
            start = pl.multiple_of(slot_ref[j // each] * pairs, pairs) + j % each * rows
            for b in range(bb):
                out_ref[j, b] = all_ref[pl.ds(start, rows), b * a_rows : (b + 1) * a_rows]


def ladder_specs(taus, integral):
    _, pairs, d_len = taus[0][0].shape
    c_rows, bb, a_rows, _ = integral.shape
    c_len = largest_part(c_rows, 8)
    specs = [
        pl.BlockSpec((c_len, pairs, d_len), lambda i, k=start // c_len: (k + i, 0, 0))
        for _, start in taus
    ]
    specs.append(pl.BlockSpec((c_len, bb, a_rows, d_len), lambda i: (i, 0, 0, 0)))
    return specs, (bb * a_rows, len(taus) * pairs), (c_rows // c_len,)


def ladder_early(taus, integral):
    specs, shape, grid = ladder_specs(taus, integral)
    return call(
        functools.partial(early_kernel, len(taus)),
        [t for t, _ in taus] + [integral],
        specs,
        jax.ShapeDtypeStruct(shape[::-1], jnp.float32),
        pl.BlockSpec(shape[::-1], lambda i: (0, 0)),
        [],
        grid=grid,
        scratch=[pltpu.VMEM(shape, jnp.float32)],
        vmem=52,
    )[0]


def ladder_late(slots, early, added, taus, integral, owners):
    specs, shape, grid = ladder_specs(taus, integral)
    pairs = taus[0][0].shape[1]
    _, bb, a_rows, _ = integral.shape
    out = (owners, bb, slots.shape[0] * pairs // owners, a_rows)
    return call(
        functools.partial(late_kernel, len(taus)),
        [slots, early, added] + [t for t, _ in taus] + [integral],
        [pl.BlockSpec(memory_space=pltpu.SMEM)]
        + [pl.BlockSpec(t.shape, lambda i: (0, 0)) for t in (early, added)]
        + specs,
        jax.ShapeDtypeStruct(out, jnp.float32),
        pl.BlockSpec(out, lambda i: (0, 0, 0, 0)),
        [],
        grid=grid,
        scratch=[
            pltpu.VMEM(shape, jnp.float32),
            pltpu.VMEM((early.shape[0] + shape[1], shape[0]), jnp.float32),
        ],
        vmem=52,
    )[0]


def spread(rows, n, z):
    order = [1] + list(range(n - 1, 1, -1))
    heres = [lax.ppermute(rows, "out", [(0, k)]) for k in order]
    for k, here in zip(order, heres):
        rows = jnp.where(z == k, here, rows)
    return rows


def everywhere(shared, vir, through):
    me = lax.axis_index("vir")

    def swap(array, mask):
        return lax.ppermute(array, "vir", [(k, k ^ mask) for k in range(vir)])

    if vir & (vir - 1) == 0 and 2 < vir <= 8:
        masks = list(range(0, vir, 2))
        slabs = [shared] + [swap(shared, m) for m in masks[1:]]
        packed, through = pack(slabs, through)
        packs = [packed, swap(packed, 1)]
        places = jnp.stack([me ^ m ^ core for core in (0, 1) for m in masks])
    else:
        packs = [lax.all_gather(shared, "vir", axis=1, tiled=True)[None]]
        places = jnp.zeros((1,), jnp.int32)
    return assemble(packs, places.astype(jnp.int32), through)


def body(factors, amplitudes):
    a_rows, c_rows, _ = factors.shape
    n = lax.axis_size("out")
    vir = lax.axis_size("vir")
    z = lax.axis_index("out")

    def send(array, *ways):
        return lax.ppermute(array, "out", ways)

    own = amplitudes.transpose(1, 0, 2)
    token = jnp.zeros((8, LANES), jnp.float32)
    shared = spread(factors[:BB], n, z)
    batch, [token] = everywhere(shared, vir, [token])
    cut = 3 * c_rows // 4 if c_rows % 64 == 0 else c_rows
    spans = [(0, cut), (cut, c_rows)] if cut < c_rows else [(0, c_rows)]
    made = []

    def make():
        nonlocal token
        part, [token] = integrals(factors, batch, *spans[len(made)], [token])
        made.append(part)

    make()
    if n == 4:
        inside = (z == 1) | (z == 2)
        second = send(amplitudes, (2, 0), (1, 3))
        first = send(own, (3, 1), (1, 0), (0, 2), (2, 3))
        onward, kept = [], [own[i:j] for i, j in spans]
        for span in spans:
            part, [token] = pick(inside, first, own, *span, [token])
            onward.append(part)
        sides, middle = [], []
        for k in range(len(spans)):
            if k:
                make()
            token, onward[k], kept[k] = fence([token, onward[k], kept[k]])
            middle.append(send(kept[k], (2, 1), (1, 2)))
            sides.append(send(onward[k], (1, 0), (0, 1), (2, 3), (3, 2)))
        token, second = fence([token, second], MUCH)
        [sides[0]] = fence(sides[:1], MUCH)
        second, [token] = turn(second, [token])
        late = [[(t, 0) for t in pair] for pair in zip(sides, middle)]
        early = [own, first, second]
        slots = jnp.array([[0, 1, 2, 3], [3, 0, 4, 1], [1, 4, 0, 3], [3, 2, 1, 0]], jnp.int32)[z]
    else:
        gathered = lax.all_gather(own, "out")
        early, late = [own], [[(gathered[k], i) for k in range(n)] for i, _ in spans]
        slots = jnp.arange(1, n + 1, dtype=jnp.int32)
    while len(made) < len(spans):
        make()

    known, added = None, None
    for part, (start, _) in zip(made, spans):
        terms = ladder_early([(t, start) for t in early], part)
        known = terms if known is None else known + terms
    for part, taus in zip(made[:-1], late):
        added = ladder_early(taus, part)
    if added is None:
        rows = sum(t.shape[1] for t, _ in late[-1])
        added = jnp.zeros((rows, BB * a_rows), jnp.float32)
    parts = ladder_late(slots, known, added, late[-1], made[-1], vir)
    swapped = lax.all_to_all(parts, "vir", split_axis=0, concat_axis=0)
    return jnp.sum(swapped, axis=0)


def solution(mesh):
    placed = (P("out", "vir", None), P("out", "vir", None))
    return jax.shard_map(
        body, mesh=mesh, in_specs=placed, out_specs=P(None, "vir", "out"), check_vma=False
    )
```
